128 devices in a mesh: dp: 8 (over y, z_lo), tensor: 16 (over z_hi, x, core).
Axes of the slice: x: 4, y: 4, z: 4 (z_hi: 2, z_lo: 2; z = z_hi * 2 + z_lo), core: 2. Of those that a mesh axis runs over, the one named last changes fastest.
Arguments:
- token_ids: int32 [512, 4], P(('dp', 'tensor')), may hold values from 0 to 76031
- lengths: int32 [512], P(('dp', 'tensor')), may hold values from 1 to 508, 130048 in all
- embedding: bfloat16 [76032, 8192], P('tensor', 'dp'), may hold values from -6 to 6
- norm_gain: bfloat16 [8192], replicated, may hold values from 0.099609375 to 1.8984375
- q_weight: bfloat16 [8192, 8192], P('dp', 'tensor'), may hold values from -0.0625 to 0.0625
- k_weight: bfloat16 [8192, 1024], P('dp', 'tensor'), may hold values from -0.0625 to 0.0625
- v_weight: bfloat16 [8192, 1024], P('dp', 'tensor'), may hold values from -0.0625 to 0.0625
- q_bias: bfloat16 [8192], P('tensor'), may hold values from -6 to 6
- k_bias: bfloat16 [1024], P('tensor'), may hold values from -6 to 6
- v_bias: bfloat16 [1024], P('tensor'), may hold values from -6 to 6
- o_weight: bfloat16 [8192, 8192], P('tensor', 'dp'), may hold values from -0.0625 to 0.0625
- key_cache: bfloat16 [512, 512, 1024], P(('dp', 'tensor')), may hold values from -400 to 400, as said below
- value_cache: bfloat16 [512, 512, 1024], P(('dp', 'tensor')), may hold values from -6 to 6
Outputs:
- hidden: bfloat16 [512, 4, 8192], P(('dp', 'tensor'))
- new_keys: bfloat16 [512, 4, 1024], P(('dp', 'tensor'))
- new_values: bfloat16 [512, 4, 1024], P(('dp', 'tensor'))
The draws below stay inside these ranges and needn't reach their ends.
Inputs may be any that keep to these rules, and one draw needn't show every extreme that they name: The next 4 tokens of sequence b take positions lengths[b] to lengths[b] + 3. `key_cache`: keys are stored already rotated; slots at or past a sequence's length are unused.
All inputs are finite; a program needn't handle non-finite values. No bound on the sum of `lengths` on one device may be relied on, other than what follows from the above.
Results may differ from the reference program's by a relative error of at most 0.03.
Values may be sent and summed in bfloat16 or wider, within the bound.
No kernel may reach another device: no remote copies, remote signals or barrier semaphores. Data moves between devices by JAX's collectives and lax.ppermute only.
A program may use at most 128 MiB of HBM per device.

```python
import math
import jax
import jax.numpy as jnp
import numpy as np
from jax import lax

D = 8192
H = 64
KVH = 8
HD = 128
VOCAB = 76032
LEN = 512
STEPS = 4
QD = 8192
KVD = 1024
SEQS = 512
N_TENSOR = 16


def draw_key_cache(key, part):
    key = jax.random.fold_in(key, 7)
    base_key = jax.random.fold_in(key, 0)
    base = 1.5 * jax.random.truncated_normal(base_key, -4.0, 4.0, (SEQS, LEN, KVD), jnp.float32)
    return base.astype(jnp.bfloat16)


def place_ends(values, key, smallest, top_value):
    index_at = [jax.random.randint(jax.random.fold_in(key, axis), (), 0, length) for axis, length in enumerate(values.shape)]
    longest = values.shape.index(max(values.shape))
    neighbour = index_at[:longest] + [(index_at[longest] + 1) % values.shape[longest]] + index_at[longest + 1:]
    return values.at[tuple(index_at)].set(smallest).at[tuple(neighbour)].set(top_value)


def level_of(stream_key, extent, cuts, low, top_value):
    def one(dim, blocks):
        draws = jax.random.uniform(jax.random.fold_in(jax.random.fold_in(stream_key, 6), dim), (blocks,), jnp.float32, low / len(cuts), top_value / len(cuts))
        return jnp.repeat(jnp.exp(draws), extent[dim] // blocks).reshape((-1,) + (1,) * (len(extent) - dim - 1))

    gain = one(*cuts[0])
    for cut in cuts[1:]:
        gain = gain * one(*cut)
    return gain


def ranked_wide(own_key, extent, number_of, slope):
    loads = [min(1 << octave, number_of + 1 - (1 << octave)) * (1 << 20) // math.isqrt((1 << octave) ** slope) + 1 for octave in range((number_of + 1).bit_length()) if 1 << octave <= number_of]
    spread = 1 + sum(loads) // (1 << 30)
    grid = np.cumsum(np.array([max(1, weight // spread) for weight in loads]))
    pick = jax.random.randint(jax.random.fold_in(own_key, 1), extent, 0, int(grid[len(loads) - 1]))
    start = jnp.left_shift(1, jnp.searchsorted(jnp.asarray(grid, jnp.int32), pick, side="right").astype(jnp.int32))
    rank = start - 1 + jax.random.randint(jax.random.fold_in(own_key, 4), extent, 0, 1 << 30) % jnp.minimum(start, number_of + 1 - start)
    return jax.random.permutation(jax.random.fold_in(own_key, 2), number_of)[rank].astype(jnp.int32)


def split_up(amount, total, limit, lean):
    loads = [(1 << 20) // math.isqrt(grade ** lean) + 1 for grade in range(2, amount + 1)]
    rest, counts = total - limit - (amount - 1), [1] * (amount - 1)
    while rest > 0:
        free = [i for i in range(amount - 1) if counts[i] < limit]
        whole, left = sum([loads[i] for i in free]), rest
        for i in free:
            more = min(limit - counts[i], max(1, left * loads[i] // whole), rest)
            counts[i] = counts[i] + more
            rest = rest - more
    return np.array([limit] + counts)


def uneven_parts(stream_key, number_of, total, reach, slope):
    if number_of == 2:
        one = jax.random.randint(stream_key, (), max(1, total - reach), min(reach, total - 1) + 1)
        return jnp.stack([one, total - one])
    sizes = jnp.asarray(split_up(number_of, total, reach, slope), jnp.int32)
    pairs = (number_of - 1) // 2
    giver, taker = sizes[1:1 + 2 * pairs:2], sizes[2:2 + 2 * pairs:2]
    room = jnp.minimum(giver - 1, reach - taker)
    passed = jax.random.randint(jax.random.fold_in(stream_key, 1), (pairs,), 0, 1 << 20) % (room + 1)
    sizes = sizes.at[1:1 + 2 * pairs:2].set(giver - passed).at[2:2 + 2 * pairs:2].set(taker + passed)
    return sizes[jax.random.permutation(jax.random.fold_in(stream_key, 2), number_of)]


def bell_draw(own_key, dims, spread, bound, shards=(), held_as=jnp.bfloat16):
    values = jax.random.normal(own_key, dims, jnp.float32) * spread
    if len(shards) > 0:
        values = level_of(own_key, dims, shards, -0.22, 0.18) * values
    return jnp.clip(values, min=-bound, max=bound).astype(held_as)


def setup_inputs(seed: int = 0) -> dict:
    streams_of = jax.random.split(jax.random.key(seed), 14)
    return {
        "token_ids": place_ends(ranked_wide(streams_of[0], (SEQS, STEPS), VOCAB, 2), jax.random.fold_in(streams_of[0], 3), 0, VOCAB - 1).astype(jnp.int32),
        "lengths": uneven_parts(streams_of[1], SEQS, SEQS * (LEN - STEPS) // 2, LEN - STEPS, 1).astype(jnp.int32),
        "embedding": bell_draw(streams_of[2], (VOCAB, D), 1.0, 6.0, ((0, 16), (1, 8))),
        "norm_gain": jnp.clip(1.0 + 0.18 * jax.random.normal(streams_of[3], (D,), jnp.float32), 0.099609375, 1.8984375).astype(jnp.bfloat16),
        "q_weight": bell_draw(streams_of[4], (D, QD), D ** -0.5, 0.0625, ((0, 8), (1, 16))),
        "k_weight": bell_draw(streams_of[5], (D, KVD), D ** -0.5, 0.0625, ((0, 8), (1, 16))),
        "v_weight": bell_draw(streams_of[6], (D, KVD), D ** -0.5, 0.0625, ((0, 8), (1, 16))),
        "q_bias": bell_draw(streams_of[7], (QD,), 1.0, 6.0, ((0, 16),)),
        "k_bias": bell_draw(streams_of[8], (KVD,), 1.0, 6.0, ((0, 16),)),
        "v_bias": bell_draw(streams_of[9], (KVD,), 0.5, 6.0, ((0, 16),)),
        "o_weight": bell_draw(streams_of[10], (QD, D), QD ** -0.5, 0.0625, ((0, 16), (1, 8))),
        "key_cache": draw_key_cache(jax.random.fold_in(streams_of[13], 71), 0),
        "value_cache": bell_draw(streams_of[12], (SEQS, LEN, KVD), 1.0, 6.0, ((0, 128),)),
    }


norm_epsilon = 1e-06
rope_base = 1000000.0
masked_low = -1e+30

def rotate(features, positions):
    head_width = features.shape[-1]
    half_width = head_width // 2
    frequency = rope_base ** (-(2.0 * jnp.arange(half_width, dtype=jnp.float32)) / head_width)
    angles = positions.astype(jnp.float32)[..., None, None] * frequency
    cosine = jnp.cos(angles)
    sine_part = jnp.sin(angles)
    leading = features[..., :half_width]
    trailing = features[..., half_width:]
    return jnp.concatenate([leading * cosine - trailing * sine_part, trailing * cosine + leading * sine_part], axis=-1)

def per_sequence(sequence_args):
    rotated, fresh_keys, fresh_values, cache_keys, cache_values, length = sequence_args
    grouped = rotated.astype(jnp.float32).reshape(STEPS, KVH, H // KVH, HD)
    keys_wide = cache_keys.astype(jnp.float32).reshape(LEN, KVH, HD)
    values_wide = cache_values.astype(jnp.float32).reshape(LEN, KVH, HD)
    fresh_wide = fresh_keys.astype(jnp.float32)
    fresh_vals = fresh_values.astype(jnp.float32)
    score_scale = HD ** (-0.5)
    cached = jnp.einsum('kgrd,jgd->kgrj', grouped, keys_wide) * score_scale
    fresh_scores = jnp.einsum('kgrd,jgd->kgrj', grouped, fresh_wide) * score_scale
    cache_valid = (jnp.arange(LEN, dtype=jnp.int32) < length)[None, None, None, :]
    fresh_valid = (jnp.arange(STEPS, dtype=jnp.int32)[None, :] <= jnp.arange(STEPS, dtype=jnp.int32)[:, None])[:, None, None, :]
    row_top = jnp.maximum(lax.optimization_barrier(jnp.max(jnp.where(cache_valid, cached, masked_low), axis=-1)), lax.optimization_barrier(jnp.max(jnp.where(fresh_valid, fresh_scores, masked_low), axis=-1)))[..., None]
    cache_exp = jnp.exp(jnp.where(cache_valid, cached - row_top, masked_low))
    fresh_exp = jnp.exp(jnp.where(fresh_valid, fresh_scores - row_top, masked_low))
    denominator = lax.optimization_barrier(jnp.sum(cache_exp, axis=-1, keepdims=True)) + lax.optimization_barrier(jnp.sum(fresh_exp, axis=-1, keepdims=True))
    cache_weights = (cache_exp / denominator).astype(jnp.bfloat16).astype(jnp.float32)
    fresh_weights = (fresh_exp / denominator).astype(jnp.bfloat16).astype(jnp.float32)
    attended = jnp.einsum('kgrj,jgd->kgrd', cache_weights, values_wide)
    attended = attended + jnp.einsum('kgrj,jgd->kgrd', fresh_weights, fresh_vals)
    return attended.reshape(STEPS, H * HD).astype(jnp.bfloat16)

def reference(token_ids, lengths, embedding, norm_gain, q_weight, k_weight, v_weight, q_bias, k_bias, v_bias, o_weight, key_cache, value_cache):
    inputs = jnp.take(embedding, token_ids, axis=0)
    widened = inputs.astype(jnp.float32)
    normed = (widened * lax.rsqrt(lax.optimization_barrier(jnp.mean(widened * widened, axis=-1, keepdims=True)) + norm_epsilon) * norm_gain.astype(jnp.float32)).astype(jnp.bfloat16)
    flat_rows = normed.reshape(SEQS * STEPS, D)
    queries = (jnp.dot(flat_rows, q_weight, preferred_element_type=jnp.float32) + q_bias.astype(jnp.float32)).astype(jnp.bfloat16)
    keys = (jnp.dot(flat_rows, k_weight, preferred_element_type=jnp.float32) + k_bias.astype(jnp.float32)).astype(jnp.bfloat16)
    new_values = (jnp.dot(flat_rows, v_weight, preferred_element_type=jnp.float32) + v_bias.astype(jnp.float32)).astype(jnp.bfloat16)
    positions = lengths[:, None] + jnp.arange(STEPS, dtype=jnp.int32)[None, :]
    rotated_queries = rotate(queries.reshape(SEQS, STEPS, H, HD).astype(jnp.float32), positions).astype(jnp.bfloat16)
    new_keys = rotate(keys.reshape(SEQS, STEPS, KVH, HD).astype(jnp.float32), positions).astype(jnp.bfloat16)
    value_heads = new_values.reshape(SEQS, STEPS, KVH, HD)
    attended = lax.map(per_sequence, (rotated_queries, new_keys, value_heads, key_cache, value_cache, lengths))
    flat_attn = attended.reshape(SEQS * STEPS, N_TENSOR, QD // N_TENSOR).transpose(1, 0, 2)
    o_blocks = o_weight.reshape(N_TENSOR, QD // N_TENSOR, D)

    def accumulate(running, block_pair):
        rounded_part = jnp.dot(block_pair[0], block_pair[1], preferred_element_type=jnp.float32).astype(jnp.bfloat16)
        rounded_part = lax.optimization_barrier(rounded_part)
        return (running + rounded_part.astype(jnp.float32), None)
    running, _ = lax.scan(accumulate, jnp.zeros((SEQS * STEPS, D), jnp.float32), (flat_attn, o_blocks))
    hidden = (widened.reshape(SEQS * STEPS, D) + running).astype(jnp.bfloat16).reshape(SEQS, STEPS, D)
    return (hidden, new_keys.reshape(SEQS, STEPS, KVD), new_values.reshape(SEQS, STEPS, KVD))
```

```python
import jax
import jax.numpy as jnp
from jax import lax
from jax.sharding import Mesh
from jax.sharding import PartitionSpec as P

HD = 128
ROUND_ROWS = 128

norm_epsilon = 1e-06
rope_base = 1000000.0
masked_low = -1e30

DP = ("y", "zl")
CHIPS = ("zh", "x")
PLANE = ("y", "zl", "zh", "x")
EVERY = ("y", "zl", "zh", "x", "core")


def rotate(features, positions):
    head_width = features.shape[-1]
    half_width = head_width // 2
    frequency = rope_base ** (-(2.0 * jnp.arange(half_width, dtype=jnp.float32)) / head_width)
    angles = positions.astype(jnp.float32)[..., None, None] * frequency
    cosine = jnp.cos(angles)
    sine_part = jnp.sin(angles)
    leading = features[..., :half_width]
    trailing = features[..., half_width:]
    return jnp.concatenate(
        [leading * cosine - trailing * sine_part, trailing * cosine + leading * sine_part], axis=-1
    )


def attend(rotated, fresh_keys, fresh_values, key_cache, value_cache, lengths):
    seq_here, step_span, heads, head_width = rotated.shape
    kv_heads = fresh_keys.shape[2]
    group_size = heads // kv_heads
    cache_len = key_cache.shape[1]
    cache_keys = key_cache.reshape(seq_here, cache_len, kv_heads, head_width)
    cache_values = value_cache.reshape(seq_here, cache_len, kv_heads, head_width)
    grouped = rotated.reshape(seq_here, step_span, kv_heads, group_size, head_width)
    score_scale = head_width ** (-0.5)
    cached = (
        jnp.einsum("skgrd,sjgd->skgrj", grouped, cache_keys, preferred_element_type=jnp.float32)
        * score_scale
    )
    fresh_scores = (
        jnp.einsum("skgrd,sjgd->skgrj", grouped, fresh_keys, preferred_element_type=jnp.float32)
        * score_scale
    )
    cache_valid = (jnp.arange(cache_len, dtype=jnp.int32)[None, :] < lengths[:, None])[
        :, None, None, None, :
    ]
    fresh_count = fresh_keys.shape[1]
    fresh_valid = (
        jnp.arange(fresh_count, dtype=jnp.int32)[None, :]
        <= jnp.arange(step_span, dtype=jnp.int32)[:, None]
    )[None, :, None, None, :]
    row_top = jnp.maximum(
        jnp.max(jnp.where(cache_valid, cached, masked_low), axis=-1),
        jnp.max(jnp.where(fresh_valid, fresh_scores, masked_low), axis=-1),
    )[..., None]
    cache_exp = jnp.exp(jnp.where(cache_valid, cached - row_top, masked_low))
    fresh_exp = jnp.exp(jnp.where(fresh_valid, fresh_scores - row_top, masked_low))
    denominator = jnp.sum(cache_exp, axis=-1, keepdims=True) + jnp.sum(
        fresh_exp, axis=-1, keepdims=True
    )
    cache_weights = (cache_exp / denominator).astype(jnp.bfloat16)
    fresh_weights = (fresh_exp / denominator).astype(jnp.bfloat16)
    attended = jnp.einsum(
        "skgrj,sjgd->skgrd", cache_weights, cache_values, preferred_element_type=jnp.float32
    )
    attended = attended + jnp.einsum(
        "skgrj,sjgd->skgrd", fresh_weights, fresh_values, preferred_element_type=jnp.float32
    )
    return attended.reshape(seq_here, step_span, heads * head_width).astype(jnp.bfloat16)


def swap_cores(value):
    return lax.ppermute(value, "core", [(0, 1), (1, 0)])


def per_device(
    token_ids,
    lengths,
    embedding,
    norm_gain,
    q_weight,
    k_weight,
    v_weight,
    q_bias,
    k_bias,
    v_bias,
    o_weight,
    key_cache,
    value_cache,
):
    seq_here, step_count = token_ids.shape
    rows_here = seq_here * step_count
    vocab_here, width_here = embedding.shape
    replicas = lax.axis_size(DP)
    chips = lax.axis_size(CHIPS)
    chip = lax.axis_index(CHIPS)
    core = lax.axis_index("core")
    replica = lax.axis_index(DP)
    parties = replicas * chips
    plane_rows = parties * rows_here

    sent_ids = jnp.broadcast_to(token_ids.reshape(1, rows_here), (parties * 2, rows_here))
    every_id = lax.all_to_all(sent_ids, EVERY, split_axis=0, concat_axis=0, tiled=True)
    plane_ids = every_id.reshape(parties, 2, rows_here).transpose(1, 0, 2).reshape(2, plane_rows)
    holder = plane_ids // (2 * vocab_here)
    place = jnp.arange(plane_rows, dtype=jnp.int32)
    same = plane_ids[:, :, None] == plane_ids[:, None, :]
    leader = jnp.min(jnp.where(same, place[None, None, :], plane_rows), axis=2)
    leads = leader == place[None, :]
    before = (
        leads[:, None, :]
        & (holder[:, :, None] == holder[:, None, :])
        & (place[None, None, :] < leader[:, :, None])
    )
    rank = jnp.sum(before.astype(jnp.int32), axis=2)
    rounds = jnp.max(rank) // ROUND_ROWS + 1
    own_holder = jnp.where(core == 0, holder[0], holder[1])
    own_rank = jnp.where(core == 0, rank[0], rank[1])
    listed_here = leads & (holder == chip)

    def exchange(turn):
        first = turn * ROUND_ROWS
        wanted = listed_here[:, None, :] & (
            rank[:, None, :] == first + jnp.arange(ROUND_ROWS, dtype=jnp.int32)[None, :, None]
        )
        listed = jnp.max(jnp.where(wanted, plane_ids[:, None, :], -1), axis=2)
        offset = listed - (2 * chip + core) * vocab_here
        inside = (listed >= 0) & (offset >= 0) & (offset < vocab_here)
        picked = jnp.take(
            embedding, jnp.clip(offset, 0, vocab_here - 1).reshape(-1), axis=0
        ).reshape(2, ROUND_ROWS, width_here)
        picked = jnp.where(inside[:, :, None], picked, jnp.zeros_like(picked))
        mine = jnp.where(core == 0, picked[0], picked[1])
        theirs = jnp.where(core == 0, picked[1], picked[0])
        merged = mine + swap_cores(theirs)
        table = lax.all_to_all(
            jnp.broadcast_to(merged[None], (chips, ROUND_ROWS, width_here)),
            CHIPS,
            split_axis=0,
            concat_axis=0,
            tiled=True,
        ).reshape(chips * ROUND_ROWS, width_here)
        here = (own_rank >= first) & (own_rank < first + ROUND_ROWS)
        slot = jnp.where(here, own_holder * ROUND_ROWS + own_rank - first, -1)
        chosen = (
            slot[:, None] == jnp.arange(chips * ROUND_ROWS, dtype=jnp.int32)[None, :]
        ).astype(jnp.bfloat16)
        return jnp.dot(chosen, table, preferred_element_type=jnp.float32).astype(jnp.bfloat16)

    plane_inputs = lax.fori_loop(
        1, rounds, lambda turn, sofar: sofar + exchange(turn), exchange(0)
    )

    both = jnp.concatenate([q_weight, k_weight, v_weight], axis=1)
    other = swap_cores(both)
    low = jnp.where(core == 0, both, other)
    high = jnp.where(core == 0, other, both)
    q_cols = q_weight.shape[1]
    k_cols = k_weight.shape[1]
    q_end, k_end = q_cols, q_cols + k_cols
    pair_weight = jnp.concatenate(
        [
            low[:, :q_end],
            high[:, :q_end],
            low[:, q_end:k_end],
            high[:, q_end:k_end],
            low[:, k_end:],
            high[:, k_end:],
        ],
        axis=1,
    )
    own_bias = jnp.concatenate([q_bias, k_bias, v_bias])
    every_bias = lax.all_gather(own_bias, CHIPS + ("core",), axis=0, tiled=False)
    every_bias = every_bias.reshape(chips, 2, -1).astype(jnp.float32)
    pair_bias = jnp.concatenate(
        [
            every_bias[:, :, :q_end].reshape(chips, -1),
            every_bias[:, :, q_end:k_end].reshape(chips, -1),
            every_bias[:, :, k_end:].reshape(chips, -1),
        ],
        axis=1,
    )
    own_gain = lax.dynamic_slice_in_dim(norm_gain, replica * width_here, width_here)

    gained = (plane_inputs.astype(jnp.float32) * own_gain.astype(jnp.float32)).astype(jnp.bfloat16)
    partial = jnp.dot(gained, pair_weight, preferred_element_type=jnp.float32).astype(jnp.bfloat16)
    strip = width_here // chips
    shown = lax.dynamic_slice_in_dim(plane_inputs, chip * strip, strip, axis=1)
    payload = jnp.concatenate([partial, shown], axis=1)
    arrived = lax.all_to_all(payload, PLANE, split_axis=0, concat_axis=0, tiled=True)
    pair_cols = pair_weight.shape[1]
    arrived = arrived.reshape(replicas, chips, rows_here, pair_cols + strip)
    inputs = (
        arrived[..., pair_cols:].transpose(2, 0, 1, 3).reshape(rows_here, -1).astype(jnp.float32)
    )
    scale = lax.rsqrt(jnp.mean(inputs * inputs, axis=-1, keepdims=True) + norm_epsilon)
    summed = jnp.sum(arrived[..., :pair_cols].astype(jnp.float32), axis=0)
    joined = (summed * scale[None] + pair_bias[:, None, :]).astype(jnp.bfloat16)
    joined = joined.transpose(1, 0, 2)
    group = 2 * q_cols
    queries = joined[..., :group].reshape(seq_here, step_count, -1, HD)
    fresh_keys = joined[..., group : group + 2 * k_cols].reshape(seq_here, step_count, -1, HD)
    fresh_values = joined[..., group + 2 * k_cols :].reshape(seq_here, step_count, -1, HD)
    positions = lengths[:, None] + jnp.arange(step_count, dtype=jnp.int32)[None, :]
    rotated = rotate(queries.astype(jnp.float32), positions).astype(jnp.bfloat16)
    new_keys = rotate(fresh_keys.astype(jnp.float32), positions).astype(jnp.bfloat16)
    attended = attend(rotated, new_keys, fresh_values, key_cache, value_cache, lengths)

    full_o = lax.all_gather(o_weight, DP, axis=0, tiled=False)
    other_o = swap_cores(full_o)
    gathered = lax.all_to_all(
        attended.reshape(rows_here, chips, 2 * q_cols).transpose(1, 0, 2),
        CHIPS,
        split_axis=0,
        concat_axis=0,
        tiled=True,
    ).reshape(chips * rows_here, 2 * q_cols)
    own_part = jnp.where(core == 0, gathered[:, :q_cols], gathered[:, q_cols:])
    other_part = jnp.where(core == 0, gathered[:, q_cols:], gathered[:, :q_cols])
    branch = jnp.concatenate(
        [
            (
                jnp.dot(own_part, full_o[block], preferred_element_type=jnp.float32)
                + jnp.dot(other_part, other_o[block], preferred_element_type=jnp.float32)
            ).astype(jnp.bfloat16)
            for block in range(replicas)
        ],
        axis=1,
    )
    branches = lax.all_to_all(branch, CHIPS, split_axis=0, concat_axis=0, tiled=True)
    branches = branches.reshape(chips, rows_here, -1).astype(jnp.float32)
    hidden = (inputs + jnp.sum(branches, axis=0)).astype(jnp.bfloat16)
    return (
        hidden.reshape(seq_here, step_count, -1),
        new_keys.reshape(seq_here, step_count, -1),
        fresh_values.reshape(seq_here, step_count, -1),
    )


def solution(mesh):
    fine = Mesh(mesh.devices.reshape(4, 2, 2, 4, 2), EVERY)
    tensor = CHIPS + ("core",)
    placed = (
        P(EVERY, None),
        P(EVERY),
        P(tensor, DP),
        P(),
        P(DP, tensor),
        P(DP, tensor),
        P(DP, tensor),
        P(tensor),
        P(tensor),
        P(tensor),
        P(tensor, DP),
        P(EVERY, None, None),
        P(EVERY, None, None),
    )
    return jax.shard_map(
        per_device,
        mesh=fine,
        in_specs=placed,
        out_specs=(
            P(EVERY, None, None),
            P(EVERY, None, None),
            P(EVERY, None, None),
        ),
        check_vma=False,
    )
```

```python
import jax
import jax.numpy as jnp
from jax import lax
from jax.experimental import pallas as pl
from jax.experimental.pallas import tpu as pltpu
from jax.sharding import Mesh
from jax.sharding import PartitionSpec as P

HD = 128
ROUND_ROWS = 72
SENT_ROWS = 80

norm_epsilon = 1e-06
rope_base = 1000000.0
masked_low = -1e30

DP = ("y", "zl")
CHIPS = ("zh", "x")
LAYER = ("zl", "zh", "x")
PLANE = ("y", "zh", "x")
EVERY = ("y", "zl", "zh", "x", "core")


def rotate(features, positions):
    head_width = features.shape[-1]
    half_width = head_width // 2
    frequency = rope_base ** (-(2.0 * jnp.arange(half_width, dtype=jnp.float32)) / head_width)
    angles = positions.astype(jnp.float32)[..., None, None] * frequency
    cosine = jnp.cos(angles)
    sine_part = jnp.sin(angles)
    leading = features[..., :half_width]
    trailing = features[..., half_width:]
    return jnp.concatenate(
        [leading * cosine - trailing * sine_part, trailing * cosine + leading * sine_part], axis=-1
    )


def attend(rotated, fresh_keys, fresh_values, key_cache, value_cache, lengths):
    seq_here, step_span, heads, head_width = rotated.shape
    kv_heads = fresh_keys.shape[2]
    group_size = heads // kv_heads
    cache_len = key_cache.shape[1]
    cache_keys = key_cache.reshape(seq_here, cache_len, kv_heads, head_width)
    cache_values = value_cache.reshape(seq_here, cache_len, kv_heads, head_width)
    grouped = rotated.reshape(seq_here, step_span, kv_heads, group_size, head_width)
    score_scale = head_width ** (-0.5)
    cached = (
        jnp.einsum("skgrd,sjgd->skgrj", grouped, cache_keys, preferred_element_type=jnp.float32)
        * score_scale
    )
    fresh_scores = (
        jnp.einsum("skgrd,sjgd->skgrj", grouped, fresh_keys, preferred_element_type=jnp.float32)
        * score_scale
    )
    cache_valid = (jnp.arange(cache_len, dtype=jnp.int32)[None, :] < lengths[:, None])[
        :, None, None, None, :
    ]
    fresh_count = fresh_keys.shape[1]
    fresh_valid = (
        jnp.arange(fresh_count, dtype=jnp.int32)[None, :]
        <= jnp.arange(step_span, dtype=jnp.int32)[:, None]
    )[None, :, None, None, :]
    row_top = jnp.maximum(
        jnp.max(jnp.where(cache_valid, cached, masked_low), axis=-1),
        jnp.max(jnp.where(fresh_valid, fresh_scores, masked_low), axis=-1),
    )[..., None]
    cache_exp = jnp.exp(jnp.where(cache_valid, cached - row_top, masked_low))
    fresh_exp = jnp.exp(jnp.where(fresh_valid, fresh_scores - row_top, masked_low))
    denominator = jnp.sum(cache_exp, axis=-1, keepdims=True) + jnp.sum(
        fresh_exp, axis=-1, keepdims=True
    )
    cache_weights = (cache_exp / denominator).astype(jnp.bfloat16)
    fresh_weights = (fresh_exp / denominator).astype(jnp.bfloat16)
    attended = jnp.einsum(
        "skgrj,sjgd->skgrd", cache_weights, cache_values, preferred_element_type=jnp.float32
    )
    attended = attended + jnp.einsum(
        "skgrj,sjgd->skgrd", fresh_weights, fresh_values, preferred_element_type=jnp.float32
    )
    return attended.reshape(seq_here, step_span, heads * head_width).astype(jnp.bfloat16)


def swap_cores(value):
    return lax.ppermute(value, "core", [(0, 1), (1, 0)])


def swap_layers(value):
    return lax.ppermute(value, "zl", [(0, 1), (1, 0)])


VMEM = pl.BlockSpec(memory_space=pltpu.VMEM)
SMEM = pl.BlockSpec(memory_space=pltpu.SMEM)


def projection_kernel(place_ref, slot_ref, table_ref, gain_ref, *rest):
    weight_refs, out_ref, wide_ref, total_ref = rest[:4], rest[4], rest[5], rest[6]
    chip, layer, core = place_ref[0], place_ref[1], place_ref[2]
    rows = slot_ref.shape[0]
    width = table_ref.shape[2]
    table_rows = table_ref.shape[1]
    cols = weight_refs[0].shape[1]
    chosen = (
        lax.broadcasted_iota(jnp.int32, (rows, table_rows), 1) == slot_ref[...]
    ).astype(jnp.bfloat16)
    for flip in range(2):
        block = (layer + flip) % 2
        found = jnp.dot(chosen, table_ref[block], preferred_element_type=jnp.float32)
        wide_ref[:, pl.ds(pl.multiple_of(block * width, width), width)] = found.astype(
            jnp.bfloat16
        )
        gained = (found * gain_ref[block]).astype(jnp.bfloat16)
        for side in range(2):
            product = jnp.dot(
                gained, weight_refs[2 * flip + side][...], preferred_element_type=jnp.float32
            )
            if flip == 0:
                total_ref[side] = product
            else:
                where = pl.multiple_of(((core + side) % 2) * cols, cols)
                out_ref[:, pl.ds(where, cols)] = (total_ref[side] + product).astype(jnp.bfloat16)
    strip = out_ref.shape[1] - 2 * cols
    out_ref[:, 2 * cols :] = wide_ref[:, pl.ds(pl.multiple_of(chip * strip, strip), strip)]


def project(place, slot, table, gain, weights, chips):
    rows = slot.shape[0]
    width = table.shape[2]
    cols = weights[0].shape[1]
    return pl.pallas_call(
        projection_kernel,
        out_shape=jax.ShapeDtypeStruct((rows, 2 * cols + 2 * width // chips), jnp.bfloat16),
        in_specs=[SMEM] + [VMEM] * 7,
        out_specs=VMEM,
        scratch_shapes=[
            pltpu.VMEM((rows, 2 * width), jnp.bfloat16),
            pltpu.VMEM((2, rows, cols), jnp.float32),
        ],
        compiler_params=pltpu.CompilerParams(vmem_limit_bytes=48 * 1024 * 1024),
        name="project",
    )(place, slot, table, gain, *weights)


def branch_kernel(place_ref, rows_ref, *rest):
    weight_refs, out_ref = rest[:4], rest[4]
    layer, core = place_ref[1], place_ref[2]
    depth, width = weight_refs[0].shape
    for flip in range(2):
        block = pl.multiple_of(((layer + flip) % 2) * width, width)
        parts = []
        for side in range(2):
            where = pl.multiple_of(((core + side) % 2) * depth, depth)
            parts.append(
                jnp.dot(
                    rows_ref[:, pl.ds(where, depth)],
                    weight_refs[2 * flip + side][...],
                    preferred_element_type=jnp.float32,
                )
            )
        out_ref[:, pl.ds(block, width)] = (parts[0] + parts[1]).astype(jnp.bfloat16)


def branch_out(place, rows, weights):
    return pl.pallas_call(
        branch_kernel,
        out_shape=jax.ShapeDtypeStruct((rows.shape[0], 2 * weights[0].shape[1]), jnp.bfloat16),
        in_specs=[SMEM] + [VMEM] * 5,
        out_specs=VMEM,
        compiler_params=pltpu.CompilerParams(vmem_limit_bytes=48 * 1024 * 1024),
        name="branch",
    )(place, rows, *weights)


def hidden_kernel(branch_ref, strip_ref, out_ref):
    chips = branch_ref.shape[1]
    strip = strip_ref.shape[3]
    for part in range(chips):
        span = slice(part * strip, (part + 1) * strip)
        total = strip_ref[0, part].astype(jnp.float32)
        for chip in range(chips):
            total = total + branch_ref[0, chip, :, span].astype(jnp.float32)
        out_ref[:, span] = total.astype(jnp.bfloat16)


def hidden_sum(branches, arrived):
    groups, chips, rows, width = branches.shape
    strip = width // chips
    last = arrived.shape[3] // strip - 1
    return pl.pallas_call(
        hidden_kernel,
        out_shape=jax.ShapeDtypeStruct((rows, groups * width), jnp.bfloat16),
        grid=(groups,),
        in_specs=[
            pl.BlockSpec((1, chips, rows, width), lambda y: (y, 0, 0, 0)),
            pl.BlockSpec((1, chips, rows, strip), lambda y: (y, 0, 0, last)),
        ],
        out_specs=pl.BlockSpec((rows, width), lambda y: (0, y)),
        compiler_params=pltpu.CompilerParams(vmem_limit_bytes=48 * 1024 * 1024),
        name="hidden_sum",
    )(branches, arrived)


def per_device(
    token_ids,
    lengths,
    embedding,
    norm_gain,
    q_weight,
    k_weight,
    v_weight,
    q_bias,
    k_bias,
    v_bias,
    o_weight,
    key_cache,
    value_cache,
):
    seq_here, step_count = token_ids.shape
    rows_here = seq_here * step_count
    vocab_here, width_here = embedding.shape
    groups = lax.axis_size("y")
    chips = lax.axis_size(CHIPS)
    chip = lax.axis_index(CHIPS)
    core = lax.axis_index("core")
    layer = lax.axis_index("zl")
    parties = groups * chips
    plane_rows = parties * rows_here
    place = jnp.stack([chip, layer, core]).astype(jnp.int32)

    both = jnp.concatenate([q_weight, k_weight, v_weight], axis=1)
    both_layer = swap_layers(both)
    weights = (both, swap_cores(both), both_layer, swap_cores(both_layer))
    o_layer = swap_layers(o_weight)
    o_weights = (o_weight, swap_cores(o_weight), o_layer, swap_cores(o_layer))
    own_bias = jnp.concatenate([q_bias, k_bias, v_bias])
    core_cols = own_bias.shape[0]
    q_cols = q_bias.shape[0]
    k_cols = k_bias.shape[0]

    sent_ids = jnp.broadcast_to(token_ids.reshape(1, rows_here), (parties * 4, rows_here))
    every_id = lax.all_to_all(sent_ids, EVERY, split_axis=0, concat_axis=0, tiled=True)
    plane_ids = (
        every_id.reshape(groups, 2, chips, 2, rows_here)
        .transpose(1, 3, 0, 2, 4)
        .reshape(4, plane_rows)
    )
    holder = plane_ids // (2 * vocab_here)
    spot = jnp.arange(plane_rows, dtype=jnp.int32)
    same = plane_ids[:, :, None] == plane_ids[:, None, :]
    leader = jnp.min(jnp.where(same, spot[None, None, :], plane_rows), axis=2)
    leads = leader == spot[None, :]
    before = (
        leads[:, None, :]
        & (holder[:, :, None] == holder[:, None, :])
        & (spot[None, None, :] < leader[:, :, None])
    )
    rank = jnp.sum(before.astype(jnp.int32), axis=2)
    rounds = jnp.max(rank) // ROUND_ROWS + 1
    own_plane = 2 * layer + core
    own_holder = lax.dynamic_index_in_dim(holder, own_plane, 0, keepdims=False)
    own_rank = lax.dynamic_index_in_dim(rank, own_plane, 0, keepdims=False)
    own_offset = plane_ids - (2 * chip + core) * vocab_here
    listed_here = leads & (own_offset >= 0) & (own_offset < vocab_here)
    row_at = jnp.arange(SENT_ROWS, dtype=jnp.int32)
    bias_rows = jnp.where(
        row_at[:, None] == ROUND_ROWS + core,
        jnp.pad(own_bias, (0, width_here - core_cols))[None, :],
        jnp.zeros((), jnp.bfloat16),
    )

    def exchange(turn):
        first = turn * ROUND_ROWS
        wanted_rank = jnp.where(row_at < ROUND_ROWS, first + row_at, -1)
        wanted = listed_here[:, None, :] & (rank[:, None, :] == wanted_rank[None, :, None])
        listed = jnp.max(jnp.where(wanted, own_offset[:, None, :], -1), axis=2)
        picked = jnp.dot(
            (
                listed.reshape(-1, 1) == jnp.arange(vocab_here, dtype=jnp.int32)[None, :]
            ).astype(jnp.bfloat16),
            embedding,
            preferred_element_type=jnp.float32,
        ).astype(jnp.bfloat16)
        picked = picked.reshape(2, 2, SENT_ROWS, width_here) + bias_rows
        mine = jnp.where(core == 0, picked[:, 0], picked[:, 1])
        theirs = jnp.where(core == 0, picked[:, 1], picked[:, 0])
        merged = mine + swap_cores(theirs)
        table = lax.all_to_all(
            jnp.broadcast_to(merged[:, None], (2, chips, SENT_ROWS, width_here)).reshape(
                2 * chips, SENT_ROWS, width_here
            ),
            LAYER,
            split_axis=0,
            concat_axis=0,
            tiled=True,
        ).reshape(2, chips * SENT_ROWS, width_here)
        here = (own_rank >= first) & (own_rank < first + ROUND_ROWS)
        slot = jnp.where(here, own_holder * SENT_ROWS + own_rank - first, -1)
        return slot.reshape(plane_rows, 1), table

    near_gain = lax.dynamic_slice_in_dim(
        norm_gain, lax.axis_index("y") * 2 * width_here, 2 * width_here
    )
    near_gain = near_gain.reshape(2, 1, width_here).astype(jnp.float32)
    slot, table = exchange(0)
    pair_bias = table[0].reshape(chips, SENT_ROWS, width_here)
    pair_bias = pair_bias[:, ROUND_ROWS : ROUND_ROWS + 2, :core_cols].astype(jnp.float32)
    payload = project(place, slot, table, near_gain, weights, chips)

    def further(turn, sofar):
        turn_slot, turn_table = exchange(turn)
        return sofar + project(place, turn_slot, turn_table, near_gain, weights, chips)

    payload = lax.fori_loop(1, rounds, further, payload)
    arrived = lax.all_to_all(payload, PLANE, split_axis=0, concat_axis=0, tiled=True)
    arrived = arrived.reshape(groups, chips, rows_here, -1)
    pair_cols = 2 * core_cols
    inputs = arrived[..., pair_cols:].astype(jnp.float32)
    square = jnp.sum(inputs * inputs, axis=(0, 1, 3))
    scale = lax.rsqrt(square / norm_gain.shape[0] + norm_epsilon)
    summed = jnp.sum(arrived[..., :pair_cols].astype(jnp.float32), axis=0)
    summed = summed.reshape(chips, rows_here, 2, core_cols)
    joined = (summed * scale[None, :, None, None] + pair_bias[:, None]).astype(jnp.bfloat16)
    joined = joined.transpose(1, 0, 2, 3)
    queries = joined[..., :q_cols].reshape(seq_here, step_count, -1, HD)
    fresh_keys = joined[..., q_cols : q_cols + k_cols].reshape(seq_here, step_count, -1, HD)
    fresh_values = joined[..., q_cols + k_cols :].reshape(seq_here, step_count, -1, HD)
    positions = lengths[:, None] + jnp.arange(step_count, dtype=jnp.int32)[None, :]
    rotated = rotate(queries.astype(jnp.float32), positions).astype(jnp.bfloat16)
    new_keys = rotate(fresh_keys.astype(jnp.float32), positions).astype(jnp.bfloat16)
    attended = attend(rotated, new_keys, fresh_values, key_cache, value_cache, lengths)

    spread = attended.reshape(rows_here, chips, 2 * q_cols).transpose(1, 0, 2)
    spread = jnp.broadcast_to(spread[None], (groups,) + spread.shape)
    gathered = lax.all_to_all(
        spread.reshape(parties, rows_here, 2 * q_cols), PLANE, split_axis=0, concat_axis=0, tiled=True
    ).reshape(plane_rows, 2 * q_cols)
    branch = branch_out(place, gathered, o_weights)
    branches = lax.all_to_all(branch, PLANE, split_axis=0, concat_axis=0, tiled=True)
    hidden = hidden_sum(branches.reshape(groups, chips, rows_here, -1), arrived)
    return (
        hidden.reshape(seq_here, step_count, -1),
        new_keys.reshape(seq_here, step_count, -1),
        fresh_values.reshape(seq_here, step_count, -1),
    )


def solution(mesh):
    fine = Mesh(mesh.devices.reshape(4, 2, 2, 4, 2), EVERY)
    tensor = CHIPS + ("core",)
    placed = (
        P(EVERY, None),
        P(EVERY),
        P(tensor, DP),
        P(),
        P(DP, tensor),
        P(DP, tensor),
        P(DP, tensor),
        P(tensor),
        P(tensor),
        P(tensor),
        P(tensor, DP),
        P(EVERY, None, None),
        P(EVERY, None, None),
    )
    return jax.shard_map(
        per_device,
        mesh=fine,
        in_specs=placed,
        out_specs=(
            P(EVERY, None, None),
            P(EVERY, None, None),
            P(EVERY, None, None),
        ),
        check_vma=False,
    )
```

```python
import jax
import jax.numpy as jnp
from jax import lax
from jax.experimental import pallas as pl
from jax.experimental.pallas import tpu as pltpu
from jax.sharding import Mesh
from jax.sharding import PartitionSpec as P

HD = 128
ROUND_ROWS = 72
SENT_ROWS = 80
CHIP_COUNT = 8

norm_epsilon = 1e-06
rope_base = 1000000.0
masked_low = -1e30

DP = ("y", "zl")
CHIPS = ("zh", "x")
LAYER = ("zl", "zh", "x")
PLANE = ("y", "zh", "x")
EVERY = ("y", "zl", "zh", "x", "core")


def swap_cores(value):
    return lax.ppermute(value, "core", [(0, 1), (1, 0)])


def swap_layers(value):
    return lax.ppermute(value, "zl", [(0, 1), (1, 0)])


VMEM = pl.BlockSpec(memory_space=pltpu.VMEM)
SMEM = pl.BlockSpec(memory_space=pltpu.SMEM)


def lookup_kernel(place_ref, id_row_ref, id_col_ref, bias_ref, hold_ref, vocab_ref, *rest):
    mine_ref, theirs_ref, rank_ref, list_ref, total_ref = rest
    step = pl.program_id(0)
    chip, core, first = place_ref[0], place_ref[2], place_ref[3]
    planes, _, rows = id_row_ref.shape
    span = vocab_ref.shape[0]
    vocab_here = span * pl.num_programs(0)

    @pl.when(step == 0)
    def _():
        total_ref[...] = jnp.zeros_like(total_ref)
        across = lax.broadcasted_iota(jnp.int32, (rows, rows), 1)
        down = lax.broadcasted_iota(jnp.int32, (rows, rows), 0)
        slot = lax.broadcasted_iota(jnp.int32, (SENT_ROWS, rows), 0)
        for plane in range(planes):
            id_row = id_row_ref[plane]
            id_col = id_col_ref[plane]
            same = id_row == id_col
            leader_row = jnp.min(jnp.where(same, down, rows), axis=0, keepdims=True)
            leader_col = jnp.min(jnp.where(same, across, rows), axis=1, keepdims=True)
            lead_col = leader_col == lax.broadcasted_iota(jnp.int32, (rows, 1), 0)
            start_row = jnp.zeros_like(id_row)
            start_col = jnp.zeros_like(id_col)
            for other in range(1, CHIP_COUNT):
                edge = other * 2 * vocab_here
                start_row = start_row + (id_row >= edge).astype(jnp.int32)
                start_col = start_col + (id_col >= edge).astype(jnp.int32)
            key_col = jnp.where(lead_col, start_col, -1)
            before = (key_col == start_row) & (down < leader_row)
            rank = jnp.sum(before.astype(jnp.int32), axis=0, keepdims=True)
            rank_ref[plane] = rank
            offset = id_row - (2 * chip + core) * vocab_here
            leads = leader_row == lax.broadcasted_iota(jnp.int32, (1, rows), 1)
            listed = leads & (offset >= 0) & (offset < vocab_here)
            wanted = jnp.where(listed, rank - first, -1)
            chosen = (wanted == slot) & (slot < ROUND_ROWS)
            list_ref[plane * SENT_ROWS : (plane + 1) * SENT_ROWS, :] = jnp.max(
                jnp.where(chosen, offset, -1), axis=1, keepdims=True
            )

    entry = lax.broadcasted_iota(jnp.int32, (planes * SENT_ROWS, span), 1) + step * span
    chosen = (entry == list_ref[...]).astype(jnp.bfloat16)
    total_ref[...] += jnp.dot(chosen, vocab_ref[...], preferred_element_type=jnp.float32)

    @pl.when(step == pl.num_programs(0) - 1)
    def _():
        for layer in range(planes // 2):
            for side, target in ((0, mine_ref), (1, theirs_ref)):
                plane = 2 * layer + (core + side) % 2
                start = pl.multiple_of(plane * SENT_ROWS, SENT_ROWS)
                target[layer] = (total_ref[pl.ds(start, SENT_ROWS), :] + bias_ref[...]).astype(
                    jnp.bfloat16
                )


def look_up(place, plane_ids, bias_rows, held, embedding):
    planes, rows = plane_ids.shape
    vocab_here, width = embedding.shape
    steps = 3
    whole = lambda *dims: pl.BlockSpec(dims, lambda i: (0,) * len(dims))
    return pl.pallas_call(
        lookup_kernel,
        out_shape=(
            jax.ShapeDtypeStruct((planes // 2, SENT_ROWS, width), jnp.bfloat16),
            jax.ShapeDtypeStruct((planes // 2, SENT_ROWS, width), jnp.bfloat16),
            jax.ShapeDtypeStruct((planes, 1, rows), jnp.int32),
        ),
        grid=(steps,),
        in_specs=[
            SMEM,
            whole(planes, 1, rows),
            whole(planes, rows, 1),
            whole(SENT_ROWS, width),
            pl.BlockSpec(memory_space=pl.ANY),
            pl.BlockSpec((vocab_here // steps, width), lambda i: (i, 0)),
        ],
        out_specs=(
            whole(planes // 2, SENT_ROWS, width),
            whole(planes // 2, SENT_ROWS, width),
            whole(planes, 1, rows),
        ),
        scratch_shapes=[
            pltpu.VMEM((planes * SENT_ROWS, 1), jnp.int32),
            pltpu.VMEM((planes * SENT_ROWS, width), jnp.float32),
        ],
        compiler_params=pltpu.CompilerParams(vmem_limit_bytes=48 * 1024 * 1024),
        name="look_up",
    )(place, plane_ids.reshape(planes, 1, rows), plane_ids.reshape(planes, rows, 1), bias_rows, held, embedding)


def attention_kernel(
    arrived_ref, bias_ref, cosine_ref, sine_ref, length_ref, keys_ref, values_ref, *rest
):
    out_ref, new_keys_ref, new_values_ref, key_buf, value_buf, key_sem, value_sem = rest
    groups, chips, rows, _ = arrived_ref.shape
    seqs, cache_len, _ = keys_ref.shape
    steps = rows // seqs
    core_cols = bias_ref.shape[2] // 2
    heads = out_ref.shape[3] // HD
    half_heads = heads // 2
    many = heads * rows
    copies = []
    for seq in range(seqs):
        copies.append(pltpu.make_async_copy(keys_ref.at[seq], key_buf.at[seq], key_sem.at[seq]))
        copies.append(
            pltpu.make_async_copy(values_ref.at[seq], value_buf.at[seq], value_sem.at[seq])
        )
    for copy in copies:
        copy.start()
    square = None
    for group in range(groups):
        for chip in range(chips):
            part = arrived_ref[group, chip, :, 2 * core_cols :].astype(jnp.float32)
            square = part * part if square is None else square + part * part
    width = groups * chips * square.shape[1]
    scale = lax.rsqrt(jnp.sum(square, axis=1, keepdims=True) / width + norm_epsilon)
    cosine = cosine_ref[...]
    sine = sine_ref[...]
    lane = lax.broadcasted_iota(jnp.int32, (rows, HD), 1)

    def rotated(features):
        return (features * cosine + pltpu.roll(features, HD // 2, 1) * sine).astype(jnp.bfloat16)

    row_at = lax.broadcasted_iota(jnp.int32, (many, 1), 0) % rows
    row_seq = row_at // steps
    row_step = row_at % steps
    fresh_at = lax.broadcasted_iota(jnp.int32, (many, rows), 1)
    fresh_valid = (fresh_at // steps == row_seq) & (fresh_at % steps <= row_step)
    cache_valid = lax.broadcasted_iota(jnp.int32, (many, cache_len), 1) < length_ref[...]
    score_scale = HD ** (-0.5)
    for copy in copies:
        copy.wait()
    for chip in range(chips):
        span = slice(chip * HD, (chip + 1) * HD)
        joined = arrived_ref[0, chip, :, : 2 * core_cols].astype(jnp.float32)
        for group in range(1, groups):
            joined = joined + arrived_ref[group, chip, :, : 2 * core_cols].astype(jnp.float32)
        joined = (joined * scale + bias_ref[chip]).astype(jnp.bfloat16).astype(jnp.float32)
        parts = []
        for head in range(heads):
            start = (head // half_heads) * core_cols + (head % half_heads) * HD
            parts.append(rotated(joined[:, start : start + HD]))
        queries = jnp.concatenate(parts, axis=0)
        low = joined[:, core_cols - HD : core_cols]
        high = joined[:, 2 * core_cols - HD :]
        fresh_keys = rotated(jnp.where(lane < HD // 2, low, pltpu.roll(high, HD // 2, 1)))
        fresh_values = jnp.where(lane < HD // 2, pltpu.roll(low, HD // 2, 1), high).astype(
            jnp.bfloat16
        )
        new_keys_ref[:, span] = fresh_keys
        new_values_ref[:, span] = fresh_values
        scores = None
        for seq in range(seqs):
            found = lax.dot_general(
                queries,
                key_buf[seq, :, span],
                (((1,), (1,)), ((), ())),
                preferred_element_type=jnp.float32,
            )
            scores = found if scores is None else jnp.where(row_seq == seq, found, scores)
        fresh_scores = lax.dot_general(
            queries, fresh_keys, (((1,), (1,)), ((), ())), preferred_element_type=jnp.float32
        )
        scores = jnp.where(cache_valid, scores * score_scale, masked_low)
        fresh_scores = jnp.where(fresh_valid, fresh_scores * score_scale, masked_low)
        top = jnp.maximum(
            jnp.max(scores, axis=1, keepdims=True), jnp.max(fresh_scores, axis=1, keepdims=True)
        )
        scores = jnp.exp(scores - top)
        fresh_scores = jnp.exp(fresh_scores - top)
        share = 1.0 / (
            jnp.sum(scores, axis=1, keepdims=True) + jnp.sum(fresh_scores, axis=1, keepdims=True)
        )
        weights = (scores * share).astype(jnp.bfloat16)
        fresh_weights = (fresh_scores * share).astype(jnp.bfloat16)
        attended = jnp.dot(fresh_weights, fresh_values, preferred_element_type=jnp.float32)
        for seq in range(seqs):
            found = jnp.dot(
                weights, value_buf[seq, :, span], preferred_element_type=jnp.float32
            )
            attended = attended + jnp.where(row_seq == seq, found, 0.0)
        attended = attended.astype(jnp.bfloat16)
        for head in range(heads):
            piece = attended[head * rows : (head + 1) * rows]
            for group in range(groups):
                out_ref[group, chip, :, head * HD : (head + 1) * HD] = piece


def attend(arrived, bias, cosine, sine, row_lengths, key_cache, value_cache):
    groups, chips, rows, _ = arrived.shape
    seqs, cache_len, kv_cols = key_cache.shape
    heads = 8
    anywhere = pl.BlockSpec(memory_space=pl.ANY)
    return pl.pallas_call(
        attention_kernel,
        out_shape=(
            jax.ShapeDtypeStruct((groups, chips, rows, heads * HD), jnp.bfloat16),
            jax.ShapeDtypeStruct((rows, kv_cols), jnp.bfloat16),
            jax.ShapeDtypeStruct((rows, kv_cols), jnp.bfloat16),
        ),
        in_specs=[VMEM] * 5 + [anywhere] * 2,
        out_specs=(VMEM, VMEM, VMEM),
        scratch_shapes=[
            pltpu.VMEM(key_cache.shape, jnp.bfloat16),
            pltpu.VMEM(key_cache.shape, jnp.bfloat16),
            pltpu.SemaphoreType.DMA((seqs,)),
            pltpu.SemaphoreType.DMA((seqs,)),
        ],
        compiler_params=pltpu.CompilerParams(vmem_limit_bytes=48 * 1024 * 1024),
        name="attend",
    )(arrived, bias, cosine, sine, row_lengths, key_cache, value_cache)


def projection_kernel(place_ref, slot_ref, table_ref, gain_ref, *rest):
    weight_refs, out_ref, wide_ref, total_ref = rest[:4], rest[4], rest[5], rest[6]
    chip, layer, core = place_ref[0], place_ref[1], place_ref[2]
    rows = slot_ref.shape[0]
    width = table_ref.shape[2]
    table_rows = table_ref.shape[1]
    cols = weight_refs[0].shape[1]
    chosen = (
        lax.broadcasted_iota(jnp.int32, (rows, table_rows), 1) == slot_ref[...]
    ).astype(jnp.bfloat16)
    for flip in range(2):
        block = (layer + flip) % 2
        found = jnp.dot(chosen, table_ref[block], preferred_element_type=jnp.float32)
        wide_ref[:, pl.ds(pl.multiple_of(block * width, width), width)] = found.astype(
            jnp.bfloat16
        )
        gained = (found * gain_ref[block]).astype(jnp.bfloat16)
        for side in range(2):
            product = jnp.dot(
                gained, weight_refs[2 * flip + side][...], preferred_element_type=jnp.float32
            )
            if flip == 0:
                total_ref[side] = product
            else:
                where = pl.multiple_of(((core + side) % 2) * cols, cols)
                out_ref[:, pl.ds(where, cols)] = (total_ref[side] + product).astype(jnp.bfloat16)
    strip = out_ref.shape[1] - 2 * cols
    out_ref[:, 2 * cols :] = wide_ref[:, pl.ds(pl.multiple_of(chip * strip, strip), strip)]


def project(place, slot, table, gain, weights, chips):
    rows = slot.shape[0]
    width = table.shape[2]
    cols = weights[0].shape[1]
    return pl.pallas_call(
        projection_kernel,
        out_shape=jax.ShapeDtypeStruct((rows, 2 * cols + 2 * width // chips), jnp.bfloat16),
        in_specs=[SMEM] + [VMEM] * 7,
        out_specs=VMEM,
        scratch_shapes=[
            pltpu.VMEM((rows, 2 * width), jnp.bfloat16),
            pltpu.VMEM((2, rows, cols), jnp.float32),
        ],
        compiler_params=pltpu.CompilerParams(vmem_limit_bytes=48 * 1024 * 1024),
        name="project",
    )(place, slot, table, gain, *weights)


def branch_kernel(place_ref, rows_ref, *rest):
    weight_refs, out_ref = rest[:4], rest[4]
    layer, core = place_ref[1], place_ref[2]
    depth, width = weight_refs[0].shape
    for flip in range(2):
        block = pl.multiple_of(((layer + flip) % 2) * width, width)
        parts = []
        for side in range(2):
            where = pl.multiple_of(((core + side) % 2) * depth, depth)
            parts.append(
                jnp.dot(
                    rows_ref[:, pl.ds(where, depth)],
                    weight_refs[2 * flip + side][...],
                    preferred_element_type=jnp.float32,
                )
            )
        out_ref[:, pl.ds(block, width)] = (parts[0] + parts[1]).astype(jnp.bfloat16)


def branch_out(place, rows, weights):
    return pl.pallas_call(
        branch_kernel,
        out_shape=jax.ShapeDtypeStruct((rows.shape[0], 2 * weights[0].shape[1]), jnp.bfloat16),
        in_specs=[SMEM] + [VMEM] * 5,
        out_specs=VMEM,
        compiler_params=pltpu.CompilerParams(vmem_limit_bytes=48 * 1024 * 1024),
        name="branch",
    )(place, rows, *weights)


def hidden_kernel(branch_ref, strip_ref, out_ref):
    chips = branch_ref.shape[1]
    strip = strip_ref.shape[3]
    for part in range(chips):
        span = slice(part * strip, (part + 1) * strip)
        total = strip_ref[0, part].astype(jnp.float32)
        for chip in range(chips):
            total = total + branch_ref[0, chip, :, span].astype(jnp.float32)
        out_ref[:, span] = total.astype(jnp.bfloat16)


def hidden_sum(branches, arrived):
    groups, chips, rows, width = branches.shape
    strip = width // chips
    last = arrived.shape[3] // strip - 1
    return pl.pallas_call(
        hidden_kernel,
        out_shape=jax.ShapeDtypeStruct((rows, groups * width), jnp.bfloat16),
        grid=(groups,),
        in_specs=[
            pl.BlockSpec((1, chips, rows, width), lambda y: (y, 0, 0, 0)),
            pl.BlockSpec((1, chips, rows, strip), lambda y: (y, 0, 0, last)),
        ],
        out_specs=pl.BlockSpec((rows, width), lambda y: (0, y)),
        compiler_params=pltpu.CompilerParams(vmem_limit_bytes=48 * 1024 * 1024),
        name="hidden_sum",
    )(branches, arrived)


def per_device(
    token_ids,
    lengths,
    embedding,
    norm_gain,
    q_weight,
    k_weight,
    v_weight,
    q_bias,
    k_bias,
    v_bias,
    o_weight,
    key_cache,
    value_cache,
):
    seq_here, step_count = token_ids.shape
    rows_here = seq_here * step_count
    vocab_here, width_here = embedding.shape
    groups = lax.axis_size("y")
    chips = lax.axis_size(CHIPS)
    chip = lax.axis_index(CHIPS)
    core = lax.axis_index("core")
    layer = lax.axis_index("zl")
    parties = groups * chips
    plane_rows = parties * rows_here
    place = jnp.stack([chip, layer, core]).astype(jnp.int32)

    both = jnp.concatenate([q_weight, k_weight, v_weight], axis=1)
    both_layer = swap_layers(both)
    weights = (both, swap_cores(both), both_layer, swap_cores(both_layer))
    o_layer = swap_layers(o_weight)
    o_weights = (o_weight, swap_cores(o_weight), o_layer, swap_cores(o_layer))
    own_bias = jnp.concatenate([q_bias, k_bias, v_bias])
    core_cols = own_bias.shape[0]
    q_cols = q_bias.shape[0]
    k_cols = k_bias.shape[0]

    sent_ids = jnp.broadcast_to(token_ids.reshape(1, rows_here), (parties * 4, rows_here))
    every_id = lax.all_to_all(sent_ids, EVERY, split_axis=0, concat_axis=0, tiled=True)
    plane_ids = (
        every_id.reshape(groups, 2, chips, 2, rows_here)
        .transpose(1, 3, 0, 2, 4)
        .reshape(4, plane_rows)
    )
    own_plane = 2 * layer + core
    own_holder = lax.dynamic_index_in_dim(plane_ids, own_plane, 0, keepdims=False)
    own_holder = own_holder // (2 * vocab_here)
    row_at = jnp.arange(SENT_ROWS, dtype=jnp.int32)
    bias_rows = jnp.where(
        row_at[:, None] == ROUND_ROWS + core,
        jnp.pad(own_bias, (0, width_here - core_cols))[None, :],
        jnp.zeros((), jnp.bfloat16),
    ).astype(jnp.float32)

    def exchange(turn):
        first = turn * ROUND_ROWS
        turn_place = jnp.concatenate([place, jnp.asarray(first, jnp.int32).reshape(1)])
        mine, theirs, rank = look_up(turn_place, plane_ids, bias_rows, both_layer, embedding)
        merged = mine + swap_cores(theirs)
        table = lax.all_to_all(
            jnp.broadcast_to(merged[:, None], (2, chips, SENT_ROWS, width_here)).reshape(
                2 * chips, SENT_ROWS, width_here
            ),
            LAYER,
            split_axis=0,
            concat_axis=0,
            tiled=True,
        ).reshape(2, chips * SENT_ROWS, width_here)
        own_rank = lax.dynamic_index_in_dim(rank, own_plane, 0, keepdims=False).reshape(-1)
        here = (own_rank >= first) & (own_rank < first + ROUND_ROWS)
        slot = jnp.where(here, own_holder * SENT_ROWS + own_rank - first, -1)
        return slot.reshape(plane_rows, 1), table, jnp.max(rank) // ROUND_ROWS + 1

    near_gain = lax.dynamic_slice_in_dim(
        norm_gain, lax.axis_index("y") * 2 * width_here, 2 * width_here
    )
    near_gain = near_gain.reshape(2, 1, width_here).astype(jnp.float32)
    slot, table, rounds = exchange(0)
    pair_bias = table[0].reshape(chips, SENT_ROWS, width_here)
    pair_bias = pair_bias[:, ROUND_ROWS : ROUND_ROWS + 2, :core_cols].astype(jnp.float32)
    pair_bias = pair_bias.reshape(chips, 1, 2 * core_cols)
    payload = project(place, slot, table, near_gain, weights, chips)

    def further(turn, sofar):
        turn_slot, turn_table, _ = exchange(turn)
        return sofar + project(place, turn_slot, turn_table, near_gain, weights, chips)

    payload = lax.fori_loop(1, rounds, further, payload)
    arrived = lax.all_to_all(payload, PLANE, split_axis=0, concat_axis=0, tiled=True)
    arrived = arrived.reshape(groups, chips, rows_here, -1)
    positions = (lengths[:, None] + jnp.arange(step_count, dtype=jnp.int32)[None, :]).reshape(-1)
    frequency = rope_base ** (-(2.0 * jnp.arange(HD // 2, dtype=jnp.float32)) / HD)
    angles = positions.astype(jnp.float32)[:, None] * frequency
    cosine, sine = jnp.cos(angles), jnp.sin(angles)
    kv_heads = key_cache.shape[2] // HD
    row_lengths = jnp.tile(jnp.repeat(lengths, step_count), 8 * kv_heads // chips).reshape(-1, 1)
    spread, new_keys, new_values = attend(
        arrived,
        pair_bias,
        jnp.concatenate([cosine, cosine], axis=1),
        jnp.concatenate([-sine, sine], axis=1),
        row_lengths,
        key_cache,
        value_cache,
    )

    gathered = lax.all_to_all(
        spread.reshape(parties, rows_here, 2 * q_cols), PLANE, split_axis=0, concat_axis=0, tiled=True
    ).reshape(plane_rows, 2 * q_cols)
    branch = branch_out(place, gathered, o_weights)
    branches = lax.all_to_all(branch, PLANE, split_axis=0, concat_axis=0, tiled=True)
    hidden = hidden_sum(branches.reshape(groups, chips, rows_here, -1), arrived)
    return (
        hidden.reshape(seq_here, step_count, -1),
        new_keys.reshape(seq_here, step_count, -1),
        new_values.reshape(seq_here, step_count, -1),
    )


def solution(mesh):
    fine = Mesh(mesh.devices.reshape(4, 2, 2, 4, 2), EVERY)
    tensor = CHIPS + ("core",)
    placed = (
        P(EVERY, None),
        P(EVERY),
        P(tensor, DP),
        P(),
        P(DP, tensor),
        P(DP, tensor),
        P(DP, tensor),
        P(tensor),
        P(tensor),
        P(tensor),
        P(tensor, DP),
        P(EVERY, None, None),
        P(EVERY, None, None),
    )
    return jax.shard_map(
        per_device,
        mesh=fine,
        in_specs=placed,
        out_specs=(
            P(EVERY, None, None),
            P(EVERY, None, None),
            P(EVERY, None, None),
        ),
        check_vma=False,
    )
```

```python
import jax
import jax.numpy as jnp
from jax import lax
from jax.experimental import pallas as pl
from jax.experimental.pallas import tpu as pltpu
from jax.sharding import Mesh
from jax.sharding import PartitionSpec as P

HD = 128
ROUND_ROWS = 126
SENT_ROWS = 128
CHIP_COUNT = 8

norm_epsilon = 1e-06
rope_base = 1000000.0
masked_low = -1e30

DP = ("y", "zl")
CHIPS = ("zh", "x")
LAYER = ("zl", "zh", "x")
PLANE = ("y", "zl", "zh", "x")
EVERY = ("y", "zl", "zh", "x", "core")


def swap_cores(value):
    return lax.ppermute(value, "core", [(0, 1), (1, 0)])


def shift(value, count, step):
    return lax.ppermute(value, "y", [(i, (i + step) % count) for i in range(count)])


VMEM = pl.BlockSpec(memory_space=pltpu.VMEM)
SMEM = pl.BlockSpec(memory_space=pltpu.SMEM)


def lookup_kernel(place_ref, id_row_ref, id_col_ref, bias_ref, vocab_ref, *rest):
    mine_ref, theirs_ref, rank_ref, list_ref, total_ref = rest
    step = pl.program_id(0)
    chip, core, first = place_ref[0], place_ref[1], place_ref[3]
    planes, _, rows = id_row_ref.shape
    span = vocab_ref.shape[0]
    vocab_here = span * pl.num_programs(0)

    @pl.when(step == 0)
    def _():
        total_ref[...] = jnp.zeros_like(total_ref)
        across = lax.broadcasted_iota(jnp.int32, (rows, rows), 1)
        down = lax.broadcasted_iota(jnp.int32, (rows, rows), 0)
        earlier = across < down
        slot = lax.broadcasted_iota(jnp.int32, (SENT_ROWS, rows), 0)
        for plane in range(planes):
            id_row = id_row_ref[plane]
            id_col = id_col_ref[plane]
            again = jnp.where((id_row == id_col) & earlier, 1, 0)
            key_col = jnp.where(jnp.max(again, axis=1, keepdims=True) == 0, id_col, -1)
            edge_row = jnp.zeros_like(id_row)
            for other in range(1, CHIP_COUNT):
                edge = other * 2 * vocab_here
                edge_row = jnp.where(id_row >= edge, edge, edge_row)
            before = (key_col >= edge_row) & (key_col < id_row)
            rank = jnp.sum(before.astype(jnp.int32), axis=0, keepdims=True)
            rank_ref[plane] = rank
            offset = id_row - (2 * chip + core) * vocab_here
            listed = (offset >= 0) & (offset < vocab_here)
            wanted = jnp.where(listed, rank - first, -1)
            chosen = (wanted == slot) & (slot < ROUND_ROWS)
            list_ref[plane * SENT_ROWS : (plane + 1) * SENT_ROWS, :] = jnp.max(
                jnp.where(chosen, offset, -1), axis=1, keepdims=True
            )

    entry = lax.broadcasted_iota(jnp.int32, (planes * SENT_ROWS, span), 1) + step * span
    chosen = (entry == list_ref[...]).astype(jnp.bfloat16)
    total_ref[...] += jnp.dot(chosen, vocab_ref[...], preferred_element_type=jnp.float32)

    @pl.when(step == pl.num_programs(0) - 1)
    def _():
        for side, target in ((0, mine_ref), (1, theirs_ref)):
            plane = (core + side) % 2
            start = pl.multiple_of(plane * SENT_ROWS, SENT_ROWS)
            target[...] = (total_ref[pl.ds(start, SENT_ROWS), :] + bias_ref[...]).astype(
                jnp.bfloat16
            )


def look_up(place, plane_ids, bias_rows, embedding):
    planes, rows = plane_ids.shape
    vocab_here, width = embedding.shape
    steps = 3
    whole = lambda *dims: pl.BlockSpec(dims, lambda i: (0,) * len(dims))
    return pl.pallas_call(
        lookup_kernel,
        out_shape=(
            jax.ShapeDtypeStruct((SENT_ROWS, width), jnp.bfloat16),
            jax.ShapeDtypeStruct((SENT_ROWS, width), jnp.bfloat16),
            jax.ShapeDtypeStruct((planes, 1, rows), jnp.int32),
        ),
        grid=(steps,),
        in_specs=[
            SMEM,
            whole(planes, 1, rows),
            whole(planes, rows, 1),
            whole(SENT_ROWS, width),
            pl.BlockSpec((vocab_here // steps, width), lambda i: (i, 0)),
        ],
        out_specs=(
            whole(SENT_ROWS, width),
            whole(SENT_ROWS, width),
            whole(planes, 1, rows),
        ),
        scratch_shapes=[
            pltpu.VMEM((planes * SENT_ROWS, 1), jnp.int32),
            pltpu.VMEM((planes * SENT_ROWS, width), jnp.float32),
        ],
        compiler_params=pltpu.CompilerParams(vmem_limit_bytes=48 * 1024 * 1024),
        name="look_up",
    )(place, plane_ids.reshape(planes, 1, rows), plane_ids.reshape(planes, rows, 1), bias_rows, embedding)


def attention_kernel(
    arrived_ref, bias_ref, cosine_ref, sine_ref, length_ref, keys_ref, values_ref, *rest
):
    out_ref, new_keys_ref, new_values_ref, key_buf, value_buf, key_sem, value_sem = rest
    groups, chips, rows, _ = arrived_ref.shape
    seqs, cache_len, _ = keys_ref.shape
    steps = rows // seqs
    core_cols = bias_ref.shape[2] // 2
    heads = out_ref.shape[3] // HD
    half_heads = heads // 2
    many = heads * rows
    copies = []
    for seq in range(seqs):
        copies.append(pltpu.make_async_copy(keys_ref.at[seq], key_buf.at[seq], key_sem.at[seq]))
        copies.append(
            pltpu.make_async_copy(values_ref.at[seq], value_buf.at[seq], value_sem.at[seq])
        )
    for copy in copies:
        copy.start()
    square = None
    for group in range(groups):
        for chip in range(chips):
            part = arrived_ref[group, chip, :, 2 * core_cols :].astype(jnp.float32)
            square = part * part if square is None else square + part * part
    width = groups * chips * square.shape[1]
    scale = lax.rsqrt(jnp.sum(square, axis=1, keepdims=True) / width + norm_epsilon)
    cosine = cosine_ref[...]
    sine = sine_ref[...]
    lane = lax.broadcasted_iota(jnp.int32, (rows, HD), 1)

    def rotated(features):
        return (features * cosine + pltpu.roll(features, HD // 2, 1) * sine).astype(jnp.bfloat16)

    row_at = lax.broadcasted_iota(jnp.int32, (many, 1), 0) % rows
    row_seq = row_at // steps
    row_step = row_at % steps
    fresh_at = lax.broadcasted_iota(jnp.int32, (many, rows), 1)
    fresh_valid = (fresh_at // steps == row_seq) & (fresh_at % steps <= row_step)
    cache_valid = lax.broadcasted_iota(jnp.int32, (many, cache_len), 1) < length_ref[...]
    score_scale = HD ** (-0.5)
    for copy in copies:
        copy.wait()
    for chip in range(chips):
        span = slice(chip * HD, (chip + 1) * HD)
        joined = arrived_ref[0, chip, :, : 2 * core_cols].astype(jnp.float32)
        for group in range(1, groups):
            joined = joined + arrived_ref[group, chip, :, : 2 * core_cols].astype(jnp.float32)
        joined = (joined * scale + bias_ref[chip]).astype(jnp.bfloat16).astype(jnp.float32)
        parts = []
        for head in range(heads):
            start = (head // half_heads) * core_cols + (head % half_heads) * HD
            parts.append(rotated(joined[:, start : start + HD]))
        queries = jnp.concatenate(parts, axis=0)
        low = joined[:, core_cols - HD : core_cols]
        high = joined[:, 2 * core_cols - HD :]
        fresh_keys = rotated(jnp.where(lane < HD // 2, low, pltpu.roll(high, HD // 2, 1)))
        fresh_values = jnp.where(lane < HD // 2, pltpu.roll(low, HD // 2, 1), high).astype(
            jnp.bfloat16
        )
        new_keys_ref[:, span] = fresh_keys
        new_values_ref[:, span] = fresh_values
        scores = None
        for seq in range(seqs):
            found = lax.dot_general(
                queries,
                key_buf[seq, :, span],
                (((1,), (1,)), ((), ())),
                preferred_element_type=jnp.float32,
            )
            scores = found if scores is None else jnp.where(row_seq == seq, found, scores)
        fresh_scores = lax.dot_general(
            queries, fresh_keys, (((1,), (1,)), ((), ())), preferred_element_type=jnp.float32
        )
        scores = jnp.where(cache_valid, scores * score_scale, masked_low)
        fresh_scores = jnp.where(fresh_valid, fresh_scores * score_scale, masked_low)
        top = jnp.maximum(
            jnp.max(scores, axis=1, keepdims=True), jnp.max(fresh_scores, axis=1, keepdims=True)
        )
        scores = jnp.exp(scores - top)
        fresh_scores = jnp.exp(fresh_scores - top)
        share = 1.0 / (
            jnp.sum(scores, axis=1, keepdims=True) + jnp.sum(fresh_scores, axis=1, keepdims=True)
        )
        weights = (scores * share).astype(jnp.bfloat16)
        fresh_weights = (fresh_scores * share).astype(jnp.bfloat16)
        attended = jnp.dot(fresh_weights, fresh_values, preferred_element_type=jnp.float32)
        for seq in range(seqs):
            found = jnp.dot(
                weights, value_buf[seq, :, span], preferred_element_type=jnp.float32
            )
            attended = attended + jnp.where(row_seq == seq, found, 0.0)
        attended = attended.astype(jnp.bfloat16)
        for head in range(heads):
            piece = attended[head * rows : (head + 1) * rows]
            for group in range(out_ref.shape[0]):
                out_ref[group, chip, :, head * HD : (head + 1) * HD] = piece


def attend(arrived, bias, cosine, sine, row_lengths, key_cache, value_cache, copies):
    _, chips, rows, _ = arrived.shape
    seqs, cache_len, kv_cols = key_cache.shape
    heads = 8
    anywhere = pl.BlockSpec(memory_space=pl.ANY)
    return pl.pallas_call(
        attention_kernel,
        out_shape=(
            jax.ShapeDtypeStruct((copies, chips, rows, heads * HD), jnp.bfloat16),
            jax.ShapeDtypeStruct((rows, kv_cols), jnp.bfloat16),
            jax.ShapeDtypeStruct((rows, kv_cols), jnp.bfloat16),
        ),
        in_specs=[VMEM] * 5 + [anywhere] * 2,
        out_specs=(VMEM, VMEM, VMEM),
        scratch_shapes=[
            pltpu.VMEM(key_cache.shape, jnp.bfloat16),
            pltpu.VMEM(key_cache.shape, jnp.bfloat16),
            pltpu.SemaphoreType.DMA((seqs,)),
            pltpu.SemaphoreType.DMA((seqs,)),
        ],
        compiler_params=pltpu.CompilerParams(vmem_limit_bytes=48 * 1024 * 1024),
        name="attend",
    )(arrived, bias, cosine, sine, row_lengths, key_cache, value_cache)


def projection_kernel(place_ref, slot_ref, table_ref, gain_ref, mine_ref, theirs_ref, *rest):
    out_ref, wide_ref, weight_buf, sem = rest[-4:]
    chip, core = place_ref[0], place_ref[1]
    rows = slot_ref.shape[0]
    table_rows = table_ref.shape[0]
    cols = mine_ref.shape[1]
    step = pl.program_id(0)
    copies = [
        pltpu.make_async_copy(source, weight_buf.at[side], sem.at[side])
        for side, source in enumerate((mine_ref, theirs_ref))
    ]

    @pl.when(step == 0)
    def _():
        for copy in copies:
            copy.start()

    chosen = (
        lax.broadcasted_iota(jnp.int32, (rows, table_rows), 1) == slot_ref[...]
    ).astype(jnp.bfloat16)
    found = jnp.dot(chosen, table_ref[...], preferred_element_type=jnp.float32)
    wide_ref[...] = found.astype(jnp.bfloat16)
    gained = (found * gain_ref[...]).astype(jnp.bfloat16)

    @pl.when(step == 0)
    def _():
        for copy in copies:
            copy.wait()

    for side in range(2):
        product = jnp.dot(gained, weight_buf[side], preferred_element_type=jnp.float32)
        where = pl.multiple_of(((core + side) % 2) * cols, cols)
        out_ref[:, pl.ds(where, cols)] = product.astype(jnp.bfloat16)
    strip = out_ref.shape[1] - 2 * cols
    out_ref[:, 2 * cols :] = wide_ref[:, pl.ds(pl.multiple_of(chip * strip, strip), strip)]


def project(place, slot, table, gain, mine, theirs, held, chips):
    rows = slot.shape[0]
    table_rows, width = table.shape
    cols = mine.shape[1]
    out_cols = 2 * cols + width // chips
    block = 256
    anywhere = pl.BlockSpec(memory_space=pl.ANY)
    return pl.pallas_call(
        projection_kernel,
        out_shape=jax.ShapeDtypeStruct((rows, out_cols), jnp.bfloat16),
        grid=(rows // block,),
        in_specs=[
            SMEM,
            pl.BlockSpec((block, 1), lambda i: (i, 0)),
            pl.BlockSpec((table_rows, width), lambda i: (0, 0)),
            pl.BlockSpec((1, width), lambda i: (0, 0)),
        ]
        + [anywhere] * (2 + len(held)),
        out_specs=pl.BlockSpec((block, out_cols), lambda i: (i, 0)),
        scratch_shapes=[
            pltpu.VMEM((block, width), jnp.bfloat16),
            pltpu.VMEM((2, width, cols), jnp.bfloat16),
            pltpu.SemaphoreType.DMA((2,)),
        ],
        compiler_params=pltpu.CompilerParams(vmem_limit_bytes=48 * 1024 * 1024),
        name="project",
    )(place, slot, table, gain, mine, theirs, *held)


def branch_kernel(place_ref, rows_ref, *rest):
    weight_refs, (out_ref, weight_buf, sem) = rest[:-3], rest[-3:]
    core, line = place_ref[1], place_ref[2]
    depth, width = weight_refs[0].shape
    count = len(weight_refs) // 2
    copies = [
        pltpu.make_async_copy(source, weight_buf.at[k], sem.at[k])
        for k, source in enumerate(weight_refs)
    ]
    for copy in copies:
        copy.start()
    for turn in range(count):
        block = pl.multiple_of(((line + count - turn) % count) * width, width)
        parts = []
        for side in range(2):
            where = pl.multiple_of(((core + side) % 2) * depth, depth)
            copies[2 * turn + side].wait()
            parts.append(
                jnp.dot(
                    rows_ref[:, pl.ds(where, depth)],
                    weight_buf[2 * turn + side],
                    preferred_element_type=jnp.float32,
                )
            )
        out_ref[:, pl.ds(block, width)] = (parts[0] + parts[1]).astype(jnp.bfloat16)


def branch_out(place, rows, weights):
    count = len(weights)
    depth, width = weights[0].shape
    return pl.pallas_call(
        branch_kernel,
        out_shape=jax.ShapeDtypeStruct((rows.shape[0], count // 2 * width), jnp.bfloat16),
        in_specs=[SMEM, VMEM] + [pl.BlockSpec(memory_space=pl.ANY)] * count,
        out_specs=VMEM,
        scratch_shapes=[
            pltpu.VMEM((count, depth, width), jnp.bfloat16),
            pltpu.SemaphoreType.DMA((count,)),
        ],
        compiler_params=pltpu.CompilerParams(vmem_limit_bytes=48 * 1024 * 1024),
        name="branch",
    )(place, rows, *weights)


def hidden_kernel(branch_ref, strip_ref, out_ref):
    layers, chips, _, width = branch_ref.shape
    strip = strip_ref.shape[3]
    for layer in range(layers):
        for part in range(width // strip):
            span = slice(part * strip, (part + 1) * strip)
            total = strip_ref[layer, part].astype(jnp.float32)
            for chip in range(chips):
                total = total + branch_ref[layer, chip, :, span].astype(jnp.float32)
            start = layer * width + part * strip
            out_ref[:, start : start + strip] = total.astype(jnp.bfloat16)


def hidden_sum(branches, arrived, width):
    layers, chips, rows, all_width = branches.shape
    groups = all_width // width
    strip = width // chips
    last = arrived.shape[3] // strip - 1
    return pl.pallas_call(
        hidden_kernel,
        out_shape=jax.ShapeDtypeStruct((rows, layers * all_width), jnp.bfloat16),
        grid=(groups,),
        in_specs=[
            pl.BlockSpec((layers, chips, rows, width), lambda y: (0, 0, 0, y)),
            pl.BlockSpec((layers, chips, rows, strip), lambda y: (y, 0, 0, last)),
        ],
        out_specs=pl.BlockSpec((rows, layers * width), lambda y: (0, y)),
        compiler_params=pltpu.CompilerParams(vmem_limit_bytes=48 * 1024 * 1024),
        name="hidden_sum",
    )(branches, arrived)


def per_device(
    token_ids,
    lengths,
    embedding,
    norm_gain,
    q_weight,
    k_weight,
    v_weight,
    q_bias,
    k_bias,
    v_bias,
    o_weight,
    key_cache,
    value_cache,
):
    seq_here, step_count = token_ids.shape
    rows_here = seq_here * step_count
    vocab_here, width_here = embedding.shape
    lines = lax.axis_size("y")
    line = lax.axis_index("y")
    replicas = lax.axis_size(DP)
    chips = lax.axis_size(CHIPS)
    chip = lax.axis_index(CHIPS)
    core = lax.axis_index("core")
    parties = replicas * chips
    plane_rows = parties * rows_here
    place = jnp.stack([chip, core, line]).astype(jnp.int32)

    both = jnp.concatenate([q_weight, k_weight, v_weight], axis=1)
    both_other = swap_cores(both)
    o_lines = [o_weight, shift(o_weight, lines, 1), None, shift(o_weight, lines, -1)]
    o_lines[2] = shift(o_lines[1], lines, 1)
    o_held = (o_lines[1], o_lines[3])
    o_weights = [piece for own in o_lines for piece in (own, swap_cores(own))]
    own_bias = jnp.concatenate([q_bias, k_bias, v_bias])
    core_cols = own_bias.shape[0]
    q_cols = q_bias.shape[0]

    sent_ids = jnp.broadcast_to(token_ids.reshape(1, rows_here), (parties * 2, rows_here))
    every_id = lax.all_to_all(sent_ids, EVERY, split_axis=0, concat_axis=0, tiled=True)
    plane_ids = every_id.reshape(parties, 2, rows_here).transpose(1, 0, 2).reshape(2, plane_rows)
    own_holder = lax.dynamic_index_in_dim(plane_ids, core, 0, keepdims=False) // (2 * vocab_here)
    row_at = jnp.arange(SENT_ROWS, dtype=jnp.int32)
    bias_rows = jnp.where(
        row_at[:, None] == ROUND_ROWS + core,
        jnp.pad(own_bias, (0, width_here - core_cols))[None, :],
        jnp.zeros((), jnp.bfloat16),
    ).astype(jnp.float32)

    def exchange(turn):
        first = turn * ROUND_ROWS
        turn_place = jnp.concatenate([place, jnp.asarray(first, jnp.int32).reshape(1)])
        mine, theirs, rank = look_up(turn_place, plane_ids, bias_rows, embedding)
        merged = mine + swap_cores(theirs)
        table = lax.all_to_all(
            jnp.broadcast_to(merged[None], (chips, SENT_ROWS, width_here)),
            CHIPS,
            split_axis=0,
            concat_axis=0,
            tiled=True,
        ).reshape(chips * SENT_ROWS, width_here)
        own_rank = lax.dynamic_index_in_dim(rank, core, 0, keepdims=False).reshape(-1)
        here = (own_rank >= first) & (own_rank < first + ROUND_ROWS)
        slot = jnp.where(here, own_holder * SENT_ROWS + own_rank - first, -1)
        return slot.reshape(plane_rows, 1), table, jnp.max(rank) // ROUND_ROWS + 1

    own_gain = lax.dynamic_slice_in_dim(norm_gain, lax.axis_index(DP) * width_here, width_here)
    own_gain = own_gain.reshape(1, width_here).astype(jnp.float32)
    slot, table, rounds = exchange(0)
    pair_bias = table.reshape(chips, SENT_ROWS, width_here)
    pair_bias = pair_bias[:, ROUND_ROWS : ROUND_ROWS + 2, :core_cols].astype(jnp.float32)
    pair_bias = pair_bias.reshape(chips, 1, 2 * core_cols)
    payload = project(place, slot, table, own_gain, both, both_other, o_held, chips)

    def further(turn, sofar):
        turn_slot, turn_table, _ = exchange(turn)
        return sofar + project(
            place, turn_slot, turn_table, own_gain, both, both_other, (), chips
        )

    payload = lax.fori_loop(1, rounds, further, payload)
    arrived = lax.all_to_all(payload, PLANE, split_axis=0, concat_axis=0, tiled=True)
    arrived = arrived.reshape(replicas, chips, rows_here, -1)
    positions = (lengths[:, None] + jnp.arange(step_count, dtype=jnp.int32)[None, :]).reshape(-1)
    frequency = rope_base ** (-(2.0 * jnp.arange(HD // 2, dtype=jnp.float32)) / HD)
    angles = positions.astype(jnp.float32)[:, None] * frequency
    cosine, sine = jnp.cos(angles), jnp.sin(angles)
    kv_heads = key_cache.shape[2] // HD
    row_lengths = jnp.tile(jnp.repeat(lengths, step_count), 8 * kv_heads // chips).reshape(-1, 1)
    spread, new_keys, new_values = attend(
        arrived,
        pair_bias,
        jnp.concatenate([cosine, cosine], axis=1),
        jnp.concatenate([-sine, sine], axis=1),
        row_lengths,
        key_cache,
        value_cache,
        replicas // lines,
    )

    gathered = lax.all_to_all(
        spread.reshape(-1, rows_here, 2 * q_cols), LAYER, split_axis=0, concat_axis=0, tiled=True
    ).reshape(-1, 2 * q_cols)
    branch = branch_out(place, gathered, o_weights)
    branches = lax.all_to_all(branch, LAYER, split_axis=0, concat_axis=0, tiled=True)
    branches = branches.reshape(replicas // lines, chips, rows_here, -1)
    hidden = hidden_sum(branches, arrived, o_weight.shape[1])
    return (
        hidden.reshape(seq_here, step_count, -1),
        new_keys.reshape(seq_here, step_count, -1),
        new_values.reshape(seq_here, step_count, -1),
    )


def solution(mesh):
    fine = Mesh(mesh.devices.reshape(4, 2, 2, 4, 2), EVERY)
    tensor = CHIPS + ("core",)
    placed = (
        P(EVERY, None),
        P(EVERY),
        P(tensor, DP),
        P(),
        P(DP, tensor),
        P(DP, tensor),
        P(DP, tensor),
        P(tensor),
        P(tensor),
        P(tensor),
        P(tensor, DP),
        P(EVERY, None, None),
        P(EVERY, None, None),
    )
    return jax.shard_map(
        per_device,
        mesh=fine,
        in_specs=placed,
        out_specs=(
            P(EVERY, None, None),
            P(EVERY, None, None),
            P(EVERY, None, None),
        ),
        check_vma=False,
    )
```

```python
import functools

import jax
import jax.numpy as jnp
from jax import lax
from jax.experimental import pallas as pl
from jax.experimental.pallas import tpu as pltpu
from jax.sharding import Mesh
from jax.sharding import PartitionSpec as P

HD = 128
ROUND_ROWS = 126
SENT_ROWS = 128
CHIP_COUNT = 8
HALVES = 1

norm_epsilon = 1e-06
rope_base = 1000000.0
masked_low = -1e30

DP = ("yh", "yl", "zl")
CHIPS = ("zh", "x")
LAYER = ("yh", "zl", "zh", "x")
PLANE = ("yh", "yl", "zl", "zh", "x")
EVERY = ("yh", "yl", "zl", "zh", "x", "core")


def swap_cores(value):
    return lax.ppermute(value, "core", [(0, 1), (1, 0)])


def swap_lines(value):
    return lax.ppermute(value, "yl", [(0, 1), (1, 0)])


VMEM = pl.BlockSpec(memory_space=pltpu.VMEM)
SMEM = pl.BlockSpec(memory_space=pltpu.SMEM)
HBM = pl.BlockSpec(memory_space=pltpu.HBM)


def lookup_kernel(place_ref, id_row_ref, id_col_ref, bias_ref, vocab_ref, *rest):
    mine_ref, theirs_ref, rank_ref, list_ref, total_ref = rest
    step = pl.program_id(0)
    chip, core, first = place_ref[0], place_ref[1], place_ref[3]
    planes, _, rows = id_row_ref.shape
    span = vocab_ref.shape[0]
    vocab_here = span * pl.num_programs(0)

    @pl.when(step == 0)
    def _():
        total_ref[...] = jnp.zeros_like(total_ref)
        across = lax.broadcasted_iota(jnp.int32, (rows, rows), 1)
        down = lax.broadcasted_iota(jnp.int32, (rows, rows), 0)
        earlier = across < down
        slot = lax.broadcasted_iota(jnp.int32, (SENT_ROWS, rows), 0)
        for plane in range(planes):
            id_row = id_row_ref[plane]
            id_col = id_col_ref[plane]
            again = jnp.where((id_row == id_col) & earlier, 1, 0)
            key_col = jnp.where(jnp.max(again, axis=1, keepdims=True) == 0, id_col, -1)
            edge_row = jnp.zeros_like(id_row)
            for other in range(1, CHIP_COUNT):
                edge = other * 2 * vocab_here
                edge_row = jnp.where(id_row >= edge, edge, edge_row)
            before = (key_col >= edge_row) & (key_col < id_row)
            rank = jnp.sum(before.astype(jnp.int32), axis=0, keepdims=True)
            rank_ref[plane] = rank
            offset = id_row - (2 * chip + core) * vocab_here
            listed = (offset >= 0) & (offset < vocab_here)
            wanted = jnp.where(listed, rank - first, -1)
            chosen = (wanted == slot) & (slot < ROUND_ROWS)
            list_ref[plane * SENT_ROWS : (plane + 1) * SENT_ROWS, :] = jnp.max(
                jnp.where(chosen, offset, -1), axis=1, keepdims=True
            )

    entry = lax.broadcasted_iota(jnp.int32, (planes * SENT_ROWS, span), 1) + step * span
    chosen = (entry == list_ref[...]).astype(jnp.bfloat16)
    total_ref[...] += jnp.dot(chosen, vocab_ref[...], preferred_element_type=jnp.float32)

    @pl.when(step == pl.num_programs(0) - 1)
    def _():
        for side, target in ((0, mine_ref), (1, theirs_ref)):
            plane = (core + side) % 2
            start = pl.multiple_of(plane * SENT_ROWS, SENT_ROWS)
            target[...] = (total_ref[pl.ds(start, SENT_ROWS), :] + bias_ref[...]).astype(
                jnp.bfloat16
            )


def look_up(place, plane_ids, bias_rows, embedding):
    planes, rows = plane_ids.shape
    vocab_here, width = embedding.shape
    steps = 3
    whole = lambda *dims: pl.BlockSpec(dims, lambda i: (0,) * len(dims))
    return pl.pallas_call(
        lookup_kernel,
        out_shape=(
            jax.ShapeDtypeStruct((SENT_ROWS, width), jnp.bfloat16),
            jax.ShapeDtypeStruct((SENT_ROWS, width), jnp.bfloat16),
            jax.ShapeDtypeStruct((planes, 1, rows), jnp.int32),
        ),
        grid=(steps,),
        in_specs=[
            SMEM,
            whole(planes, 1, rows),
            whole(planes, rows, 1),
            whole(SENT_ROWS, width),
            pl.BlockSpec((vocab_here // steps, width), lambda i: (i, 0)),
        ],
        out_specs=(
            whole(SENT_ROWS, width),
            whole(SENT_ROWS, width),
            whole(planes, 1, rows),
        ),
        scratch_shapes=[
            pltpu.VMEM((planes * SENT_ROWS, 1), jnp.int32),
            pltpu.VMEM((planes * SENT_ROWS, width), jnp.float32),
        ],
        compiler_params=pltpu.CompilerParams(vmem_limit_bytes=48 * 1024 * 1024),
        name="look_up",
    )(place, plane_ids.reshape(planes, 1, rows), plane_ids.reshape(planes, rows, 1), bias_rows, embedding)


def attention_kernel(
    half,
    arrived_ref, bias_ref, cosine_ref, sine_ref, length_ref, keys_ref, values_ref, *rest
):
    out_ref, new_keys_ref, new_values_ref, key_buf, value_buf, key_sem, value_sem = rest
    groups, chips, rows, _ = arrived_ref.shape
    seqs, cache_len, _ = key_buf.shape
    steps = rows // seqs
    core_cols = bias_ref.shape[2] // 2
    heads = out_ref.shape[3] // HD
    half_heads = heads // 2
    many = heads * rows
    copies = []
    for seq in range(seqs):
        copies.append(pltpu.make_async_copy(keys_ref.at[half * seqs + seq], key_buf.at[seq], key_sem.at[seq]))
        copies.append(
            pltpu.make_async_copy(
                values_ref.at[half * seqs + seq], value_buf.at[seq], value_sem.at[seq]
            )
        )
    for copy in copies:
        copy.start()
    square = None
    for group in range(groups):
        for chip in range(chips):
            part = arrived_ref[group, chip, :, 2 * core_cols :].astype(jnp.float32)
            square = part * part if square is None else square + part * part
    width = groups * chips * square.shape[1]
    scale = lax.rsqrt(jnp.sum(square, axis=1, keepdims=True) / width + norm_epsilon)
    cosine = cosine_ref[...]
    sine = sine_ref[...]
    lane = lax.broadcasted_iota(jnp.int32, (rows, HD), 1)

    def rotated(features):
        return features * cosine + pltpu.roll(features, HD // 2, 1) * sine

    row_at = lax.broadcasted_iota(jnp.int32, (many, 1), 0) % rows
    row_seq = row_at // steps
    row_step = row_at % steps
    fresh_at = lax.broadcasted_iota(jnp.int32, (many, rows), 1)
    fresh_valid = (fresh_at // steps == row_seq) & (fresh_at % steps <= row_step)
    cache_valid = lax.broadcasted_iota(jnp.int32, (many, cache_len), 1) < length_ref[...]
    score_scale = HD ** (-0.5)
    for copy in copies:
        copy.wait()
    for chip in range(chips):
        span = slice(chip * HD, (chip + 1) * HD)
        joined = arrived_ref[0, chip, :, : 2 * core_cols].astype(jnp.float32)
        for group in range(1, groups):
            joined = joined + arrived_ref[group, chip, :, : 2 * core_cols].astype(jnp.float32)
        joined = (joined * scale + bias_ref[chip]).astype(jnp.bfloat16).astype(jnp.float32)
        parts = []
        for head in range(heads):
            start = (head // half_heads) * core_cols + (head % half_heads) * HD
            parts.append(rotated(joined[:, start : start + HD]))
        queries = jnp.concatenate(parts, axis=0).astype(jnp.bfloat16)
        low = joined[:, core_cols - HD : core_cols]
        high = joined[:, 2 * core_cols - HD :]
        fresh_keys = rotated(jnp.where(lane < HD // 2, low, pltpu.roll(high, HD // 2, 1))).astype(
            jnp.bfloat16
        )
        fresh_values = jnp.where(lane < HD // 2, pltpu.roll(low, HD // 2, 1), high).astype(
            jnp.bfloat16
        )
        new_keys_ref[:, span] = fresh_keys
        new_values_ref[:, span] = fresh_values
        scores = None
        for seq in range(seqs):
            found = lax.dot_general(
                queries,
                key_buf[seq, :, span],
                (((1,), (1,)), ((), ())),
                preferred_element_type=jnp.float32,
            )
            scores = found if scores is None else jnp.where(row_seq == seq, found, scores)
        fresh_scores = lax.dot_general(
            queries, fresh_keys, (((1,), (1,)), ((), ())), preferred_element_type=jnp.float32
        )
        scores = jnp.where(cache_valid, scores * score_scale, masked_low)
        fresh_scores = jnp.where(fresh_valid, fresh_scores * score_scale, masked_low)
        top = jnp.maximum(
            jnp.max(scores, axis=1, keepdims=True), jnp.max(fresh_scores, axis=1, keepdims=True)
        )
        scores = jnp.exp(scores - top)
        fresh_scores = jnp.exp(fresh_scores - top)
        share = 1.0 / (
            jnp.sum(scores, axis=1, keepdims=True) + jnp.sum(fresh_scores, axis=1, keepdims=True)
        )
        weights = (scores * share).astype(jnp.bfloat16)
        fresh_weights = (fresh_scores * share).astype(jnp.bfloat16)
        attended = jnp.dot(fresh_weights, fresh_values, preferred_element_type=jnp.float32)
        for seq in range(seqs):
            found = jnp.dot(
                weights, value_buf[seq, :, span], preferred_element_type=jnp.float32
            )
            attended = attended + jnp.where(row_seq == seq, found, 0.0)
        for head in range(heads):
            piece = attended[head * rows : (head + 1) * rows].astype(jnp.bfloat16)
            for group in range(out_ref.shape[0]):
                out_ref[group, chip, :, head * HD : (head + 1) * HD] = piece


def attend(half, arrived, bias, cosine, sine, row_lengths, key_cache, value_cache, copies):
    _, chips, rows, _ = arrived.shape
    seqs, cache_len, kv_cols = key_cache.shape
    seqs = seqs // HALVES
    heads = 8
    return pl.pallas_call(
        functools.partial(attention_kernel, half),
        out_shape=(
            jax.ShapeDtypeStruct((copies, chips, rows, heads * HD), jnp.bfloat16),
            jax.ShapeDtypeStruct((rows, kv_cols), jnp.bfloat16),
            jax.ShapeDtypeStruct((rows, kv_cols), jnp.bfloat16),
        ),
        in_specs=[VMEM] * 5 + [HBM] * 2,
        out_specs=(VMEM, VMEM, VMEM),
        scratch_shapes=[
            pltpu.VMEM((seqs, cache_len, kv_cols), jnp.bfloat16),
            pltpu.VMEM((seqs, cache_len, kv_cols), jnp.bfloat16),
            pltpu.SemaphoreType.DMA((seqs,)),
            pltpu.SemaphoreType.DMA((seqs,)),
        ],
        compiler_params=pltpu.CompilerParams(vmem_limit_bytes=48 * 1024 * 1024),
        name="attend",
    )(arrived, bias, cosine, sine, row_lengths, key_cache, value_cache)


def projection_kernel(place_ref, slot_ref, table_ref, gain_ref, mine_ref, theirs_ref, *rest):
    out_ref, wide_ref, weight_buf, sem = rest[-4:]
    chip, core = place_ref[0], place_ref[1]
    rows = slot_ref.shape[0]
    table_rows = table_ref.shape[0]
    cols = mine_ref.shape[1]
    step = pl.program_id(0)
    copies = [
        pltpu.make_async_copy(source, weight_buf.at[side], sem.at[side])
        for side, source in enumerate((mine_ref, theirs_ref))
    ]

    @pl.when(step == 0)
    def _():
        for copy in copies:
            copy.start()

    chosen = (
        lax.broadcasted_iota(jnp.int32, (rows, table_rows), 1) == slot_ref[...]
    ).astype(jnp.bfloat16)
    found = jnp.dot(chosen, table_ref[...], preferred_element_type=jnp.float32)
    wide_ref[...] = found.astype(jnp.bfloat16)
    gained = (found * gain_ref[...]).astype(jnp.bfloat16)

    @pl.when(step == 0)
    def _():
        for copy in copies:
            copy.wait()

    for side in range(2):
        product = jnp.dot(gained, weight_buf[side], preferred_element_type=jnp.float32)
        where = pl.multiple_of(((core + side) % 2) * cols, cols)
        out_ref[:, pl.ds(where, cols)] = product.astype(jnp.bfloat16)
    strip = out_ref.shape[1] - 2 * cols
    out_ref[:, 2 * cols :] = wide_ref[:, pl.ds(pl.multiple_of(chip * strip, strip), strip)]


def project(place, slot, table, gain, mine, theirs, held, chips):
    rows = slot.shape[0]
    table_rows, width = table.shape
    cols = mine.shape[1]
    out_cols = 2 * cols + width // chips
    block = 256
    return pl.pallas_call(
        projection_kernel,
        out_shape=jax.ShapeDtypeStruct((rows, out_cols), jnp.bfloat16),
        grid=(rows // block,),
        in_specs=[
            SMEM,
            pl.BlockSpec((block, 1), lambda i: (i, 0)),
            pl.BlockSpec((table_rows, width), lambda i: (0, 0)),
            pl.BlockSpec((1, width), lambda i: (0, 0)),
        ]
        + [HBM] * (2 + len(held)),
        out_specs=pl.BlockSpec((block, out_cols), lambda i: (i, 0)),
        scratch_shapes=[
            pltpu.VMEM((block, width), jnp.bfloat16),
            pltpu.VMEM((2, width, cols), jnp.bfloat16),
            pltpu.SemaphoreType.DMA((2,)),
        ],
        compiler_params=pltpu.CompilerParams(vmem_limit_bytes=48 * 1024 * 1024),
        name="project",
    )(place, slot, table, gain, mine, theirs, *held)


def branch_kernel(place_ref, rows_ref, *rest):
    weight_refs, (out_ref, weight_buf, sem) = rest[:-3], rest[-3:]
    core, line = place_ref[1], place_ref[2]
    depth, width = weight_refs[0].shape
    count = len(weight_refs) // 2
    copies = [
        pltpu.make_async_copy(source, weight_buf.at[k], sem.at[k])
        for k, source in enumerate(weight_refs)
    ]
    for copy in copies:
        copy.start()
    for turn in range(count):
        block = pl.multiple_of(((line + count - turn) % count) * width, width)
        parts = []
        for side in range(2):
            where = pl.multiple_of(((core + side) % 2) * depth, depth)
            copies[2 * turn + side].wait()
            parts.append(
                jnp.dot(
                    rows_ref[:, pl.ds(where, depth)],
                    weight_buf[2 * turn + side],
                    preferred_element_type=jnp.float32,
                )
            )
        out_ref[:, pl.ds(block, width)] = (parts[0] + parts[1]).astype(jnp.bfloat16)


def branch_out(place, rows, weights):
    count = len(weights)
    depth, width = weights[0].shape
    return pl.pallas_call(
        branch_kernel,
        out_shape=jax.ShapeDtypeStruct((rows.shape[0], count // 2 * width), jnp.bfloat16),
        in_specs=[SMEM, VMEM] + [HBM] * count,
        out_specs=VMEM,
        scratch_shapes=[
            pltpu.VMEM((count, depth, width), jnp.bfloat16),
            pltpu.SemaphoreType.DMA((count,)),
        ],
        compiler_params=pltpu.CompilerParams(vmem_limit_bytes=48 * 1024 * 1024),
        name="branch",
    )(place, rows, *weights)


def hidden_kernel(steps, *refs):
    out_ref = refs[-1]
    branch_refs, strip_refs = refs[:HALVES], refs[HALVES:-1]
    _, layers, chips, rows, width = branch_refs[0].shape
    strip = strip_refs[0].shape[3]
    for half in range(HALVES):
        for layer in range(layers):
            for part in range(width // strip):
                span = slice(part * strip, (part + 1) * strip)
                total = strip_refs[half][layer, part].astype(jnp.float32)
                for chip in range(chips):
                    total = total + branch_refs[half][0, layer, chip, :, span].astype(jnp.float32)
                start = layer * width + part * strip
                for seq in range(rows // steps):
                    out_ref[half * (rows // steps) + seq, :, start : start + strip] = total[
                        seq * steps : (seq + 1) * steps
                    ].astype(jnp.bfloat16)


def hidden_sum(branches, arrived, width, steps):
    upper, layers, chips, rows, pair_width = branches[0].shape
    lower = pair_width // width
    strip = width // chips
    last = arrived[0].shape[3] // strip - 1
    seqs = HALVES * rows // steps
    return pl.pallas_call(
        functools.partial(hidden_kernel, steps),
        out_shape=jax.ShapeDtypeStruct((seqs, steps, upper * layers * pair_width), jnp.bfloat16),
        grid=(upper * lower,),
        in_specs=[
            pl.BlockSpec(
                (1, layers, chips, rows, width), lambda y: (y // lower, 0, 0, 0, y % lower)
            )
        ]
        * HALVES
        + [pl.BlockSpec((layers, chips, rows, strip), lambda y: (y, 0, 0, last))] * HALVES,
        out_specs=pl.BlockSpec((seqs, steps, layers * width), lambda y: (0, 0, y)),
        compiler_params=pltpu.CompilerParams(vmem_limit_bytes=48 * 1024 * 1024),
        name="hidden_sum",
    )(*branches, *arrived)


def per_device(
    token_ids,
    lengths,
    embedding,
    norm_gain,
    q_weight,
    k_weight,
    v_weight,
    q_bias,
    k_bias,
    v_bias,
    o_weight,
    key_cache,
    value_cache,
):
    seq_here, step_count = token_ids.shape
    rows_here = seq_here * step_count
    vocab_here, width_here = embedding.shape
    line = lax.axis_index("yl")
    replicas = lax.axis_size(DP)
    chips = lax.axis_size(CHIPS)
    chip = lax.axis_index(CHIPS)
    core = lax.axis_index("core")
    parties = replicas * chips
    plane_rows = parties * rows_here
    place = jnp.stack([chip, core, line]).astype(jnp.int32)

    both = jnp.concatenate([q_weight, k_weight, v_weight], axis=1)
    both_other = swap_cores(both)
    o_line = swap_lines(o_weight)
    o_weights = (o_weight, swap_cores(o_weight), o_line, swap_cores(o_line))
    own_bias = jnp.concatenate([q_bias, k_bias, v_bias])
    core_cols = own_bias.shape[0]
    q_cols = q_bias.shape[0]

    sent_ids = jnp.broadcast_to(token_ids.reshape(1, rows_here), (parties * 2, rows_here))
    every_id = lax.all_to_all(sent_ids, EVERY, split_axis=0, concat_axis=0, tiled=True)
    plane_ids = every_id.reshape(parties, 2, rows_here).transpose(1, 0, 2).reshape(2, plane_rows)
    own_holder = lax.dynamic_index_in_dim(plane_ids, core, 0, keepdims=False) // (2 * vocab_here)
    row_at = jnp.arange(SENT_ROWS, dtype=jnp.int32)
    bias_rows = jnp.where(
        row_at[:, None] == ROUND_ROWS + core,
        jnp.pad(own_bias, (0, width_here - core_cols))[None, :],
        jnp.zeros((), jnp.bfloat16),
    ).astype(jnp.float32)

    def exchange(turn):
        first = turn * ROUND_ROWS
        turn_place = jnp.concatenate([place, jnp.asarray(first, jnp.int32).reshape(1)])
        mine, theirs, rank = look_up(turn_place, plane_ids, bias_rows, embedding)
        merged = mine + swap_cores(theirs)
        table = lax.all_to_all(
            jnp.broadcast_to(merged[None], (chips, SENT_ROWS, width_here)),
            CHIPS,
            split_axis=0,
            concat_axis=0,
            tiled=True,
        ).reshape(chips * SENT_ROWS, width_here)
        own_rank = lax.dynamic_index_in_dim(rank, core, 0, keepdims=False).reshape(-1)
        here = (own_rank >= first) & (own_rank < first + ROUND_ROWS)
        slot = jnp.where(here, own_holder * SENT_ROWS + own_rank - first, -1)
        return slot, table, jnp.max(rank) // ROUND_ROWS + 1

    own_gain = lax.dynamic_slice_in_dim(norm_gain, lax.axis_index(DP) * width_here, width_here)
    own_gain = own_gain.reshape(1, width_here).astype(jnp.float32)
    slot, table, rounds = exchange(0)
    pair_bias = table.reshape(chips, SENT_ROWS, width_here)
    pair_bias = pair_bias[:, ROUND_ROWS : ROUND_ROWS + 2, :core_cols].astype(jnp.float32)
    pair_bias = pair_bias.reshape(chips, 1, 2 * core_cols)
    half_rows = rows_here // HALVES
    kv_heads = key_cache.shape[2] // HD
    positions = (lengths[:, None] + jnp.arange(step_count, dtype=jnp.int32)[None, :]).reshape(-1)
    frequency = rope_base ** (-(2.0 * jnp.arange(HD // 2, dtype=jnp.float32)) / HD)
    angles = positions.astype(jnp.float32)[:, None] * frequency
    cosine, sine = jnp.cos(angles), jnp.sin(angles)
    cosine = jnp.concatenate([cosine, cosine], axis=1)
    sine = jnp.concatenate([-sine, sine], axis=1)
    row_lengths = jnp.repeat(lengths, step_count)

    def part_of(values, half):
        return values.reshape(parties, HALVES, half_rows)[:, half].reshape(-1, 1)

    payloads = tuple(
        project(place, part_of(slot, half), table, own_gain, both, both_other, (o_line,), chips)
        for half in range(HALVES)
    )

    def further(turn, sofar):
        turn_slot, turn_table, _ = exchange(turn)
        return tuple(
            sofar[half]
            + project(
                place, part_of(turn_slot, half), turn_table, own_gain, both, both_other, (), chips
            )
            for half in range(HALVES)
        )

    payloads = lax.fori_loop(1, rounds, further, payloads)
    layer_count = lax.axis_size(("yh", "zl"))
    arrived, new_keys, new_values, branches = [], [], [], []
    for half in range(HALVES):
        here = lax.all_to_all(payloads[half], PLANE, split_axis=0, concat_axis=0, tiled=True)
        here = here.reshape(replicas, chips, half_rows, -1)
        rows = slice(half * half_rows, (half + 1) * half_rows)
        spread, keys, values = attend(
            half,
            here,
            pair_bias,
            cosine[rows],
            sine[rows],
            jnp.tile(row_lengths[rows], 8 * kv_heads // chips).reshape(-1, 1),
            key_cache,
            value_cache,
            layer_count,
        )
        gathered = lax.all_to_all(
            spread.reshape(-1, half_rows, 2 * q_cols), LAYER, split_axis=0, concat_axis=0, tiled=True
        ).reshape(-1, 2 * q_cols)
        branch = branch_out(place, gathered, o_weights)
        back = lax.all_to_all(branch, LAYER, split_axis=0, concat_axis=0, tiled=True)
        branches.append(back.reshape(2, layer_count // 2, chips, half_rows, -1))
        arrived.append(here)
        new_keys.append(keys)
        new_values.append(values)
    hidden = hidden_sum(branches, arrived, o_weight.shape[1], step_count)
    new_keys = jnp.concatenate(new_keys, axis=0)
    new_values = jnp.concatenate(new_values, axis=0)
    return (
        hidden,
        new_keys.reshape(seq_here, step_count, -1),
        new_values.reshape(seq_here, step_count, -1),
    )


def solution(mesh):
    fine = Mesh(mesh.devices.reshape(2, 2, 2, 2, 4, 2), EVERY)
    tensor = CHIPS + ("core",)
    placed = (
        P(EVERY, None),
        P(EVERY),
        P(tensor, DP),
        P(),
        P(DP, tensor),
        P(DP, tensor),
        P(DP, tensor),
        P(tensor),
        P(tensor),
        P(tensor),
        P(tensor, DP),
        P(EVERY, None, None),
        P(EVERY, None, None),
    )
    return jax.shard_map(
        per_device,
        mesh=fine,
        in_specs=placed,
        out_specs=(
            P(EVERY, None, None),
            P(EVERY, None, None),
            P(EVERY, None, None),
        ),
        check_vma=False,
    )
```

```python
import functools

import jax
import jax.numpy as jnp
from jax import lax
from jax.experimental import pallas as pl
from jax.experimental.pallas import tpu as pltpu
from jax.sharding import Mesh
from jax.sharding import PartitionSpec as P

HD = 128
ROUND_ROWS = 126
SENT_ROWS = 128
CHIP_COUNT = 8
HALVES = 2

norm_epsilon = 1e-06
rope_base = 1000000.0
masked_low = -1e30

DP = ("yh", "yl", "zl")
CHIPS = ("zh", "x")
LAYER = ("yh", "zl", "zh", "x")
PLANE = ("yh", "yl", "zl", "zh", "x")
EVERY = ("yh", "yl", "zl", "zh", "x", "core")


def swap_cores(value):
    return lax.ppermute(value, "core", [(0, 1), (1, 0)])


def swap_lines(value):
    return lax.ppermute(value, "yl", [(0, 1), (1, 0)])


VMEM = pl.BlockSpec(memory_space=pltpu.VMEM)
SMEM = pl.BlockSpec(memory_space=pltpu.SMEM)
HBM = pl.BlockSpec(memory_space=pltpu.HBM)


def turned(row):
    wide = jnp.broadcast_to(row.astype(jnp.float32), (8, row.shape[1]))
    return jnp.transpose(wide)[:, :1].astype(jnp.int32)


def lookup_kernel(place_ref, id_row_ref, bias_ref, vocab_ref, *rest):
    mine_ref, theirs_ref, rank_ref, list_ref, total_ref = rest
    step = pl.program_id(0)
    chip, core, first = place_ref[0], place_ref[1], place_ref[3]
    planes, _, rows = id_row_ref.shape
    span = vocab_ref.shape[0]
    vocab_here = span * pl.num_programs(0)

    @pl.when(step == 0)
    def _():
        total_ref[...] = jnp.zeros_like(total_ref)
        across = lax.broadcasted_iota(jnp.int32, (rows, rows), 1)
        down = lax.broadcasted_iota(jnp.int32, (rows, rows), 0)
        earlier = across < down
        slot = lax.broadcasted_iota(jnp.int32, (SENT_ROWS, rows), 0)
        for plane in range(planes):
            id_row = id_row_ref[plane]
            id_col = turned(id_row)
            again = jnp.where((id_row == id_col) & earlier, 1, 0)
            key_col = jnp.where(jnp.max(again, axis=1, keepdims=True) == 0, id_col, -1)
            edge_row = jnp.zeros_like(id_row)
            for other in range(1, CHIP_COUNT):
                edge = other * 2 * vocab_here
                edge_row = jnp.where(id_row >= edge, edge, edge_row)
            before = (key_col >= edge_row) & (key_col < id_row)
            rank = jnp.sum(before.astype(jnp.int32), axis=0, keepdims=True)
            rank_ref[plane] = rank
            offset = id_row - (2 * chip + core) * vocab_here
            listed = (offset >= 0) & (offset < vocab_here)
            wanted = jnp.where(listed, rank - first, -1)
            chosen = (wanted == slot) & (slot < ROUND_ROWS)
            list_ref[plane * SENT_ROWS : (plane + 1) * SENT_ROWS, :] = jnp.max(
                jnp.where(chosen, offset, -1), axis=1, keepdims=True
            )

    entry = lax.broadcasted_iota(jnp.int32, (planes * SENT_ROWS, span), 1) + step * span
    chosen = (entry == list_ref[...]).astype(jnp.bfloat16)
    total_ref[...] += jnp.dot(chosen, vocab_ref[...], preferred_element_type=jnp.float32)

    @pl.when(step == pl.num_programs(0) - 1)
    def _():
        for side, target in ((0, mine_ref), (1, theirs_ref)):
            plane = (core + side) % 2
            start = pl.multiple_of(plane * SENT_ROWS, SENT_ROWS)
            target[...] = (total_ref[pl.ds(start, SENT_ROWS), :] + bias_ref[...]).astype(
                jnp.bfloat16
            )


def look_up(place, plane_ids, bias_rows, embedding):
    planes, rows = plane_ids.shape
    vocab_here, width = embedding.shape
    steps = 3
    whole = lambda *dims: pl.BlockSpec(dims, lambda i: (0,) * len(dims))
    return pl.pallas_call(
        lookup_kernel,
        out_shape=(
            jax.ShapeDtypeStruct((SENT_ROWS, width), jnp.bfloat16),
            jax.ShapeDtypeStruct((SENT_ROWS, width), jnp.bfloat16),
            jax.ShapeDtypeStruct((planes, 1, rows), jnp.int32),
        ),
        grid=(steps,),
        in_specs=[
            SMEM,
            whole(planes, 1, rows),
            whole(SENT_ROWS, width),
            pl.BlockSpec((vocab_here // steps, width), lambda i: (i, 0)),
        ],
        out_specs=(
            whole(SENT_ROWS, width),
            whole(SENT_ROWS, width),
            whole(planes, 1, rows),
        ),
        scratch_shapes=[
            pltpu.VMEM((planes * SENT_ROWS, 1), jnp.int32),
            pltpu.VMEM((planes * SENT_ROWS, width), jnp.float32),
        ],
        compiler_params=pltpu.CompilerParams(vmem_limit_bytes=48 * 1024 * 1024),
        name="look_up",
    )(place, plane_ids.reshape(planes, 1, rows), bias_rows, embedding)


def attention_kernel(
    half,
    arrived_ref, bias_ref, cosine_ref, sine_ref, length_ref, keys_ref, values_ref, *rest
):
    out_ref, new_keys_ref, new_values_ref, key_buf, value_buf, key_sem, value_sem = rest
    groups, chips, rows, _ = arrived_ref.shape
    seqs, cache_len, _ = key_buf.shape
    steps = rows // seqs
    core_cols = bias_ref.shape[2] // 2
    heads = out_ref.shape[3] // HD
    half_heads = heads // 2
    many = heads * rows
    copies = []
    for seq in range(seqs):
        copies.append(pltpu.make_async_copy(keys_ref.at[half * seqs + seq], key_buf.at[seq], key_sem.at[seq]))
        copies.append(
            pltpu.make_async_copy(
                values_ref.at[half * seqs + seq], value_buf.at[seq], value_sem.at[seq]
            )
        )
    for copy in copies:
        copy.start()
    square = None
    for group in range(groups):
        for chip in range(chips):
            part = arrived_ref[group, chip, :, 2 * core_cols :].astype(jnp.float32)
            square = part * part if square is None else square + part * part
    width = groups * chips * square.shape[1]
    scale = lax.rsqrt(jnp.sum(square, axis=1, keepdims=True) / width + norm_epsilon)
    cosine = cosine_ref[...]
    sine = sine_ref[...]
    lane = lax.broadcasted_iota(jnp.int32, (rows, HD), 1)

    def rotated(features):
        return features * cosine + pltpu.roll(features, HD // 2, 1) * sine

    row_at = lax.broadcasted_iota(jnp.int32, (many, 1), 0) % rows
    row_seq = row_at // steps
    row_step = row_at % steps
    fresh_at = lax.broadcasted_iota(jnp.int32, (many, rows), 1)
    fresh_valid = (fresh_at // steps == row_seq) & (fresh_at % steps <= row_step)
    cache_valid = lax.broadcasted_iota(jnp.int32, (many, cache_len), 1) < length_ref[...]
    score_scale = HD ** (-0.5)
    for copy in copies:
        copy.wait()
    for chip in range(chips):
        span = slice(chip * HD, (chip + 1) * HD)
        joined = arrived_ref[0, chip, :, : 2 * core_cols].astype(jnp.float32)
        for group in range(1, groups):
            joined = joined + arrived_ref[group, chip, :, : 2 * core_cols].astype(jnp.float32)
        joined = (joined * scale + bias_ref[chip]).astype(jnp.bfloat16).astype(jnp.float32)
        parts = []
        for head in range(heads):
            start = (head // half_heads) * core_cols + (head % half_heads) * HD
            parts.append(rotated(joined[:, start : start + HD]))
        queries = jnp.concatenate(parts, axis=0).astype(jnp.bfloat16)
        low = joined[:, core_cols - HD : core_cols]
        high = joined[:, 2 * core_cols - HD :]
        fresh_keys = rotated(jnp.where(lane < HD // 2, low, pltpu.roll(high, HD // 2, 1))).astype(
            jnp.bfloat16
        )
        fresh_values = jnp.where(lane < HD // 2, pltpu.roll(low, HD // 2, 1), high).astype(
            jnp.bfloat16
        )
        new_keys_ref[:, span] = fresh_keys
        new_values_ref[:, span] = fresh_values
        scores = None
        for seq in range(seqs):
            found = lax.dot_general(
                queries,
                key_buf[seq, :, span],
                (((1,), (1,)), ((), ())),
                preferred_element_type=jnp.float32,
            )
            scores = found if scores is None else jnp.where(row_seq == seq, found, scores)
        fresh_scores = lax.dot_general(
            queries, fresh_keys, (((1,), (1,)), ((), ())), preferred_element_type=jnp.float32
        )
        scores = jnp.where(cache_valid, scores * score_scale, masked_low)
        fresh_scores = jnp.where(fresh_valid, fresh_scores * score_scale, masked_low)
        top = jnp.maximum(
            jnp.max(scores, axis=1, keepdims=True), jnp.max(fresh_scores, axis=1, keepdims=True)
        )
        scores = jnp.exp(scores - top)
        fresh_scores = jnp.exp(fresh_scores - top)
        share = 1.0 / (
            jnp.sum(scores, axis=1, keepdims=True) + jnp.sum(fresh_scores, axis=1, keepdims=True)
        )
        weights = (scores * share).astype(jnp.bfloat16)
        fresh_weights = (fresh_scores * share).astype(jnp.bfloat16)
        attended = jnp.dot(fresh_weights, fresh_values, preferred_element_type=jnp.float32)
        for seq in range(seqs):
            found = jnp.dot(
                weights, value_buf[seq, :, span], preferred_element_type=jnp.float32
            )
            attended = attended + jnp.where(row_seq == seq, found, 0.0)
        for head in range(heads):
            piece = attended[head * rows : (head + 1) * rows].astype(jnp.bfloat16)
            for group in range(out_ref.shape[0]):
                out_ref[group, chip, :, head * HD : (head + 1) * HD] = piece


def attend(half, arrived, bias, cosine, sine, row_lengths, key_cache, value_cache, copies):
    _, chips, rows, _ = arrived.shape
    seqs, cache_len, kv_cols = key_cache.shape
    seqs = seqs // HALVES
    heads = 8
    return pl.pallas_call(
        functools.partial(attention_kernel, half),
        out_shape=(
            jax.ShapeDtypeStruct((copies, chips, rows, heads * HD), jnp.bfloat16),
            jax.ShapeDtypeStruct((rows, kv_cols), jnp.bfloat16),
            jax.ShapeDtypeStruct((rows, kv_cols), jnp.bfloat16),
        ),
        in_specs=[VMEM] * 5 + [HBM] * 2,
        out_specs=(VMEM, VMEM, VMEM),
        scratch_shapes=[
            pltpu.VMEM((seqs, cache_len, kv_cols), jnp.bfloat16),
            pltpu.VMEM((seqs, cache_len, kv_cols), jnp.bfloat16),
            pltpu.SemaphoreType.DMA((seqs,)),
            pltpu.SemaphoreType.DMA((seqs,)),
        ],
        compiler_params=pltpu.CompilerParams(vmem_limit_bytes=48 * 1024 * 1024),
        name="attend",
    )(arrived, bias, cosine, sine, row_lengths, key_cache, value_cache)


def projection_kernel(place_ref, slot_ref, table_ref, gain_ref, mine_ref, theirs_ref, *rest):
    out_ref, wide_ref, weight_buf, sem = rest[-4:]
    chip, core = place_ref[0], place_ref[1]
    table_rows = table_ref.shape[0]
    cols = mine_ref.shape[1]
    step = pl.program_id(0)
    slot = turned(slot_ref[...])
    rows = slot.shape[0]
    copies = [
        pltpu.make_async_copy(source, weight_buf.at[side], sem.at[side])
        for side, source in enumerate((mine_ref, theirs_ref))
    ]

    @pl.when(step == 0)
    def _():
        for copy in copies:
            copy.start()

    chosen = (
        lax.broadcasted_iota(jnp.int32, (rows, table_rows), 1) == slot
    ).astype(jnp.bfloat16)
    found = jnp.dot(chosen, table_ref[...], preferred_element_type=jnp.float32)
    wide_ref[...] = found.astype(jnp.bfloat16)
    gained = (found * gain_ref[...]).astype(jnp.bfloat16)

    @pl.when(step == 0)
    def _():
        for copy in copies:
            copy.wait()

    for side in range(2):
        product = jnp.dot(gained, weight_buf[side], preferred_element_type=jnp.float32)
        where = pl.multiple_of(((core + side) % 2) * cols, cols)
        out_ref[:, pl.ds(where, cols)] = product.astype(jnp.bfloat16)
    strip = out_ref.shape[1] - 2 * cols
    out_ref[:, 2 * cols :] = wide_ref[:, pl.ds(pl.multiple_of(chip * strip, strip), strip)]


def project(place, slot, table, gain, mine, theirs, held, chips):
    rows = slot.shape[1]
    table_rows, width = table.shape
    cols = mine.shape[1]
    out_cols = 2 * cols + width // chips
    block = 256
    return pl.pallas_call(
        projection_kernel,
        out_shape=jax.ShapeDtypeStruct((rows, out_cols), jnp.bfloat16),
        grid=(rows // block,),
        in_specs=[
            SMEM,
            pl.BlockSpec((1, block), lambda i: (0, i)),
            pl.BlockSpec((table_rows, width), lambda i: (0, 0)),
            pl.BlockSpec((1, width), lambda i: (0, 0)),
        ]
        + [HBM] * (2 + len(held)),
        out_specs=pl.BlockSpec((block, out_cols), lambda i: (i, 0)),
        scratch_shapes=[
            pltpu.VMEM((block, width), jnp.bfloat16),
            pltpu.VMEM((2, width, cols), jnp.bfloat16),
            pltpu.SemaphoreType.DMA((2,)),
        ],
        compiler_params=pltpu.CompilerParams(vmem_limit_bytes=48 * 1024 * 1024),
        name="project",
    )(place, slot, table, gain, mine, theirs, *held)


def branch_kernel(place_ref, rows_ref, *rest):
    weight_refs, out_ref = rest[:-1], rest[-1]
    core, line = place_ref[1], place_ref[2]
    depth, width = weight_refs[0].shape
    count = len(weight_refs) // 2
    for turn in range(count):
        block = pl.multiple_of(((line + count - turn) % count) * width, width)
        parts = []
        for side in range(2):
            where = pl.multiple_of(((core + side) % 2) * depth, depth)
            parts.append(
                jnp.dot(
                    rows_ref[:, pl.ds(where, depth)],
                    weight_refs[2 * turn + side][...],
                    preferred_element_type=jnp.float32,
                )
            )
        out_ref[:, pl.ds(block, width)] = (parts[0] + parts[1]).astype(jnp.bfloat16)


def branch_out(place, rows, weights):
    count = len(weights)
    width = weights[0].shape[1]
    return pl.pallas_call(
        branch_kernel,
        out_shape=jax.ShapeDtypeStruct((rows.shape[0], count // 2 * width), jnp.bfloat16),
        in_specs=[SMEM, VMEM] + [VMEM] * count,
        out_specs=VMEM,
        compiler_params=pltpu.CompilerParams(vmem_limit_bytes=48 * 1024 * 1024),
        name="branch",
    )(place, rows, *weights)


def hidden_kernel(steps, *refs):
    out_ref = refs[-1]
    branch_refs, strip_refs = refs[:HALVES], refs[HALVES:-1]
    _, layers, chips, rows, width = branch_refs[0].shape
    strip = strip_refs[0].shape[3]
    for half in range(HALVES):
        for layer in range(layers):
            for part in range(width // strip):
                span = slice(part * strip, (part + 1) * strip)
                total = strip_refs[half][layer, part].astype(jnp.float32)
                for chip in range(chips):
                    total = total + branch_refs[half][0, layer, chip, :, span].astype(jnp.float32)
                start = layer * width + part * strip
                for seq in range(rows // steps):
                    out_ref[half * (rows // steps) + seq, :, start : start + strip] = total[
                        seq * steps : (seq + 1) * steps
                    ].astype(jnp.bfloat16)


def hidden_sum(branches, arrived, width, steps):
    upper, layers, chips, rows, pair_width = branches[0].shape
    lower = pair_width // width
    strip = width // chips
    last = arrived[0].shape[3] // strip - 1
    seqs = HALVES * rows // steps
    return pl.pallas_call(
        functools.partial(hidden_kernel, steps),
        out_shape=jax.ShapeDtypeStruct((seqs, steps, upper * layers * pair_width), jnp.bfloat16),
        grid=(upper * lower,),
        in_specs=[
            pl.BlockSpec(
                (1, layers, chips, rows, width), lambda y: (y // lower, 0, 0, 0, y % lower)
            )
        ]
        * HALVES
        + [pl.BlockSpec((layers, chips, rows, strip), lambda y: (y, 0, 0, last))] * HALVES,
        out_specs=pl.BlockSpec((seqs, steps, layers * width), lambda y: (0, 0, y)),
        compiler_params=pltpu.CompilerParams(vmem_limit_bytes=48 * 1024 * 1024),
        name="hidden_sum",
    )(*branches, *arrived)


def per_device(
    token_ids,
    lengths,
    embedding,
    norm_gain,
    q_weight,
    k_weight,
    v_weight,
    q_bias,
    k_bias,
    v_bias,
    o_weight,
    key_cache,
    value_cache,
):
    seq_here, step_count = token_ids.shape
    rows_here = seq_here * step_count
    vocab_here, width_here = embedding.shape
    line = lax.axis_index("yl")
    replicas = lax.axis_size(DP)
    chips = lax.axis_size(CHIPS)
    chip = lax.axis_index(CHIPS)
    core = lax.axis_index("core")
    parties = replicas * chips
    plane_rows = parties * rows_here
    place = jnp.stack([chip, core, line]).astype(jnp.int32)

    both = jnp.concatenate([q_weight, k_weight, v_weight], axis=1)
    both_other = swap_cores(both)
    o_line = swap_lines(o_weight)
    o_weights = (o_weight, swap_cores(o_weight), o_line, swap_cores(o_line))
    own_bias = jnp.concatenate([q_bias, k_bias, v_bias])
    core_cols = own_bias.shape[0]
    q_cols = q_bias.shape[0]

    sent_ids = jnp.broadcast_to(token_ids.reshape(1, rows_here), (parties * 2, rows_here))
    every_id = lax.all_to_all(sent_ids, EVERY, split_axis=0, concat_axis=0, tiled=True)
    plane_ids = every_id.reshape(parties, 2, rows_here).transpose(1, 0, 2).reshape(2, plane_rows)
    own_holder = lax.dynamic_index_in_dim(plane_ids, core, 0, keepdims=False) // (2 * vocab_here)
    row_at = jnp.arange(SENT_ROWS, dtype=jnp.int32)
    bias_rows = jnp.where(
        row_at[:, None] == ROUND_ROWS + core,
        jnp.pad(own_bias, (0, width_here - core_cols))[None, :],
        jnp.zeros((), jnp.bfloat16),
    ).astype(jnp.float32)

    def exchange(turn):
        first = turn * ROUND_ROWS
        turn_place = jnp.concatenate([place, jnp.asarray(first, jnp.int32).reshape(1)])
        mine, theirs, rank = look_up(turn_place, plane_ids, bias_rows, embedding)
        merged = mine + swap_cores(theirs)
        table = lax.all_to_all(
            jnp.broadcast_to(merged[None], (chips, SENT_ROWS, width_here)),
            CHIPS,
            split_axis=0,
            concat_axis=0,
            tiled=True,
        ).reshape(chips * SENT_ROWS, width_here)
        own_rank = lax.dynamic_index_in_dim(rank, core, 0, keepdims=False).reshape(-1)
        here = (own_rank >= first) & (own_rank < first + ROUND_ROWS)
        slot = jnp.where(here, own_holder * SENT_ROWS + own_rank - first, -1)
        return slot, table, jnp.max(rank) // ROUND_ROWS + 1

    own_gain = lax.dynamic_slice_in_dim(norm_gain, lax.axis_index(DP) * width_here, width_here)
    own_gain = own_gain.reshape(1, width_here).astype(jnp.float32)
    slot, table, rounds = exchange(0)
    pair_bias = table.reshape(chips, SENT_ROWS, width_here)
    pair_bias = pair_bias[:, ROUND_ROWS : ROUND_ROWS + 2, :core_cols].astype(jnp.float32)
    pair_bias = pair_bias.reshape(chips, 1, 2 * core_cols)
    half_rows = rows_here // HALVES
    kv_heads = key_cache.shape[2] // HD
    positions = (lengths[:, None] + jnp.arange(step_count, dtype=jnp.int32)[None, :]).reshape(-1)
    frequency = rope_base ** (-(2.0 * jnp.arange(HD // 2, dtype=jnp.float32)) / HD)
    angles = positions.astype(jnp.float32)[:, None] * frequency
    cosine, sine = jnp.cos(angles), jnp.sin(angles)
    cosine = jnp.concatenate([cosine, cosine], axis=1)
    sine = jnp.concatenate([-sine, sine], axis=1)
    row_lengths = jnp.repeat(lengths, step_count)

    def part_of(values, half):
        return values.reshape(parties, HALVES, half_rows)[:, half].reshape(1, -1)

    payloads = tuple(
        project(place, part_of(slot, half), table, own_gain, both, both_other, (o_line,), chips)
        for half in range(HALVES)
    )

    def further(turn, sofar):
        turn_slot, turn_table, _ = exchange(turn)
        return tuple(
            sofar[half]
            + project(
                place, part_of(turn_slot, half), turn_table, own_gain, both, both_other, (), chips
            )
            for half in range(HALVES)
        )

    payloads = lax.fori_loop(1, rounds, further, payloads)
    layer_count = lax.axis_size(("yh", "zl"))
    arrived, new_keys, new_values, branches = [], [], [], []
    for half in range(HALVES):
        here = lax.all_to_all(payloads[half], PLANE, split_axis=0, concat_axis=0, tiled=True)
        here = here.reshape(replicas, chips, half_rows, -1)
        rows = slice(half * half_rows, (half + 1) * half_rows)
        spread, keys, values = attend(
            half,
            here,
            pair_bias,
            cosine[rows],
            sine[rows],
            jnp.tile(row_lengths[rows], 8 * kv_heads // chips).reshape(-1, 1),
            key_cache,
            value_cache,
            layer_count,
        )
        gathered = lax.all_to_all(
            spread.reshape(-1, half_rows, 2 * q_cols), LAYER, split_axis=0, concat_axis=0, tiled=True
        ).reshape(-1, 2 * q_cols)
        branch = branch_out(place, gathered, o_weights)
        back = lax.all_to_all(branch, LAYER, split_axis=0, concat_axis=0, tiled=True)
        branches.append(back.reshape(2, layer_count // 2, chips, half_rows, -1))
        arrived.append(here)
        new_keys.append(keys)
        new_values.append(values)
    hidden = hidden_sum(branches, arrived, o_weight.shape[1], step_count)
    new_keys = jnp.concatenate(new_keys, axis=0)
    new_values = jnp.concatenate(new_values, axis=0)
    return (
        hidden,
        new_keys.reshape(seq_here, step_count, -1),
        new_values.reshape(seq_here, step_count, -1),
    )


def solution(mesh):
    fine = Mesh(mesh.devices.reshape(2, 2, 2, 2, 4, 2), EVERY)
    tensor = CHIPS + ("core",)
    placed = (
        P(EVERY, None),
        P(EVERY),
        P(tensor, DP),
        P(),
        P(DP, tensor),
        P(DP, tensor),
        P(DP, tensor),
        P(tensor),
        P(tensor),
        P(tensor),
        P(tensor, DP),
        P(EVERY, None, None),
        P(EVERY, None, None),
    )
    return jax.shard_map(
        per_device,
        mesh=fine,
        in_specs=placed,
        out_specs=(
            P(EVERY, None, None),
            P(EVERY, None, None),
            P(EVERY, None, None),
        ),
        check_vma=False,
    )
```

```python
import functools

import jax
import jax.numpy as jnp
from jax import lax
from jax.experimental import pallas as pl
from jax.experimental.pallas import tpu as pltpu
from jax.sharding import Mesh
from jax.sharding import PartitionSpec as P

HD = 128
ROUND_ROWS = 126
SENT_ROWS = 128
CHIP_COUNT = 8
WHOLE_VMEM = 60 * 1024 * 1024
HALVES = 1

norm_epsilon = 1e-06
rope_base = 1000000.0
masked_low = -1e30

DP = ("yh", "yl", "zl")
CHIPS = ("zh", "x")
LAYER = ("yh", "zl", "zh", "x")
PLANE = ("yh", "yl", "zl", "zh", "x")
EVERY = ("yh", "yl", "zl", "zh", "x", "core")


def swap_cores(value):
    return lax.ppermute(value, "core", [(0, 1), (1, 0)])


def swap_lines(value):
    return lax.ppermute(value, "yl", [(0, 1), (1, 0)])


VMEM = pl.BlockSpec(memory_space=pltpu.VMEM)
SMEM = pl.BlockSpec(memory_space=pltpu.SMEM)
HBM = pl.BlockSpec(memory_space=pltpu.HBM)


def turned(row):
    wide = jnp.broadcast_to(row.astype(jnp.float32), (8, row.shape[1]))
    return jnp.transpose(wide)[:, :1].astype(jnp.int32)


def lookup_kernel(place_ref, id_row_ref, q_ref, k_ref, v_ref, vocab_ref, *rest):
    mine_ref, theirs_ref, rank_ref, list_ref, total_ref = rest
    step = pl.program_id(0)
    chip, core, first = place_ref[0], place_ref[1], place_ref[3]
    planes, _, rows = id_row_ref.shape
    span = vocab_ref.shape[0]
    vocab_here = span * pl.num_programs(0)

    @pl.when(step == 0)
    def _():
        total_ref[...] = jnp.zeros_like(total_ref)
        across = lax.broadcasted_iota(jnp.int32, (rows, rows), 1)
        down = lax.broadcasted_iota(jnp.int32, (rows, rows), 0)
        earlier = across < down
        slot = lax.broadcasted_iota(jnp.int32, (SENT_ROWS, rows), 0)
        for plane in range(planes):
            id_row = id_row_ref[plane]
            id_col = turned(id_row)
            again = jnp.where((id_row == id_col) & earlier, 1, 0)
            key_col = jnp.where(jnp.max(again, axis=1, keepdims=True) == 0, id_col, -1)
            edge_row = jnp.zeros_like(id_row)
            for other in range(1, CHIP_COUNT):
                edge = other * 2 * vocab_here
                edge_row = jnp.where(id_row >= edge, edge, edge_row)
            before = (key_col >= edge_row) & (key_col < id_row)
            rank = jnp.sum(before.astype(jnp.int32), axis=0, keepdims=True)
            rank_ref[plane] = rank
            offset = id_row - (2 * chip + core) * vocab_here
            listed = (offset >= 0) & (offset < vocab_here)
            wanted = jnp.where(listed, rank - first, -1)
            chosen = (wanted == slot) & (slot < ROUND_ROWS)
            list_ref[plane * SENT_ROWS : (plane + 1) * SENT_ROWS, :] = jnp.max(
                jnp.where(chosen, offset, -1), axis=1, keepdims=True
            )

    entry = lax.broadcasted_iota(jnp.int32, (planes * SENT_ROWS, span), 1) + step * span
    chosen = (entry == list_ref[...]).astype(jnp.bfloat16)
    total_ref[...] += jnp.dot(chosen, vocab_ref[...], preferred_element_type=jnp.float32)

    @pl.when(step == pl.num_programs(0) - 1)
    def _():
        width = total_ref.shape[1]
        pieces = [piece[...].astype(jnp.float32) for piece in (q_ref, k_ref, v_ref)]
        filled = sum(piece.shape[1] for piece in pieces)
        pieces.append(jnp.zeros((1, width - filled), jnp.float32))
        bias = jnp.broadcast_to(jnp.concatenate(pieces, axis=1), (16, width))
        is_bias = (
            lax.broadcasted_iota(jnp.int32, (16, 1), 0) == ROUND_ROWS + core - (SENT_ROWS - 16)
        )
        for side, target in ((0, mine_ref), (1, theirs_ref)):
            plane = (core + side) % 2
            start = pl.multiple_of(plane * SENT_ROWS, SENT_ROWS)
            target[...] = total_ref[pl.ds(start, SENT_ROWS), :].astype(jnp.bfloat16)
            tail = total_ref[pl.ds(start + SENT_ROWS - 16, 16), :]
            tail = jnp.where(is_bias, bias, tail)
            target[SENT_ROWS - 16 :, :] = tail.astype(jnp.bfloat16)


def look_up(place, plane_ids, biases, embedding):
    planes, rows = plane_ids.shape
    vocab_here, width = embedding.shape
    steps = 3
    whole = lambda *dims: pl.BlockSpec(dims, lambda i: (0,) * len(dims))
    return pl.pallas_call(
        lookup_kernel,
        out_shape=(
            jax.ShapeDtypeStruct((SENT_ROWS, width), jnp.bfloat16),
            jax.ShapeDtypeStruct((SENT_ROWS, width), jnp.bfloat16),
            jax.ShapeDtypeStruct((planes, 1, rows), jnp.int32),
        ),
        grid=(steps,),
        in_specs=[
            SMEM,
            whole(planes, 1, rows),
            *[whole(1, bias.shape[0]) for bias in biases],
            pl.BlockSpec((vocab_here // steps, width), lambda i: (i, 0)),
        ],
        out_specs=(
            whole(SENT_ROWS, width),
            whole(SENT_ROWS, width),
            whole(planes, 1, rows),
        ),
        scratch_shapes=[
            pltpu.VMEM((planes * SENT_ROWS, 1), jnp.int32),
            pltpu.VMEM((planes * SENT_ROWS, width), jnp.float32),
        ],
        compiler_params=pltpu.CompilerParams(vmem_limit_bytes=48 * 1024 * 1024),
        name="look_up",
    )(
        place,
        plane_ids.reshape(planes, 1, rows),
        *[bias.reshape(1, -1) for bias in biases],
        embedding,
    )


def attention_kernel(
    half,
    arrived_ref, bias_ref, cosine_ref, sine_ref, length_ref, keys_ref, values_ref, *rest
):
    out_ref, new_keys_ref, new_values_ref = rest[:3]
    key_buf, value_buf, query_buf, key_sem, value_sem = rest[3:]
    groups, chips, rows, _ = arrived_ref.shape
    seqs, cache_len, _ = key_buf.shape
    steps = rows // seqs
    core_cols = bias_ref.shape[2] // 2
    heads = out_ref.shape[3] // HD
    half_heads = heads // 2
    many = heads * rows
    copies = []
    for seq in range(seqs):
        copies.append(pltpu.make_async_copy(keys_ref.at[half * seqs + seq], key_buf.at[seq], key_sem.at[seq]))
        copies.append(
            pltpu.make_async_copy(
                values_ref.at[half * seqs + seq], value_buf.at[seq], value_sem.at[seq]
            )
        )
    for copy in copies:
        copy.start()
    square = None
    for group in range(groups):
        for chip in range(chips):
            part = arrived_ref[group, chip, :, 2 * core_cols :].astype(jnp.float32)
            square = part * part if square is None else square + part * part
    width = groups * chips * square.shape[1]
    scale = lax.rsqrt(jnp.sum(square, axis=1, keepdims=True) / width + norm_epsilon)
    cosine = cosine_ref[...]
    sine = sine_ref[...]
    lane = lax.broadcasted_iota(jnp.int32, (rows, HD), 1)

    def rotated(features):
        return features * cosine + pltpu.roll(features, HD // 2, 1) * sine

    row_at = lax.broadcasted_iota(jnp.int32, (many, 1), 0) % rows
    row_seq = row_at // steps
    row_step = row_at % steps
    fresh_at = lax.broadcasted_iota(jnp.int32, (many, rows), 1)
    fresh_valid = (fresh_at // steps == row_seq) & (fresh_at % steps <= row_step)
    cache_valid = lax.broadcasted_iota(jnp.int32, (many, cache_len), 1) < length_ref[...]
    score_scale = HD ** (-0.5)
    for chip in range(chips):
        span = slice(chip * HD, (chip + 1) * HD)
        joined = arrived_ref[0, chip, :, : 2 * core_cols].astype(jnp.float32)
        for group in range(1, groups):
            joined = joined + arrived_ref[group, chip, :, : 2 * core_cols].astype(jnp.float32)
        joined = (joined * scale + bias_ref[chip]).astype(jnp.bfloat16).astype(jnp.float32)
        parts = []
        for head in range(heads):
            start = (head // half_heads) * core_cols + (head % half_heads) * HD
            parts.append(rotated(joined[:, start : start + HD]))
        query_buf[chip] = jnp.concatenate(parts, axis=0).astype(jnp.bfloat16)
        low = joined[:, core_cols - HD : core_cols]
        high = joined[:, 2 * core_cols - HD :]
        fresh_keys = rotated(jnp.where(lane < HD // 2, low, pltpu.roll(high, HD // 2, 1))).astype(
            jnp.bfloat16
        )
        fresh_values = jnp.where(lane < HD // 2, pltpu.roll(low, HD // 2, 1), high).astype(
            jnp.bfloat16
        )
        new_keys_ref[:, span] = fresh_keys
        new_values_ref[:, span] = fresh_values
    for copy in copies:
        copy.wait()
    for chip in range(chips):
        span = slice(chip * HD, (chip + 1) * HD)
        queries = query_buf[chip]
        fresh_keys = new_keys_ref[:, span]
        fresh_values = new_values_ref[:, span]
        scores = None
        for seq in range(seqs):
            found = lax.dot_general(
                queries,
                key_buf[seq, :, span],
                (((1,), (1,)), ((), ())),
                preferred_element_type=jnp.float32,
            )
            scores = found if scores is None else jnp.where(row_seq == seq, found, scores)
        fresh_scores = lax.dot_general(
            queries, fresh_keys, (((1,), (1,)), ((), ())), preferred_element_type=jnp.float32
        )
        scores = jnp.where(cache_valid, scores * score_scale, masked_low)
        fresh_scores = jnp.where(fresh_valid, fresh_scores * score_scale, masked_low)
        top = jnp.maximum(
            jnp.max(scores, axis=1, keepdims=True), jnp.max(fresh_scores, axis=1, keepdims=True)
        )
        scores = jnp.exp(scores - top)
        fresh_scores = jnp.exp(fresh_scores - top)
        share = 1.0 / (
            jnp.sum(scores, axis=1, keepdims=True) + jnp.sum(fresh_scores, axis=1, keepdims=True)
        )
        weights = (scores * share).astype(jnp.bfloat16)
        fresh_weights = (fresh_scores * share).astype(jnp.bfloat16)
        attended = jnp.dot(fresh_weights, fresh_values, preferred_element_type=jnp.float32)
        for seq in range(seqs):
            found = jnp.dot(
                weights, value_buf[seq, :, span], preferred_element_type=jnp.float32
            )
            attended = attended + jnp.where(row_seq == seq, found, 0.0)
        for head in range(heads):
            piece = attended[head * rows : (head + 1) * rows].astype(jnp.bfloat16)
            for group in range(out_ref.shape[0]):
                out_ref[group, chip, :, head * HD : (head + 1) * HD] = piece


def attend(half, arrived, bias, cosine, sine, row_lengths, key_cache, value_cache, copies):
    _, chips, rows, _ = arrived.shape
    seqs, cache_len, kv_cols = key_cache.shape
    seqs = seqs // HALVES
    heads = 8
    return pl.pallas_call(
        functools.partial(attention_kernel, half),
        out_shape=(
            jax.ShapeDtypeStruct((copies, chips, rows, heads * HD), jnp.bfloat16),
            jax.ShapeDtypeStruct((rows, kv_cols), jnp.bfloat16),
            jax.ShapeDtypeStruct((rows, kv_cols), jnp.bfloat16),
        ),
        in_specs=[VMEM] * 5 + [HBM] * 2,
        out_specs=(VMEM, VMEM, VMEM),
        scratch_shapes=[
            pltpu.VMEM((seqs, cache_len, kv_cols), jnp.bfloat16),
            pltpu.VMEM((seqs, cache_len, kv_cols), jnp.bfloat16),
            pltpu.VMEM((chips, heads * rows, HD), jnp.bfloat16),
            pltpu.SemaphoreType.DMA((seqs,)),
            pltpu.SemaphoreType.DMA((seqs,)),
        ],
        compiler_params=pltpu.CompilerParams(vmem_limit_bytes=WHOLE_VMEM),
        name="attend",
    )(arrived, bias, cosine, sine, row_lengths, key_cache, value_cache)


def projection_kernel(place_ref, slot_ref, table_ref, gain_ref, mine_ref, theirs_ref, *rest):
    out_ref, wide_ref, weight_buf, sem = rest[-4:]
    chip, core = place_ref[0], place_ref[1]
    table_rows = table_ref.shape[0]
    cols = mine_ref.shape[1]
    step = pl.program_id(0)
    slot = turned(slot_ref[...])
    rows = slot.shape[0]
    copies = []
    for side, source in enumerate((mine_ref, theirs_ref)):
        where = pl.multiple_of(((core + side) % 2) * cols, cols)
        copies.append(
            pltpu.make_async_copy(source, weight_buf.at[:, pl.ds(where, cols)], sem.at[side])
        )

    @pl.when(step == 0)
    def _():
        for copy in copies:
            copy.start()

    chosen = (
        lax.broadcasted_iota(jnp.int32, (rows, table_rows), 1) == slot
    ).astype(jnp.bfloat16)
    found = jnp.dot(chosen, table_ref[...], preferred_element_type=jnp.float32)
    wide_ref[...] = found.astype(jnp.bfloat16)
    gained = (found * gain_ref[...]).astype(jnp.bfloat16)

    @pl.when(step == 0)
    def _():
        for copy in copies:
            copy.wait()

    product = jnp.dot(gained, weight_buf[...], preferred_element_type=jnp.float32)
    out_ref[:, : 2 * cols] = product.astype(jnp.bfloat16)
    strip = out_ref.shape[1] - 2 * cols
    out_ref[:, 2 * cols :] = wide_ref[:, pl.ds(pl.multiple_of(chip * strip, strip), strip)]


def project(place, slot, table, gain, mine, theirs, held, chips):
    rows = slot.shape[1]
    table_rows, width = table.shape
    cols = mine.shape[1]
    out_cols = 2 * cols + width // chips
    block = 256
    return pl.pallas_call(
        projection_kernel,
        out_shape=jax.ShapeDtypeStruct((rows, out_cols), jnp.bfloat16),
        grid=(rows // block,),
        in_specs=[
            SMEM,
            pl.BlockSpec((1, block), lambda i: (0, i)),
            pl.BlockSpec((table_rows, width), lambda i: (0, 0)),
            pl.BlockSpec((1, width), lambda i: (0, 0)),
        ]
        + [HBM] * (2 + len(held)),
        out_specs=pl.BlockSpec((block, out_cols), lambda i: (i, 0)),
        scratch_shapes=[
            pltpu.VMEM((block, width), jnp.bfloat16),
            pltpu.VMEM((width, 2 * cols), jnp.bfloat16),
            pltpu.SemaphoreType.DMA((2,)),
        ],
        compiler_params=pltpu.CompilerParams(vmem_limit_bytes=48 * 1024 * 1024),
        name="project",
    )(place, slot, table, gain, mine, theirs, *held)


def branch_kernel(place_ref, rows_ref, *rest):
    weight_refs, out_ref = rest[:-1], rest[-1]
    core, line = place_ref[1], place_ref[2]
    depth, width = weight_refs[0].shape
    count = len(weight_refs) // 2
    for turn in range(count):
        block = pl.multiple_of(((line + count - turn) % count) * width, width)
        parts = []
        for side in range(2):
            where = pl.multiple_of(((core + side) % 2) * depth, depth)
            parts.append(
                jnp.dot(
                    rows_ref[:, pl.ds(where, depth)],
                    weight_refs[2 * turn + side][...],
                    preferred_element_type=jnp.float32,
                )
            )
        out_ref[:, pl.ds(block, width)] = (parts[0] + parts[1]).astype(jnp.bfloat16)


def branch_out(place, rows, weights):
    count = len(weights)
    width = weights[0].shape[1]
    return pl.pallas_call(
        branch_kernel,
        out_shape=jax.ShapeDtypeStruct((rows.shape[0], count // 2 * width), jnp.bfloat16),
        in_specs=[SMEM, VMEM] + [VMEM] * count,
        out_specs=VMEM,
        compiler_params=pltpu.CompilerParams(vmem_limit_bytes=WHOLE_VMEM),
        name="branch",
    )(place, rows, *weights)


def hidden_kernel(steps, *refs):
    out_ref = refs[-1]
    branch_refs, strip_refs = refs[:HALVES], refs[HALVES:-1]
    _, layers, chips, rows, width = branch_refs[0].shape
    strip = strip_refs[0].shape[3]
    for half in range(HALVES):
        for layer in range(layers):
            for part in range(width // strip):
                span = slice(part * strip, (part + 1) * strip)
                total = strip_refs[half][layer, part].astype(jnp.float32)
                for chip in range(chips):
                    total = total + branch_refs[half][0, layer, chip, :, span].astype(jnp.float32)
                start = layer * width + part * strip
                for seq in range(rows // steps):
                    out_ref[half * (rows // steps) + seq, :, start : start + strip] = total[
                        seq * steps : (seq + 1) * steps
                    ].astype(jnp.bfloat16)


def hidden_sum(branches, arrived, width, steps):
    upper, layers, chips, rows, pair_width = branches[0].shape
    lower = pair_width // width
    strip = width // chips
    last = arrived[0].shape[3] // strip - 1
    seqs = HALVES * rows // steps
    return pl.pallas_call(
        functools.partial(hidden_kernel, steps),
        out_shape=jax.ShapeDtypeStruct((seqs, steps, upper * layers * pair_width), jnp.bfloat16),
        grid=(upper * lower,),
        in_specs=[
            pl.BlockSpec(
                (1, layers, chips, rows, width), lambda y: (y // lower, 0, 0, 0, y % lower)
            )
        ]
        * HALVES
        + [pl.BlockSpec((layers, chips, rows, strip), lambda y: (y, 0, 0, last))] * HALVES,
        out_specs=pl.BlockSpec((seqs, steps, layers * width), lambda y: (0, 0, y)),
        compiler_params=pltpu.CompilerParams(vmem_limit_bytes=48 * 1024 * 1024),
        name="hidden_sum",
    )(*branches, *arrived)


def per_device(
    token_ids,
    lengths,
    embedding,
    norm_gain,
    q_weight,
    k_weight,
    v_weight,
    q_bias,
    k_bias,
    v_bias,
    o_weight,
    key_cache,
    value_cache,
):
    seq_here, step_count = token_ids.shape
    rows_here = seq_here * step_count
    vocab_here, width_here = embedding.shape
    line = lax.axis_index("yl")
    replicas = lax.axis_size(DP)
    chips = lax.axis_size(CHIPS)
    chip = lax.axis_index(CHIPS)
    core = lax.axis_index("core")
    parties = replicas * chips
    plane_rows = parties * rows_here
    place = jnp.stack([chip, core, line]).astype(jnp.int32)

    both = jnp.concatenate([q_weight, k_weight, v_weight], axis=1)
    both_other = swap_cores(both)
    o_line = swap_lines(o_weight)
    o_weights = (o_weight, swap_cores(o_weight), o_line, swap_cores(o_line))
    core_cols = q_bias.shape[0] + k_bias.shape[0] + v_bias.shape[0]
    q_cols = q_bias.shape[0]

    sent_ids = jnp.broadcast_to(token_ids.reshape(1, rows_here), (parties * 2, rows_here))
    every_id = lax.all_to_all(sent_ids, EVERY, split_axis=0, concat_axis=0, tiled=True)
    plane_ids = every_id.reshape(parties, 2, rows_here).transpose(1, 0, 2).reshape(2, plane_rows)
    own_holder = lax.dynamic_index_in_dim(plane_ids, core, 0, keepdims=False) // (2 * vocab_here)
    def exchange(turn):
        first = turn * ROUND_ROWS
        turn_place = jnp.concatenate([place, jnp.asarray(first, jnp.int32).reshape(1)])
        mine, theirs, rank = look_up(turn_place, plane_ids, (q_bias, k_bias, v_bias), embedding)
        merged = mine + swap_cores(theirs)
        table = lax.all_to_all(
            jnp.broadcast_to(merged[None], (chips, SENT_ROWS, width_here)),
            CHIPS,
            split_axis=0,
            concat_axis=0,
            tiled=True,
        ).reshape(chips * SENT_ROWS, width_here)
        own_rank = lax.dynamic_index_in_dim(rank, core, 0, keepdims=False).reshape(-1)
        here = (own_rank >= first) & (own_rank < first + ROUND_ROWS)
        slot = jnp.where(here, own_holder * SENT_ROWS + own_rank - first, -1)
        return slot, table, jnp.max(rank) // ROUND_ROWS + 1

    own_gain = lax.dynamic_slice_in_dim(norm_gain, lax.axis_index(DP) * width_here, width_here)
    own_gain = own_gain.reshape(1, width_here).astype(jnp.float32)
    slot, table, rounds = exchange(0)
    pair_bias = table.reshape(chips, SENT_ROWS, width_here)
    pair_bias = pair_bias[:, ROUND_ROWS : ROUND_ROWS + 2, :core_cols].astype(jnp.float32)
    pair_bias = pair_bias.reshape(chips, 1, 2 * core_cols)
    half_rows = rows_here // HALVES
    kv_heads = key_cache.shape[2] // HD
    positions = (lengths[:, None] + jnp.arange(step_count, dtype=jnp.int32)[None, :]).reshape(-1)
    frequency = rope_base ** (-(2.0 * jnp.arange(HD // 2, dtype=jnp.float32)) / HD)
    angles = positions.astype(jnp.float32)[:, None] * frequency
    cosine, sine = jnp.cos(angles), jnp.sin(angles)
    cosine = jnp.concatenate([cosine, cosine], axis=1)
    sine = jnp.concatenate([-sine, sine], axis=1)
    row_lengths = jnp.repeat(lengths, step_count)

    def part_of(values, half):
        return values.reshape(parties, HALVES, half_rows)[:, half].reshape(1, -1)

    payloads = tuple(
        project(place, part_of(slot, half), table, own_gain, both, both_other, (o_line,), chips)
        for half in range(HALVES)
    )

    def further(turn, sofar):
        turn_slot, turn_table, _ = exchange(turn)
        return tuple(
            sofar[half]
            + project(
                place, part_of(turn_slot, half), turn_table, own_gain, both, both_other, (), chips
            )
            for half in range(HALVES)
        )

    payloads = lax.fori_loop(1, rounds, further, payloads)
    layer_count = lax.axis_size(("yh", "zl"))
    arrived, new_keys, new_values, branches = [], [], [], []
    for half in range(HALVES):
        here = lax.all_to_all(payloads[half], PLANE, split_axis=0, concat_axis=0, tiled=True)
        here = here.reshape(replicas, chips, half_rows, -1)
        rows = slice(half * half_rows, (half + 1) * half_rows)
        spread, keys, values = attend(
            half,
            here,
            pair_bias,
            cosine[rows],
            sine[rows],
            jnp.tile(row_lengths[rows], 8 * kv_heads // chips).reshape(-1, 1),
            key_cache,
            value_cache,
            layer_count,
        )
        gathered = lax.all_to_all(
            spread.reshape(-1, half_rows, 2 * q_cols), LAYER, split_axis=0, concat_axis=0, tiled=True
        ).reshape(-1, 2 * q_cols)
        branch = branch_out(place, gathered, o_weights)
        back = lax.all_to_all(branch, LAYER, split_axis=0, concat_axis=0, tiled=True)
        branches.append(back.reshape(2, layer_count // 2, chips, half_rows, -1))
        arrived.append(here)
        new_keys.append(keys)
        new_values.append(values)
    hidden = hidden_sum(branches, arrived, o_weight.shape[1], step_count)
    new_keys = jnp.concatenate(new_keys, axis=0)
    new_values = jnp.concatenate(new_values, axis=0)
    return (
        hidden,
        new_keys.reshape(seq_here, step_count, -1),
        new_values.reshape(seq_here, step_count, -1),
    )


def solution(mesh):
    fine = Mesh(mesh.devices.reshape(2, 2, 2, 2, 4, 2), EVERY)
    tensor = CHIPS + ("core",)
    placed = (
        P(EVERY, None),
        P(EVERY),
        P(tensor, DP),
        P(),
        P(DP, tensor),
        P(DP, tensor),
        P(DP, tensor),
        P(tensor),
        P(tensor),
        P(tensor),
        P(tensor, DP),
        P(EVERY, None, None),
        P(EVERY, None, None),
    )
    return jax.shard_map(
        per_device,
        mesh=fine,
        in_specs=placed,
        out_specs=(
            P(EVERY, None, None),
            P(EVERY, None, None),
            P(EVERY, None, None),
        ),
        check_vma=False,
    )
```

```python
import functools

import jax
import jax.numpy as jnp
from jax import lax
from jax.experimental import pallas as pl
from jax.experimental.pallas import tpu as pltpu
from jax.sharding import Mesh
from jax.sharding import PartitionSpec as P

HD = 128
ROUND_ROWS = 126
SENT_ROWS = 128
CHIP_COUNT = 8
WHOLE_VMEM = 60 * 1024 * 1024
HALVES = 1

norm_epsilon = 1e-06
rope_base = 1000000.0
masked_low = -1e30

DP = ("yh", "yl", "zl")
CHIPS = ("zh", "x")
LAYER = ("yh", "zl", "zh", "x")
PLANE = ("yh", "yl", "zl", "zh", "x")
EVERY = ("yh", "yl", "zl", "zh", "x", "core")


def swap_cores(value):
    return lax.ppermute(value, "core", [(0, 1), (1, 0)])


def swap_lines(value):
    return lax.ppermute(value, "yl", [(0, 1), (1, 0)])


VMEM = pl.BlockSpec(memory_space=pltpu.VMEM)
SMEM = pl.BlockSpec(memory_space=pltpu.SMEM)
HBM = pl.BlockSpec(memory_space=pltpu.HBM)


def turned(row):
    wide = jnp.broadcast_to(row.astype(jnp.float32), (8, row.shape[1]))
    return jnp.transpose(wide)[:, :1].astype(jnp.int32)


def lookup_kernel(place_ref, id_row_ref, q_ref, k_ref, v_ref, vocab_ref, *rest):
    mine_ref, theirs_ref, rank_ref, list_ref, total_ref = rest
    step = pl.program_id(0)
    chip, core, first = place_ref[0], place_ref[1], place_ref[3]
    planes, _, rows = id_row_ref.shape
    span = vocab_ref.shape[0]
    vocab_here = span * pl.num_programs(0)

    @pl.when(step == 0)
    def _():
        total_ref[...] = jnp.zeros_like(total_ref)
        across = lax.broadcasted_iota(jnp.int32, (rows, rows), 1)
        down = lax.broadcasted_iota(jnp.int32, (rows, rows), 0)
        earlier = across < down
        slot = lax.broadcasted_iota(jnp.int32, (SENT_ROWS, rows), 0)
        for plane in range(planes):
            id_row = id_row_ref[plane]
            id_col = turned(id_row)
            again = jnp.where((id_row == id_col) & earlier, 1, 0)
            key_col = jnp.where(jnp.max(again, axis=1, keepdims=True) == 0, id_col, -1)
            edge_row = jnp.zeros_like(id_row)
            for other in range(1, CHIP_COUNT):
                edge = other * 2 * vocab_here
                edge_row = jnp.where(id_row >= edge, edge, edge_row)
            before = (key_col >= edge_row) & (key_col < id_row)
            rank = jnp.sum(before.astype(jnp.int32), axis=0, keepdims=True)
            rank_ref[plane] = rank
            offset = id_row - (2 * chip + core) * vocab_here
            listed = (offset >= 0) & (offset < vocab_here)
            wanted = jnp.where(listed, rank - first, -1)
            chosen = (wanted == slot) & (slot < ROUND_ROWS)
            list_ref[plane * SENT_ROWS : (plane + 1) * SENT_ROWS, :] = jnp.max(
                jnp.where(chosen, offset, -1), axis=1, keepdims=True
            )

    entry = lax.broadcasted_iota(jnp.int32, (planes * SENT_ROWS, span), 1) + step * span
    chosen = (entry == list_ref[...]).astype(jnp.bfloat16)
    total_ref[...] += jnp.dot(chosen, vocab_ref[...], preferred_element_type=jnp.float32)

    @pl.when(step == pl.num_programs(0) - 1)
    def _():
        width = total_ref.shape[1]
        pieces = [piece[...].astype(jnp.float32) for piece in (q_ref, k_ref, v_ref)]
        filled = sum(piece.shape[1] for piece in pieces)
        pieces.append(jnp.zeros((1, width - filled), jnp.float32))
        bias = jnp.broadcast_to(jnp.concatenate(pieces, axis=1), (16, width))
        is_bias = (
            lax.broadcasted_iota(jnp.int32, (16, 1), 0) == ROUND_ROWS + core - (SENT_ROWS - 16)
        )
        for side, target in ((0, mine_ref), (1, theirs_ref)):
            plane = (core + side) % 2
            start = pl.multiple_of(plane * SENT_ROWS, SENT_ROWS)
            target[...] = total_ref[pl.ds(start, SENT_ROWS), :].astype(jnp.bfloat16)
            tail = total_ref[pl.ds(start + SENT_ROWS - 16, 16), :]
            tail = jnp.where(is_bias, bias, tail)
            target[SENT_ROWS - 16 :, :] = tail.astype(jnp.bfloat16)


def look_up(place, plane_ids, biases, embedding):
    planes, rows = plane_ids.shape
    vocab_here, width = embedding.shape
    steps = 3
    whole = lambda *dims: pl.BlockSpec(dims, lambda i: (0,) * len(dims))
    return pl.pallas_call(
        lookup_kernel,
        out_shape=(
            jax.ShapeDtypeStruct((SENT_ROWS, width), jnp.bfloat16),
            jax.ShapeDtypeStruct((SENT_ROWS, width), jnp.bfloat16),
            jax.ShapeDtypeStruct((planes, 1, rows), jnp.int32),
        ),
        grid=(steps,),
        in_specs=[
            SMEM,
            whole(planes, 1, rows),
            *[whole(1, bias.shape[0]) for bias in biases],
            pl.BlockSpec((vocab_here // steps, width), lambda i: (i, 0)),
        ],
        out_specs=(
            whole(SENT_ROWS, width),
            whole(SENT_ROWS, width),
            whole(planes, 1, rows),
        ),
        scratch_shapes=[
            pltpu.VMEM((planes * SENT_ROWS, 1), jnp.int32),
            pltpu.VMEM((planes * SENT_ROWS, width), jnp.float32),
        ],
        compiler_params=pltpu.CompilerParams(vmem_limit_bytes=48 * 1024 * 1024),
        name="look_up",
    )(
        place,
        plane_ids.reshape(planes, 1, rows),
        *[bias.reshape(1, -1) for bias in biases],
        embedding,
    )


def attention_kernel(
    half,
    arrived_ref, bias_ref, cosine_ref, sine_ref, length_ref, keys_ref, values_ref, *rest
):
    out_ref, new_keys_ref, new_values_ref = rest[:3]
    key_buf, value_buf, query_buf, key_sem, value_sem = rest[3:]
    groups, chips, rows, _ = arrived_ref.shape
    seqs, cache_len, _ = key_buf.shape
    steps = rows // seqs
    core_cols = bias_ref.shape[2] // 2
    heads = out_ref.shape[3] // HD
    many = heads * rows
    copies = []
    for seq in range(seqs):
        copies.append(pltpu.make_async_copy(keys_ref.at[half * seqs + seq], key_buf.at[seq], key_sem.at[seq]))
        copies.append(
            pltpu.make_async_copy(
                values_ref.at[half * seqs + seq], value_buf.at[seq], value_sem.at[seq]
            )
        )
    for copy in copies:
        copy.start()
    square = None
    for group in range(groups):
        for chip in range(chips):
            part = arrived_ref[group, chip, :, 2 * core_cols :].astype(jnp.float32)
            square = part * part if square is None else square + part * part
    width = groups * chips * square.shape[1]
    scale = lax.rsqrt(jnp.sum(square, axis=1, keepdims=True) / width + norm_epsilon)
    cosine = cosine_ref[...]
    sine = sine_ref[...]
    lane = lax.broadcasted_iota(jnp.int32, (rows, HD), 1)

    def rotated(features):
        return features * cosine + pltpu.roll(features, HD // 2, 1) * sine

    row_at = lax.broadcasted_iota(jnp.int32, (many, 1), 0) % rows
    row_seq = row_at // steps
    row_step = row_at % steps
    fresh_at = lax.broadcasted_iota(jnp.int32, (many, rows), 1)
    fresh_valid = (fresh_at // steps == row_seq) & (fresh_at % steps <= row_step)
    cache_valid = lax.broadcasted_iota(jnp.int32, (many, cache_len), 1) < length_ref[...]
    score_scale = HD ** (-0.5)
    for chip in range(chips):
        span = slice(chip * HD, (chip + 1) * HD)
        joined = arrived_ref[0, chip, :, : 2 * core_cols].astype(jnp.float32)
        for group in range(1, groups):
            joined = joined + arrived_ref[group, chip, :, : 2 * core_cols].astype(jnp.float32)
        joined = (joined * scale + bias_ref[chip]).astype(jnp.bfloat16).astype(jnp.float32)
        parts = []
        for head in range(heads):
            parts.append(rotated(joined[:, head * HD : (head + 1) * HD]))
        query_buf[chip] = jnp.concatenate(parts, axis=0).astype(jnp.bfloat16)
        low = joined[:, heads * HD : (heads + 1) * HD]
        high = joined[:, (heads + 1) * HD :]
        fresh_keys = rotated(jnp.where(lane < HD // 2, low, pltpu.roll(high, HD // 2, 1))).astype(
            jnp.bfloat16
        )
        fresh_values = jnp.where(lane < HD // 2, pltpu.roll(low, HD // 2, 1), high).astype(
            jnp.bfloat16
        )
        new_keys_ref[:, span] = fresh_keys
        new_values_ref[:, span] = fresh_values
    for copy in copies:
        copy.wait()
    for chip in range(chips):
        span = slice(chip * HD, (chip + 1) * HD)
        queries = query_buf[chip]
        fresh_keys = new_keys_ref[:, span]
        fresh_values = new_values_ref[:, span]
        scores = None
        for seq in range(seqs):
            found = lax.dot_general(
                queries,
                key_buf[seq, :, span],
                (((1,), (1,)), ((), ())),
                preferred_element_type=jnp.float32,
            )
            scores = found if scores is None else jnp.where(row_seq == seq, found, scores)
        fresh_scores = lax.dot_general(
            queries, fresh_keys, (((1,), (1,)), ((), ())), preferred_element_type=jnp.float32
        )
        scores = jnp.where(cache_valid, scores * score_scale, masked_low)
        fresh_scores = jnp.where(fresh_valid, fresh_scores * score_scale, masked_low)
        top = jnp.maximum(
            jnp.max(scores, axis=1, keepdims=True), jnp.max(fresh_scores, axis=1, keepdims=True)
        )
        scores = jnp.exp(scores - top)
        fresh_scores = jnp.exp(fresh_scores - top)
        share = 1.0 / (
            jnp.sum(scores, axis=1, keepdims=True) + jnp.sum(fresh_scores, axis=1, keepdims=True)
        )
        weights = (scores * share).astype(jnp.bfloat16)
        fresh_weights = (fresh_scores * share).astype(jnp.bfloat16)
        attended = jnp.dot(fresh_weights, fresh_values, preferred_element_type=jnp.float32)
        for seq in range(seqs):
            found = jnp.dot(
                weights, value_buf[seq, :, span], preferred_element_type=jnp.float32
            )
            attended = attended + jnp.where(row_seq == seq, found, 0.0)
        for head in range(heads):
            piece = attended[head * rows : (head + 1) * rows].astype(jnp.bfloat16)
            for group in range(out_ref.shape[0]):
                out_ref[group, chip, :, head * HD : (head + 1) * HD] = piece


def attend(half, arrived, bias, cosine, sine, row_lengths, key_cache, value_cache, copies):
    _, chips, rows, _ = arrived.shape
    seqs, cache_len, kv_cols = key_cache.shape
    seqs = seqs // HALVES
    heads = 8
    return pl.pallas_call(
        functools.partial(attention_kernel, half),
        out_shape=(
            jax.ShapeDtypeStruct((copies, chips, rows, heads * HD), jnp.bfloat16),
            jax.ShapeDtypeStruct((rows, kv_cols), jnp.bfloat16),
            jax.ShapeDtypeStruct((rows, kv_cols), jnp.bfloat16),
        ),
        in_specs=[VMEM] * 5 + [HBM] * 2,
        out_specs=(VMEM, VMEM, VMEM),
        scratch_shapes=[
            pltpu.VMEM((seqs, cache_len, kv_cols), jnp.bfloat16),
            pltpu.VMEM((seqs, cache_len, kv_cols), jnp.bfloat16),
            pltpu.VMEM((chips, heads * rows, HD), jnp.bfloat16),
            pltpu.SemaphoreType.DMA((seqs,)),
            pltpu.SemaphoreType.DMA((seqs,)),
        ],
        compiler_params=pltpu.CompilerParams(vmem_limit_bytes=48 * 1024 * 1024),
        name="attend",
    )(arrived, bias, cosine, sine, row_lengths, key_cache, value_cache)


def projection_kernel(place_ref, slot_ref, table_ref, gain_ref, *rest):
    out_ref, wide_ref, weight_buf, kv_buf, sem = rest[-5:]
    chip, core = place_ref[0], place_ref[1]
    table_rows = table_ref.shape[0]
    q_cols, kv_cols = rest[0].shape[1], rest[2].shape[0]
    cols = q_cols + 2 * kv_cols
    step = pl.program_id(0)
    slot = turned(slot_ref[...])
    rows = slot.shape[0]
    copies = []
    for side in range(2):
        owner = (core + side) % 2
        spots = [weight_buf.at[:, pl.ds(pl.multiple_of(owner * q_cols, q_cols), q_cols)]]
        for part in range(2):
            first = pl.multiple_of((2 * owner + part) * kv_cols, kv_cols)
            spots.append(kv_buf.at[pl.ds(first, kv_cols), :])
        for part, spot in enumerate(spots):
            number = 2 * part + side
            copies.append(pltpu.make_async_copy(rest[number], spot, sem.at[number]))

    @pl.when(step == 0)
    def _():
        for copy in copies:
            copy.start()

    chosen = (
        lax.broadcasted_iota(jnp.int32, (rows, table_rows), 1) == slot
    ).astype(jnp.bfloat16)
    found = jnp.dot(chosen, table_ref[...], preferred_element_type=jnp.float32)
    wide_ref[...] = found.astype(jnp.bfloat16)
    gained = (found * gain_ref[...]).astype(jnp.bfloat16)

    @pl.when(step == 0)
    def _():
        for copy in copies:
            copy.wait()

    product = jnp.dot(gained, weight_buf[...], preferred_element_type=jnp.float32)
    out_ref[:, : 2 * q_cols] = product.astype(jnp.bfloat16)
    product = lax.dot_general(
        gained, kv_buf[...], (((1,), (1,)), ((), ())), preferred_element_type=jnp.float32
    )
    out_ref[:, 2 * q_cols : 2 * cols] = product.astype(jnp.bfloat16)
    strip = out_ref.shape[1] - 2 * cols
    out_ref[:, 2 * cols :] = wide_ref[:, pl.ds(pl.multiple_of(chip * strip, strip), strip)]


def project(place, slot, table, gain, weights, held, chips):
    rows = slot.shape[1]
    table_rows, width = table.shape
    q_cols, kv_cols = weights[0].shape[1], weights[2].shape[0]
    cols = q_cols + 2 * kv_cols
    out_cols = 2 * cols + width // chips
    block = 256
    return pl.pallas_call(
        projection_kernel,
        out_shape=jax.ShapeDtypeStruct((rows, out_cols), jnp.bfloat16),
        grid=(rows // block,),
        in_specs=[
            SMEM,
            pl.BlockSpec((1, block), lambda i: (0, i)),
            pl.BlockSpec((table_rows, width), lambda i: (0, 0)),
            pl.BlockSpec((1, width), lambda i: (0, 0)),
        ]
        + [HBM] * (len(weights) + len(held)),
        out_specs=pl.BlockSpec((block, out_cols), lambda i: (i, 0)),
        scratch_shapes=[
            pltpu.VMEM((block, width), jnp.bfloat16),
            pltpu.VMEM((width, 2 * q_cols), jnp.bfloat16),
            pltpu.VMEM((4 * kv_cols, width), jnp.bfloat16),
            pltpu.SemaphoreType.DMA((len(weights),)),
        ],
        compiler_params=pltpu.CompilerParams(vmem_limit_bytes=48 * 1024 * 1024),
        name="project",
    )(place, slot, table, gain, *weights, *held)


def branch_kernel(place_ref, rows_ref, *rest):
    weight_refs, out_ref = rest[:-1], rest[-1]
    core, line = place_ref[1], place_ref[2]
    depth, width = weight_refs[0].shape
    count = len(weight_refs) // 2
    for turn in range(count):
        block = pl.multiple_of(((line + count - turn) % count) * width, width)
        parts = []
        for side in range(2):
            where = pl.multiple_of(((core + side) % 2) * depth, depth)
            parts.append(
                jnp.dot(
                    rows_ref[:, pl.ds(where, depth)],
                    weight_refs[2 * turn + side][...],
                    preferred_element_type=jnp.float32,
                )
            )
        out_ref[:, pl.ds(block, width)] = (parts[0] + parts[1]).astype(jnp.bfloat16)


def branch_out(place, rows, weights):
    count = len(weights)
    width = weights[0].shape[1]
    return pl.pallas_call(
        branch_kernel,
        out_shape=jax.ShapeDtypeStruct((rows.shape[0], count // 2 * width), jnp.bfloat16),
        in_specs=[SMEM, VMEM] + [VMEM] * count,
        out_specs=VMEM,
        compiler_params=pltpu.CompilerParams(vmem_limit_bytes=WHOLE_VMEM),
        name="branch",
    )(place, rows, *weights)


def hidden_kernel(steps, branch_ref, strip_ref, out_ref):
    upper, layers, chips, rows, pair_width = branch_ref.shape
    groups = strip_ref.shape[0]
    strip = out_ref.shape[2] // (groups * chips)
    width = strip * chips
    lower = pair_width // width
    for group in range(groups):
        high, low, layer = group // (lower * layers), group // layers % lower, group % layers
        for part in range(chips):
            start = low * width + part * strip
            total = strip_ref[group, part, :, strip_ref.shape[3] - strip :].astype(jnp.float32)
            for chip in range(chips):
                total = total + branch_ref[high, layer, chip, :, start : start + strip].astype(
                    jnp.float32
                )
            start = group * width + part * strip
            for seq in range(rows // steps):
                out_ref[seq, :, start : start + strip] = total[
                    seq * steps : (seq + 1) * steps
                ].astype(jnp.bfloat16)


def hidden_sum(branches, arrived, steps):
    upper, layers, _, rows, pair_width = branches.shape
    return pl.pallas_call(
        functools.partial(hidden_kernel, steps),
        out_shape=jax.ShapeDtypeStruct(
            (rows // steps, steps, upper * layers * pair_width), jnp.bfloat16
        ),
        in_specs=[VMEM] * 2,
        out_specs=VMEM,
        compiler_params=pltpu.CompilerParams(vmem_limit_bytes=48 * 1024 * 1024),
        name="hidden_sum",
    )(branches, arrived)


def per_device(
    token_ids,
    lengths,
    embedding,
    norm_gain,
    q_weight,
    k_weight,
    v_weight,
    q_bias,
    k_bias,
    v_bias,
    o_weight,
    key_cache,
    value_cache,
):
    seq_here, step_count = token_ids.shape
    rows_here = seq_here * step_count
    vocab_here, width_here = embedding.shape
    line = lax.axis_index("yl")
    replicas = lax.axis_size(DP)
    chips = lax.axis_size(CHIPS)
    chip = lax.axis_index(CHIPS)
    core = lax.axis_index("core")
    parties = replicas * chips
    plane_rows = parties * rows_here
    place = jnp.stack([chip, core, line]).astype(jnp.int32)

    weights = []
    for own in (q_weight, k_weight.T, v_weight.T):
        weights += [own, swap_cores(own)]
    o_line = swap_lines(o_weight)
    o_weights = (o_weight, swap_cores(o_weight), o_line, swap_cores(o_line))
    core_cols = q_bias.shape[0] + k_bias.shape[0] + v_bias.shape[0]
    q_cols = q_bias.shape[0]

    sent_ids = jnp.broadcast_to(token_ids.reshape(1, rows_here), (parties * 2, rows_here))
    every_id = lax.all_to_all(sent_ids, EVERY, split_axis=0, concat_axis=0, tiled=True)
    plane_ids = every_id.reshape(parties, 2, rows_here).transpose(1, 0, 2).reshape(2, plane_rows)
    own_holder = lax.dynamic_index_in_dim(plane_ids, core, 0, keepdims=False) // (2 * vocab_here)
    def exchange(turn):
        first = turn * ROUND_ROWS
        turn_place = jnp.concatenate([place, jnp.asarray(first, jnp.int32).reshape(1)])
        mine, theirs, rank = look_up(turn_place, plane_ids, (q_bias, k_bias, v_bias), embedding)
        merged = mine + swap_cores(theirs)
        table = lax.all_to_all(
            jnp.broadcast_to(merged[None], (chips, SENT_ROWS, width_here)),
            CHIPS,
            split_axis=0,
            concat_axis=0,
            tiled=True,
        ).reshape(chips * SENT_ROWS, width_here)
        own_rank = lax.dynamic_index_in_dim(rank, core, 0, keepdims=False).reshape(-1)
        here = (own_rank >= first) & (own_rank < first + ROUND_ROWS)
        slot = jnp.where(here, own_holder * SENT_ROWS + own_rank - first, -1)
        return slot, table, jnp.max(rank) // ROUND_ROWS + 1

    own_gain = lax.dynamic_slice_in_dim(norm_gain, lax.axis_index(DP) * width_here, width_here)
    own_gain = own_gain.reshape(1, width_here).astype(jnp.float32)
    slot, table, rounds = exchange(0)
    pair_bias = table.reshape(chips, SENT_ROWS, width_here)
    pair_bias = pair_bias[:, ROUND_ROWS : ROUND_ROWS + 2, :core_cols].astype(jnp.float32)
    pair_bias = jnp.concatenate(
        [
            pair_bias[:, :, :q_cols].reshape(chips, 1, -1),
            pair_bias[:, :, q_cols:].reshape(chips, 1, -1),
        ],
        axis=2,
    )
    half_rows = rows_here // HALVES
    kv_heads = key_cache.shape[2] // HD
    positions = (lengths[:, None] + jnp.arange(step_count, dtype=jnp.int32)[None, :]).reshape(-1)
    frequency = rope_base ** (-(2.0 * jnp.arange(HD // 2, dtype=jnp.float32)) / HD)
    angles = positions.astype(jnp.float32)[:, None] * frequency
    cosine, sine = jnp.cos(angles), jnp.sin(angles)
    cosine = jnp.concatenate([cosine, cosine], axis=1)
    sine = jnp.concatenate([-sine, sine], axis=1)
    row_lengths = jnp.repeat(lengths, step_count)

    def part_of(values, half):
        return values.reshape(parties, HALVES, half_rows)[:, half].reshape(1, -1)

    payloads = tuple(
        project(place, part_of(slot, half), table, own_gain, weights, (o_line,), chips)
        for half in range(HALVES)
    )

    def further(turn, sofar):
        turn_slot, turn_table, _ = exchange(turn)
        return tuple(
            sofar[half]
            + project(
                place, part_of(turn_slot, half), turn_table, own_gain, weights, (), chips
            )
            for half in range(HALVES)
        )

    payloads = lax.fori_loop(1, rounds, further, payloads)
    layer_count = lax.axis_size(("yh", "zl"))
    arrived, new_keys, new_values, branches = [], [], [], []
    for half in range(HALVES):
        here = lax.all_to_all(payloads[half], PLANE, split_axis=0, concat_axis=0, tiled=True)
        here = here.reshape(replicas, chips, half_rows, -1)
        rows = slice(half * half_rows, (half + 1) * half_rows)
        spread, keys, values = attend(
            half,
            here,
            pair_bias,
            cosine[rows],
            sine[rows],
            jnp.tile(row_lengths[rows], 8 * kv_heads // chips).reshape(-1, 1),
            key_cache,
            value_cache,
            layer_count,
        )
        gathered = lax.all_to_all(
            spread.reshape(-1, half_rows, 2 * q_cols), LAYER, split_axis=0, concat_axis=0, tiled=True
        ).reshape(-1, 2 * q_cols)
        branch = branch_out(place, gathered, o_weights)
        back = lax.all_to_all(branch, LAYER, split_axis=0, concat_axis=0, tiled=True)
        branches.append(back.reshape(2, layer_count // 2, chips, half_rows, -1))
        arrived.append(here)
        new_keys.append(keys)
        new_values.append(values)
    hidden = hidden_sum(branches[0], arrived[0], step_count)
    new_keys = jnp.concatenate(new_keys, axis=0)
    new_values = jnp.concatenate(new_values, axis=0)
    return (
        hidden,
        new_keys.reshape(seq_here, step_count, -1),
        new_values.reshape(seq_here, step_count, -1),
    )


def solution(mesh):
    fine = Mesh(mesh.devices.reshape(2, 2, 2, 2, 4, 2), EVERY)
    tensor = CHIPS + ("core",)
    placed = (
        P(EVERY, None),
        P(EVERY),
        P(tensor, DP),
        P(),
        P(DP, tensor),
        P(DP, tensor),
        P(DP, tensor),
        P(tensor),
        P(tensor),
        P(tensor),
        P(tensor, DP),
        P(EVERY, None, None),
        P(EVERY, None, None),
    )
    return jax.shard_map(
        per_device,
        mesh=fine,
        in_specs=placed,
        out_specs=(
            P(EVERY, None, None),
            P(EVERY, None, None),
            P(EVERY, None, None),
        ),
        check_vma=False,
    )
```

```python
import functools

import jax
import jax.numpy as jnp
from jax import lax
from jax.experimental import pallas as pl
from jax.experimental.pallas import tpu as pltpu
from jax.sharding import Mesh
from jax.sharding import PartitionSpec as P

HD = 128
ROUND_ROWS = 118
SENT_ROWS = 120
CHIP_COUNT = 8
WHOLE_VMEM = 60 * 1024 * 1024
HALVES = 1

norm_epsilon = 1e-06
rope_base = 1000000.0
masked_low = -1e30

DP = ("yh", "yl", "zl")
CHIPS = ("zh", "x")
LAYER = ("yh", "zl", "zh", "x")
PLANE = ("yh", "yl", "zl", "zh", "x")
EVERY = ("yh", "yl", "zl", "zh", "x", "core")


def swap_cores(value):
    return lax.ppermute(value, "core", [(0, 1), (1, 0)])


def swap_lines(value):
    return lax.ppermute(value, "yl", [(0, 1), (1, 0)])


VMEM = pl.BlockSpec(memory_space=pltpu.VMEM)
SMEM = pl.BlockSpec(memory_space=pltpu.SMEM)
HBM = pl.BlockSpec(memory_space=pltpu.HBM)


def turned(row):
    wide = jnp.broadcast_to(row.astype(jnp.float32), (8, row.shape[1]))
    return jnp.transpose(wide)[:, :1].astype(jnp.int32)


def lookup_kernel(place_ref, id_row_ref, q_ref, k_ref, v_ref, vocab_ref, *rest):
    mine_ref, theirs_ref, rank_ref, list_ref, total_ref = rest
    step = pl.program_id(0)
    chip, core, first = place_ref[0], place_ref[1], place_ref[3]
    planes, _, rows = id_row_ref.shape
    span = vocab_ref.shape[0]
    vocab_here = span * pl.num_programs(0)

    @pl.when(step == 0)
    def _():
        total_ref[...] = jnp.zeros_like(total_ref)
        across = lax.broadcasted_iota(jnp.int32, (rows, rows), 1)
        down = lax.broadcasted_iota(jnp.int32, (rows, rows), 0)
        earlier = across < down
        slot = lax.broadcasted_iota(jnp.int32, (SENT_ROWS, rows), 0)
        for plane in range(planes):
            id_row = id_row_ref[plane]
            id_col = turned(id_row)
            keys = []
            for low in range(0, rows, rows // 4):
                high = low + rows // 4
                own_col = id_col[low:high]
                again = (id_row[:, :high] == own_col) & earlier[low:high, :high]
                found = jnp.max(jnp.where(again, 1, 0), axis=1, keepdims=True)
                keys.append(jnp.where(found == 0, own_col, -1))
            key_col = jnp.concatenate(keys, axis=0)
            edge_row = jnp.zeros_like(id_row)
            for other in range(1, CHIP_COUNT):
                edge = other * 2 * vocab_here
                edge_row = jnp.where(id_row >= edge, edge, edge_row)
            before = (key_col >= edge_row) & (key_col < id_row)
            rank = jnp.sum(before.astype(jnp.int32), axis=0, keepdims=True)
            rank_ref[plane] = rank
            offset = id_row - (2 * chip + core) * vocab_here
            listed = (offset >= 0) & (offset < vocab_here)
            wanted = jnp.where(listed, rank - first, -1)
            chosen = (wanted == slot) & (slot < ROUND_ROWS)
            list_ref[plane * SENT_ROWS : (plane + 1) * SENT_ROWS, :] = jnp.max(
                jnp.where(chosen, offset, -1), axis=1, keepdims=True
            )

    entry = lax.broadcasted_iota(jnp.int32, (planes * SENT_ROWS, span), 1) + step * span
    chosen = (entry == list_ref[...]).astype(jnp.bfloat16)
    total_ref[...] += jnp.dot(chosen, vocab_ref[...], preferred_element_type=jnp.float32)

    @pl.when(step == pl.num_programs(0) - 1)
    def _():
        width = total_ref.shape[1]
        pieces = [piece[...].astype(jnp.float32) for piece in (q_ref, k_ref, v_ref)]
        filled = sum(piece.shape[1] for piece in pieces)
        pieces.append(jnp.zeros((1, width - filled), jnp.float32))
        bias = jnp.broadcast_to(jnp.concatenate(pieces, axis=1), (8, width))
        is_bias = (
            lax.broadcasted_iota(jnp.int32, (8, 1), 0) == ROUND_ROWS + core - (SENT_ROWS - 8)
        )
        for side, target in ((0, mine_ref), (1, theirs_ref)):
            plane = (core + side) % 2
            start = pl.multiple_of(plane * SENT_ROWS, SENT_ROWS)
            tail = pl.ds(start + SENT_ROWS - 8, 8)
            total_ref[tail, :] = jnp.where(is_bias, bias, total_ref[tail, :])
            target[...] = total_ref[pl.ds(start, SENT_ROWS), :].astype(jnp.bfloat16)


def look_up(place, plane_ids, biases, embedding):
    planes, rows = plane_ids.shape
    vocab_here, width = embedding.shape
    steps = 3
    whole = lambda *dims: pl.BlockSpec(dims, lambda i: (0,) * len(dims))
    return pl.pallas_call(
        lookup_kernel,
        out_shape=(
            jax.ShapeDtypeStruct((SENT_ROWS, width), jnp.bfloat16),
            jax.ShapeDtypeStruct((SENT_ROWS, width), jnp.bfloat16),
            jax.ShapeDtypeStruct((planes, 1, rows), jnp.int32),
        ),
        grid=(steps,),
        in_specs=[
            SMEM,
            whole(planes, 1, rows),
            *[whole(1, bias.shape[0]) for bias in biases],
            pl.BlockSpec((vocab_here // steps, width), lambda i: (i, 0)),
        ],
        out_specs=(
            whole(SENT_ROWS, width),
            whole(SENT_ROWS, width),
            whole(planes, 1, rows),
        ),
        scratch_shapes=[
            pltpu.VMEM((planes * SENT_ROWS, 1), jnp.int32),
            pltpu.VMEM((planes * SENT_ROWS, width), jnp.float32),
        ],
        compiler_params=pltpu.CompilerParams(vmem_limit_bytes=48 * 1024 * 1024),
        name="look_up",
    )(
        place,
        plane_ids.reshape(planes, 1, rows),
        *[bias.reshape(1, -1) for bias in biases],
        embedding,
    )


def attention_kernel(
    half,
    arrived_ref, bias_ref, cosine_ref, sine_ref, length_ref, keys_ref, values_ref, *rest
):
    out_ref, new_keys_ref, new_values_ref = rest[:3]
    key_buf, value_buf, query_buf, key_sem, value_sem = rest[3:]
    groups, chips, rows, _ = arrived_ref.shape
    seqs, cache_len, _ = key_buf.shape
    steps = rows // seqs
    core_cols = bias_ref.shape[2] // 2
    heads = out_ref.shape[3] // HD
    many = heads * rows
    key_copies, value_copies = [], []
    for seq in range(seqs):
        source = half * seqs + seq
        key_copies.append(
            pltpu.make_async_copy(keys_ref.at[source], key_buf.at[seq], key_sem.at[seq])
        )
        value_copies.append(
            pltpu.make_async_copy(values_ref.at[source], value_buf.at[seq], value_sem.at[seq])
        )
    for copy in key_copies + value_copies:
        copy.start()
    square = None
    for group in range(groups):
        for chip in range(chips):
            part = arrived_ref[group, chip, :, 2 * core_cols :].astype(jnp.float32)
            square = part * part if square is None else square + part * part
    width = groups * chips * square.shape[1]
    scale = lax.rsqrt(jnp.sum(square, axis=1, keepdims=True) / width + norm_epsilon)
    cosine = cosine_ref[...]
    sine = sine_ref[...]
    lane = lax.broadcasted_iota(jnp.int32, (rows, HD), 1)

    def rotated(features):
        return features * cosine + pltpu.roll(features, HD // 2, 1) * sine

    row_at = lax.broadcasted_iota(jnp.int32, (many, 1), 0) % rows
    row_seq = row_at // steps
    row_step = row_at % steps
    fresh_at = lax.broadcasted_iota(jnp.int32, (many, rows), 1)
    fresh_valid = (fresh_at // steps == row_seq) & (fresh_at % steps <= row_step)
    cache_valid = lax.broadcasted_iota(jnp.int32, (many, cache_len), 1) < length_ref[...]
    score_scale = HD ** (-0.5)
    for chip in range(chips):
        span = slice(chip * HD, (chip + 1) * HD)
        joined = arrived_ref[0, chip, :, : 2 * core_cols].astype(jnp.float32)
        for group in range(1, groups):
            joined = joined + arrived_ref[group, chip, :, : 2 * core_cols].astype(jnp.float32)
        joined = (joined * scale + bias_ref[chip]).astype(jnp.bfloat16).astype(jnp.float32)
        parts = []
        for head in range(heads):
            parts.append(rotated(joined[:, head * HD : (head + 1) * HD]))
        query_buf[chip] = jnp.concatenate(parts, axis=0).astype(jnp.bfloat16)
        low = joined[:, heads * HD : (heads + 1) * HD]
        high = joined[:, (heads + 1) * HD :]
        fresh_keys = rotated(jnp.where(lane < HD // 2, low, pltpu.roll(high, HD // 2, 1))).astype(
            jnp.bfloat16
        )
        fresh_values = jnp.where(lane < HD // 2, pltpu.roll(low, HD // 2, 1), high).astype(
            jnp.bfloat16
        )
        new_keys_ref[:, span] = fresh_keys
        new_values_ref[:, span] = fresh_values
    for copy in key_copies:
        copy.wait()
    for chip in range(chips):
        span = slice(chip * HD, (chip + 1) * HD)
        queries = query_buf[chip]
        fresh_keys = new_keys_ref[:, span]
        fresh_values = new_values_ref[:, span]
        scores = None
        for seq in range(seqs):
            found = lax.dot_general(
                queries,
                key_buf[seq, :, span],
                (((1,), (1,)), ((), ())),
                preferred_element_type=jnp.float32,
            )
            scores = found if scores is None else jnp.where(row_seq == seq, found, scores)
        fresh_scores = lax.dot_general(
            queries, fresh_keys, (((1,), (1,)), ((), ())), preferred_element_type=jnp.float32
        )
        scores = jnp.where(cache_valid, scores * score_scale, masked_low)
        fresh_scores = jnp.where(fresh_valid, fresh_scores * score_scale, masked_low)
        top = jnp.maximum(
            jnp.max(scores, axis=1, keepdims=True), jnp.max(fresh_scores, axis=1, keepdims=True)
        )
        scores = jnp.exp(scores - top)
        fresh_scores = jnp.exp(fresh_scores - top)
        share = 1.0 / (
            jnp.sum(scores, axis=1, keepdims=True) + jnp.sum(fresh_scores, axis=1, keepdims=True)
        )
        weights = (scores * share).astype(jnp.bfloat16)
        fresh_weights = (fresh_scores * share).astype(jnp.bfloat16)
        attended = jnp.dot(fresh_weights, fresh_values, preferred_element_type=jnp.float32)
        if chip == 0:
            for copy in value_copies:
                copy.wait()
        for seq in range(seqs):
            found = jnp.dot(
                weights, value_buf[seq, :, span], preferred_element_type=jnp.float32
            )
            attended = attended + jnp.where(row_seq == seq, found, 0.0)
        for head in range(heads):
            piece = attended[head * rows : (head + 1) * rows].astype(jnp.bfloat16)
            for group in range(out_ref.shape[0]):
                out_ref[group, chip, :, head * HD : (head + 1) * HD] = piece


def attend(half, arrived, bias, cosine, sine, row_lengths, key_cache, value_cache, copies):
    _, chips, rows, _ = arrived.shape
    seqs, cache_len, kv_cols = key_cache.shape
    seqs = seqs // HALVES
    heads = 8
    return pl.pallas_call(
        functools.partial(attention_kernel, half),
        out_shape=(
            jax.ShapeDtypeStruct((copies, chips, rows, heads * HD), jnp.bfloat16),
            jax.ShapeDtypeStruct((rows, kv_cols), jnp.bfloat16),
            jax.ShapeDtypeStruct((rows, kv_cols), jnp.bfloat16),
        ),
        in_specs=[VMEM] * 5 + [HBM] * 2,
        out_specs=(VMEM, VMEM, VMEM),
        scratch_shapes=[
            pltpu.VMEM((seqs, cache_len, kv_cols), jnp.bfloat16),
            pltpu.VMEM((seqs, cache_len, kv_cols), jnp.bfloat16),
            pltpu.VMEM((chips, heads * rows, HD), jnp.bfloat16),
            pltpu.SemaphoreType.DMA((seqs,)),
            pltpu.SemaphoreType.DMA((seqs,)),
        ],
        compiler_params=pltpu.CompilerParams(vmem_limit_bytes=48 * 1024 * 1024),
        name="attend",
    )(arrived, bias, cosine, sine, row_lengths, key_cache, value_cache)


def projection_kernel(place_ref, slot_ref, table_ref, gain_ref, *rest):
    out_ref, wide_ref, weight_buf, kv_buf, sem = rest[-5:]
    chip, core = place_ref[0], place_ref[1]
    table_rows = table_ref.shape[0]
    q_cols, kv_cols = rest[0].shape[1], rest[2].shape[0]
    cols = q_cols + 2 * kv_cols
    step = pl.program_id(0)
    slot = turned(slot_ref[...])
    rows = slot.shape[0]
    copies = []
    for side in range(2):
        owner = (core + side) % 2
        spots = [weight_buf.at[:, pl.ds(pl.multiple_of(owner * q_cols, q_cols), q_cols)]]
        for part in range(2):
            first = pl.multiple_of((2 * owner + part) * kv_cols, kv_cols)
            spots.append(kv_buf.at[pl.ds(first, kv_cols), :])
        for part, spot in enumerate(spots):
            number = 2 * part + side
            copies.append(pltpu.make_async_copy(rest[number], spot, sem.at[number]))

    @pl.when(step == 0)
    def _():
        for copy in copies:
            copy.start()

    chosen = (
        lax.broadcasted_iota(jnp.int32, (rows, table_rows), 1) == slot
    ).astype(jnp.bfloat16)
    found = jnp.dot(chosen, table_ref[...], preferred_element_type=jnp.float32)
    wide_ref[...] = found.astype(jnp.bfloat16)
    gained = (found * gain_ref[...]).astype(jnp.bfloat16)

    @pl.when(step == 0)
    def _():
        for copy in copies:
            copy.wait()

    product = jnp.dot(gained, weight_buf[...], preferred_element_type=jnp.float32)
    out_ref[:, : 2 * q_cols] = product.astype(jnp.bfloat16)
    product = lax.dot_general(
        gained, kv_buf[...], (((1,), (1,)), ((), ())), preferred_element_type=jnp.float32
    )
    out_ref[:, 2 * q_cols : 2 * cols] = product.astype(jnp.bfloat16)
    strip = out_ref.shape[1] - 2 * cols
    out_ref[:, 2 * cols :] = wide_ref[:, pl.ds(pl.multiple_of(chip * strip, strip), strip)]


def project(place, slot, table, gain, weights, held, chips):
    rows = slot.shape[1]
    table_rows, width = table.shape
    q_cols, kv_cols = weights[0].shape[1], weights[2].shape[0]
    cols = q_cols + 2 * kv_cols
    out_cols = 2 * cols + width // chips
    block = 512
    return pl.pallas_call(
        projection_kernel,
        out_shape=jax.ShapeDtypeStruct((rows, out_cols), jnp.bfloat16),
        grid=(rows // block,),
        in_specs=[
            SMEM,
            pl.BlockSpec((1, block), lambda i: (0, i)),
            pl.BlockSpec((table_rows, width), lambda i: (0, 0)),
            pl.BlockSpec((1, width), lambda i: (0, 0)),
        ]
        + [HBM] * (len(weights) + len(held)),
        out_specs=pl.BlockSpec((block, out_cols), lambda i: (i, 0)),
        scratch_shapes=[
            pltpu.VMEM((block, width), jnp.bfloat16),
            pltpu.VMEM((width, 2 * q_cols), jnp.bfloat16),
            pltpu.VMEM((4 * kv_cols, width), jnp.bfloat16),
            pltpu.SemaphoreType.DMA((len(weights),)),
        ],
        compiler_params=pltpu.CompilerParams(vmem_limit_bytes=48 * 1024 * 1024),
        name="project",
    )(place, slot, table, gain, *weights, *held)


def branch_kernel(place_ref, rows_ref, *rest):
    weight_refs, out_ref = rest[:-1], rest[-1]
    core, line = place_ref[1], place_ref[2]
    depth, width = weight_refs[0].shape
    count = len(weight_refs) // 2
    for turn in range(count):
        block = pl.multiple_of(((line + count - turn) % count) * width, width)
        parts = []
        for side in range(2):
            where = pl.multiple_of(((core + side) % 2) * depth, depth)
            parts.append(
                jnp.dot(
                    rows_ref[:, pl.ds(where, depth)],
                    weight_refs[2 * turn + side][...],
                    preferred_element_type=jnp.float32,
                )
            )
        out_ref[:, pl.ds(block, width)] = (parts[0] + parts[1]).astype(jnp.bfloat16)


def branch_out(place, rows, weights):
    count = len(weights)
    width = weights[0].shape[1]
    return pl.pallas_call(
        branch_kernel,
        out_shape=jax.ShapeDtypeStruct((rows.shape[0], count // 2 * width), jnp.bfloat16),
        in_specs=[SMEM, VMEM] + [VMEM] * count,
        out_specs=VMEM,
        compiler_params=pltpu.CompilerParams(vmem_limit_bytes=WHOLE_VMEM),
        name="branch",
    )(place, rows, *weights)


def hidden_kernel(steps, branch_ref, strip_ref, out_ref):
    upper, layers, chips, rows, pair_width = branch_ref.shape
    groups = strip_ref.shape[0]
    strip = out_ref.shape[2] // (groups * chips)
    width = strip * chips
    lower = pair_width // width
    for group in range(groups):
        high, low, layer = group // (lower * layers), group // layers % lower, group % layers
        for part in range(chips):
            start = low * width + part * strip
            total = strip_ref[group, part, :, strip_ref.shape[3] - strip :].astype(jnp.float32)
            for chip in range(chips):
                total = total + branch_ref[high, layer, chip, :, start : start + strip].astype(
                    jnp.float32
                )
            start = group * width + part * strip
            for seq in range(rows // steps):
                out_ref[seq, :, start : start + strip] = total[
                    seq * steps : (seq + 1) * steps
                ].astype(jnp.bfloat16)


def hidden_sum(branches, arrived, steps):
    upper, layers, _, rows, pair_width = branches.shape
    return pl.pallas_call(
        functools.partial(hidden_kernel, steps),
        out_shape=jax.ShapeDtypeStruct(
            (rows // steps, steps, upper * layers * pair_width), jnp.bfloat16
        ),
        in_specs=[VMEM] * 2,
        out_specs=VMEM,
        compiler_params=pltpu.CompilerParams(vmem_limit_bytes=48 * 1024 * 1024),
        name="hidden_sum",
    )(branches, arrived)


def per_device(
    token_ids,
    lengths,
    embedding,
    norm_gain,
    q_weight,
    k_weight,
    v_weight,
    q_bias,
    k_bias,
    v_bias,
    o_weight,
    key_cache,
    value_cache,
):
    seq_here, step_count = token_ids.shape
    rows_here = seq_here * step_count
    vocab_here, width_here = embedding.shape
    line = lax.axis_index("yl")
    replicas = lax.axis_size(DP)
    chips = lax.axis_size(CHIPS)
    chip = lax.axis_index(CHIPS)
    core = lax.axis_index("core")
    parties = replicas * chips
    plane_rows = parties * rows_here
    place = jnp.stack([chip, core, line]).astype(jnp.int32)

    weights = []
    for own in (q_weight, k_weight.T, v_weight.T):
        weights += [own, swap_cores(own)]
    o_line = swap_lines(o_weight)
    o_weights = (o_weight, swap_cores(o_weight), o_line, swap_cores(o_line))
    core_cols = q_bias.shape[0] + k_bias.shape[0] + v_bias.shape[0]
    q_cols = q_bias.shape[0]

    sent_ids = jnp.broadcast_to(token_ids.reshape(1, rows_here), (parties * 2, rows_here))
    every_id = lax.all_to_all(sent_ids, EVERY, split_axis=0, concat_axis=0, tiled=True)
    plane_ids = every_id.reshape(parties, 2, rows_here).transpose(1, 0, 2).reshape(2, plane_rows)
    own_holder = lax.dynamic_index_in_dim(plane_ids, core, 0, keepdims=False) // (2 * vocab_here)
    def exchange(turn):
        first = turn * ROUND_ROWS
        turn_place = jnp.concatenate([place, jnp.asarray(first, jnp.int32).reshape(1)])
        mine, theirs, rank = look_up(turn_place, plane_ids, (q_bias, k_bias, v_bias), embedding)
        merged = mine + swap_cores(theirs)
        table = lax.all_to_all(
            jnp.broadcast_to(merged[None], (chips, SENT_ROWS, width_here)),
            CHIPS,
            split_axis=0,
            concat_axis=0,
            tiled=True,
        ).reshape(chips * SENT_ROWS, width_here)
        own_rank = lax.dynamic_index_in_dim(rank, core, 0, keepdims=False).reshape(-1)
        here = (own_rank >= first) & (own_rank < first + ROUND_ROWS)
        slot = jnp.where(here, own_holder * SENT_ROWS + own_rank - first, -1)
        return slot, table, jnp.max(rank) // ROUND_ROWS + 1

    own_gain = lax.dynamic_slice_in_dim(norm_gain, lax.axis_index(DP) * width_here, width_here)
    own_gain = own_gain.reshape(1, width_here).astype(jnp.float32)
    slot, table, rounds = exchange(0)
    pair_bias = table.reshape(chips, SENT_ROWS, width_here)
    pair_bias = pair_bias[:, ROUND_ROWS : ROUND_ROWS + 2, :core_cols].astype(jnp.float32)
    pair_bias = jnp.concatenate(
        [
            pair_bias[:, :, :q_cols].reshape(chips, 1, -1),
            pair_bias[:, :, q_cols:].reshape(chips, 1, -1),
        ],
        axis=2,
    )
    half_rows = rows_here // HALVES
    kv_heads = key_cache.shape[2] // HD
    positions = (lengths[:, None] + jnp.arange(step_count, dtype=jnp.int32)[None, :]).reshape(-1)
    frequency = rope_base ** (-(2.0 * jnp.arange(HD // 2, dtype=jnp.float32)) / HD)
    angles = positions.astype(jnp.float32)[:, None] * frequency
    cosine, sine = jnp.cos(angles), jnp.sin(angles)
    cosine = jnp.concatenate([cosine, cosine], axis=1)
    sine = jnp.concatenate([-sine, sine], axis=1)
    row_lengths = jnp.repeat(lengths, step_count)

    def part_of(values, half):
        return values.reshape(parties, HALVES, half_rows)[:, half].reshape(1, -1)

    payloads = tuple(
        project(place, part_of(slot, half), table, own_gain, weights, (o_line,), chips)
        for half in range(HALVES)
    )

    def further(turn, sofar):
        turn_slot, turn_table, _ = exchange(turn)
        return tuple(
            sofar[half]
            + project(
                place, part_of(turn_slot, half), turn_table, own_gain, weights, (), chips
            )
            for half in range(HALVES)
        )

    payloads = lax.fori_loop(1, rounds, further, payloads)
    layer_count = lax.axis_size(("yh", "zl"))
    arrived, new_keys, new_values, branches = [], [], [], []
    for half in range(HALVES):
        here = lax.all_to_all(payloads[half], PLANE, split_axis=0, concat_axis=0, tiled=True)
        here = here.reshape(replicas, chips, half_rows, -1)
        rows = slice(half * half_rows, (half + 1) * half_rows)
        spread, keys, values = attend(
            half,
            here,
            pair_bias,
            cosine[rows],
            sine[rows],
            jnp.tile(row_lengths[rows], 8 * kv_heads // chips).reshape(-1, 1),
            key_cache,
            value_cache,
            layer_count,
        )
        gathered = lax.all_to_all(
            spread.reshape(-1, half_rows, 2 * q_cols), LAYER, split_axis=0, concat_axis=0, tiled=True
        ).reshape(-1, 2 * q_cols)
        branch = branch_out(place, gathered, o_weights)
        back = lax.all_to_all(branch, LAYER, split_axis=0, concat_axis=0, tiled=True)
        branches.append(back.reshape(2, layer_count // 2, chips, half_rows, -1))
        arrived.append(here)
        new_keys.append(keys)
        new_values.append(values)
    hidden = hidden_sum(branches[0], arrived[0], step_count)
    new_keys = jnp.concatenate(new_keys, axis=0)
    new_values = jnp.concatenate(new_values, axis=0)
    return (
        hidden,
        new_keys.reshape(seq_here, step_count, -1),
        new_values.reshape(seq_here, step_count, -1),
    )


def solution(mesh):
    fine = Mesh(mesh.devices.reshape(2, 2, 2, 2, 4, 2), EVERY)
    tensor = CHIPS + ("core",)
    placed = (
        P(EVERY, None),
        P(EVERY),
        P(tensor, DP),
        P(),
        P(DP, tensor),
        P(DP, tensor),
        P(DP, tensor),
        P(tensor),
        P(tensor),
        P(tensor),
        P(tensor, DP),
        P(EVERY, None, None),
        P(EVERY, None, None),
    )
    return jax.shard_map(
        per_device,
        mesh=fine,
        in_specs=placed,
        out_specs=(
            P(EVERY, None, None),
            P(EVERY, None, None),
            P(EVERY, None, None),
        ),
        check_vma=False,
    )
```

```python
import functools

import jax
import jax.numpy as jnp
from jax import lax
from jax.experimental import pallas as pl
from jax.experimental.pallas import tpu as pltpu
from jax.sharding import Mesh
from jax.sharding import PartitionSpec as P

HD = 128
ROUND_ROWS = 118
SENT_ROWS = 120
CHIP_COUNT = 8
WHOLE_VMEM = 60 * 1024 * 1024
HALVES = 1

norm_epsilon = 1e-06
rope_base = 1000000.0
masked_low = -1e30

DP = ("yh", "yl", "zl")
CHIPS = ("zh", "x")
LAYER = ("yh", "zl", "zh", "x")
PLANE = ("yh", "yl", "zl", "zh", "x")
EVERY = ("yh", "yl", "zl", "zh", "x", "core")


def swap_cores(value):
    return lax.ppermute(value, "core", [(0, 1), (1, 0)])


def swap_lines(value):
    return lax.ppermute(value, "yl", [(0, 1), (1, 0)])


VMEM = pl.BlockSpec(memory_space=pltpu.VMEM)
SMEM = pl.BlockSpec(memory_space=pltpu.SMEM)
HBM = pl.BlockSpec(memory_space=pltpu.HBM)


def turned(row):
    wide = jnp.broadcast_to(row.astype(jnp.float32), (8, row.shape[1]))
    return jnp.transpose(wide)[:, :1].astype(jnp.int32)


def lookup_kernel(place_ref, id_row_ref, q_ref, k_ref, v_ref, vocab_ref, *rest):
    mine_ref, theirs_ref, rank_ref, list_ref, total_ref, vocab_buf, sem = rest
    chip, core, first = place_ref[0], place_ref[1], place_ref[3]
    planes, _, rows = id_row_ref.shape
    vocab_here = vocab_ref.shape[0]
    steps = sem.shape[0]
    span = vocab_here // steps
    copies = [
        pltpu.make_async_copy(
            vocab_ref.at[pl.ds(step * span, span), :],
            vocab_buf.at[pl.ds(step * span, span), :],
            sem.at[step],
        )
        for step in range(steps)
    ]
    for copy in copies:
        copy.start()
    across = lax.broadcasted_iota(jnp.int32, (rows, rows), 1)
    down = lax.broadcasted_iota(jnp.int32, (rows, rows), 0)
    earlier = across < down
    slot = lax.broadcasted_iota(jnp.int32, (SENT_ROWS, rows), 0)
    for plane in range(planes):
        id_row = id_row_ref[plane]
        id_col = turned(id_row)
        again = jnp.where((id_row == id_col) & earlier, 1, 0)
        key_col = jnp.where(jnp.max(again, axis=1, keepdims=True) == 0, id_col, -1)
        edge_row = jnp.zeros_like(id_row)
        for other in range(1, CHIP_COUNT):
            edge = other * 2 * vocab_here
            edge_row = jnp.where(id_row >= edge, edge, edge_row)
        before = (key_col >= edge_row) & (key_col < id_row)
        rank = jnp.sum(before.astype(jnp.int32), axis=0, keepdims=True)
        rank_ref[plane] = rank
        offset = id_row - (2 * chip + core) * vocab_here
        listed = (offset >= 0) & (offset < vocab_here)
        wanted = jnp.where(listed, rank - first, -1)
        chosen = (wanted == slot) & (slot < ROUND_ROWS)
        list_ref[plane * SENT_ROWS : (plane + 1) * SENT_ROWS, :] = jnp.max(
            jnp.where(chosen, offset, -1), axis=1, keepdims=True
        )

    total = None
    for step in range(steps):
        entry = lax.broadcasted_iota(jnp.int32, (planes * SENT_ROWS, span), 1) + step * span
        chosen = (entry == list_ref[...]).astype(jnp.bfloat16)
        copies[step].wait()
        found = jnp.dot(
            chosen, vocab_buf[step * span : (step + 1) * span, :], preferred_element_type=jnp.float32
        )
        total = found if total is None else total + found
    total_ref[...] = total
    width = total_ref.shape[1]
    pieces = [piece[...].astype(jnp.float32) for piece in (q_ref, k_ref, v_ref)]
    filled = sum(piece.shape[1] for piece in pieces)
    pieces.append(jnp.zeros((1, width - filled), jnp.float32))
    bias = jnp.broadcast_to(jnp.concatenate(pieces, axis=1), (8, width))
    is_bias = (
        lax.broadcasted_iota(jnp.int32, (8, 1), 0) == ROUND_ROWS + core - (SENT_ROWS - 8)
    )
    for side, target in ((0, mine_ref), (1, theirs_ref)):
        plane = (core + side) % 2
        start = pl.multiple_of(plane * SENT_ROWS, SENT_ROWS)
        tail = pl.ds(start + SENT_ROWS - 8, 8)
        total_ref[tail, :] = jnp.where(is_bias, bias, total_ref[tail, :])
        target[...] = total_ref[pl.ds(start, SENT_ROWS), :].astype(jnp.bfloat16)


def look_up(place, plane_ids, biases, embedding):
    planes, rows = plane_ids.shape
    vocab_here, width = embedding.shape
    steps = 3
    return pl.pallas_call(
        lookup_kernel,
        out_shape=(
            jax.ShapeDtypeStruct((SENT_ROWS, width), jnp.bfloat16),
            jax.ShapeDtypeStruct((SENT_ROWS, width), jnp.bfloat16),
            jax.ShapeDtypeStruct((planes, 1, rows), jnp.int32),
        ),
        in_specs=[SMEM] + [VMEM] * (1 + len(biases)) + [HBM],
        out_specs=(VMEM, VMEM, VMEM),
        scratch_shapes=[
            pltpu.VMEM((planes * SENT_ROWS, 1), jnp.int32),
            pltpu.VMEM((planes * SENT_ROWS, width), jnp.float32),
            pltpu.VMEM((vocab_here, width), jnp.bfloat16),
            pltpu.SemaphoreType.DMA((steps,)),
        ],
        compiler_params=pltpu.CompilerParams(vmem_limit_bytes=48 * 1024 * 1024),
        name="look_up",
    )(
        place,
        plane_ids.reshape(planes, 1, rows),
        *[bias.reshape(1, -1) for bias in biases],
        embedding,
    )


def attention_kernel(
    half,
    arrived_ref, bias_ref, cosine_ref, sine_ref, length_ref, keys_ref, values_ref, *rest
):
    out_ref, new_keys_ref, new_values_ref = rest[:3]
    key_buf, value_buf, query_buf, key_sem, value_sem = rest[3:]
    groups, chips, rows, _ = arrived_ref.shape
    seqs, cache_len, _ = key_buf.shape
    steps = rows // seqs
    core_cols = bias_ref.shape[2] // 2
    heads = out_ref.shape[3] // HD
    many = heads * rows
    key_copies, value_copies = [], []
    for seq in range(seqs):
        source = half * seqs + seq
        key_copies.append(
            pltpu.make_async_copy(keys_ref.at[source], key_buf.at[seq], key_sem.at[seq])
        )
        value_copies.append(
            pltpu.make_async_copy(values_ref.at[source], value_buf.at[seq], value_sem.at[seq])
        )
    for copy in key_copies + value_copies:
        copy.start()
    square = None
    for group in range(groups):
        for chip in range(chips):
            part = arrived_ref[group, chip, :, 2 * core_cols :].astype(jnp.float32)
            square = part * part if square is None else square + part * part
    width = groups * chips * square.shape[1]
    scale = lax.rsqrt(jnp.sum(square, axis=1, keepdims=True) / width + norm_epsilon)
    cosine = cosine_ref[...]
    sine = sine_ref[...]
    lane = lax.broadcasted_iota(jnp.int32, (rows, HD), 1)

    def rotated(features):
        return features * cosine + pltpu.roll(features, HD // 2, 1) * sine

    row_at = lax.broadcasted_iota(jnp.int32, (many, 1), 0) % rows
    row_seq = row_at // steps
    row_step = row_at % steps
    fresh_at = lax.broadcasted_iota(jnp.int32, (many, rows), 1)
    fresh_valid = (fresh_at // steps == row_seq) & (fresh_at % steps <= row_step)
    cache_valid = lax.broadcasted_iota(jnp.int32, (many, cache_len), 1) < length_ref[...]
    score_scale = HD ** (-0.5)
    for chip in range(chips):
        span = slice(chip * HD, (chip + 1) * HD)
        joined = arrived_ref[0, chip, :, : 2 * core_cols].astype(jnp.float32)
        for group in range(1, groups):
            joined = joined + arrived_ref[group, chip, :, : 2 * core_cols].astype(jnp.float32)
        joined = (joined * scale + bias_ref[chip]).astype(jnp.bfloat16).astype(jnp.float32)
        parts = []
        for head in range(heads):
            parts.append(rotated(joined[:, head * HD : (head + 1) * HD]))
        query_buf[chip] = jnp.concatenate(parts, axis=0).astype(jnp.bfloat16)
        low = joined[:, heads * HD : (heads + 1) * HD]
        high = joined[:, (heads + 1) * HD :]
        fresh_keys = rotated(jnp.where(lane < HD // 2, low, pltpu.roll(high, HD // 2, 1))).astype(
            jnp.bfloat16
        )
        fresh_values = jnp.where(lane < HD // 2, pltpu.roll(low, HD // 2, 1), high).astype(
            jnp.bfloat16
        )
        new_keys_ref[:, span] = fresh_keys
        new_values_ref[:, span] = fresh_values
    for copy in key_copies:
        copy.wait()
    for chip in range(chips):
        span = slice(chip * HD, (chip + 1) * HD)
        queries = query_buf[chip]
        fresh_keys = new_keys_ref[:, span]
        fresh_values = new_values_ref[:, span]
        scores = None
        for seq in range(seqs):
            found = lax.dot_general(
                queries,
                key_buf[seq, :, span],
                (((1,), (1,)), ((), ())),
                preferred_element_type=jnp.float32,
            )
            scores = found if scores is None else jnp.where(row_seq == seq, found, scores)
        fresh_scores = lax.dot_general(
            queries, fresh_keys, (((1,), (1,)), ((), ())), preferred_element_type=jnp.float32
        )
        scores = jnp.where(cache_valid, scores * score_scale, masked_low)
        fresh_scores = jnp.where(fresh_valid, fresh_scores * score_scale, masked_low)
        top = jnp.maximum(
            jnp.max(scores, axis=1, keepdims=True), jnp.max(fresh_scores, axis=1, keepdims=True)
        )
        scores = jnp.exp(scores - top)
        fresh_scores = jnp.exp(fresh_scores - top)
        share = 1.0 / (
            jnp.sum(scores, axis=1, keepdims=True) + jnp.sum(fresh_scores, axis=1, keepdims=True)
        )
        weights = (scores * share).astype(jnp.bfloat16)
        fresh_weights = (fresh_scores * share).astype(jnp.bfloat16)
        attended = jnp.dot(fresh_weights, fresh_values, preferred_element_type=jnp.float32)
        if chip == 0:
            for copy in value_copies:
                copy.wait()
        for seq in range(seqs):
            found = jnp.dot(
                weights, value_buf[seq, :, span], preferred_element_type=jnp.float32
            )
            attended = attended + jnp.where(row_seq == seq, found, 0.0)
        for head in range(heads):
            piece = attended[head * rows : (head + 1) * rows].astype(jnp.bfloat16)
            for group in range(out_ref.shape[0]):
                out_ref[group, chip, :, head * HD : (head + 1) * HD] = piece


def attend(half, arrived, bias, cosine, sine, row_lengths, key_cache, value_cache, copies):
    _, chips, rows, _ = arrived.shape
    seqs, cache_len, kv_cols = key_cache.shape
    seqs = seqs // HALVES
    heads = 8
    return pl.pallas_call(
        functools.partial(attention_kernel, half),
        out_shape=(
            jax.ShapeDtypeStruct((copies, chips, rows, heads * HD), jnp.bfloat16),
            jax.ShapeDtypeStruct((rows, kv_cols), jnp.bfloat16),
            jax.ShapeDtypeStruct((rows, kv_cols), jnp.bfloat16),
        ),
        in_specs=[VMEM] * 5 + [HBM] * 2,
        out_specs=(VMEM, VMEM, VMEM),
        scratch_shapes=[
            pltpu.VMEM((seqs, cache_len, kv_cols), jnp.bfloat16),
            pltpu.VMEM((seqs, cache_len, kv_cols), jnp.bfloat16),
            pltpu.VMEM((chips, heads * rows, HD), jnp.bfloat16),
            pltpu.SemaphoreType.DMA((seqs,)),
            pltpu.SemaphoreType.DMA((seqs,)),
        ],
        compiler_params=pltpu.CompilerParams(vmem_limit_bytes=48 * 1024 * 1024),
        name="attend",
    )(arrived, bias, cosine, sine, row_lengths, key_cache, value_cache)


def projection_kernel(place_ref, slot_ref, table_ref, gain_ref, *rest):
    out_ref, wide_ref, weight_buf, kv_buf, sem = rest[-5:]
    chip, core = place_ref[0], place_ref[1]
    table_rows = table_ref.shape[0]
    q_cols, kv_cols = rest[0].shape[1], rest[2].shape[0]
    cols = q_cols + 2 * kv_cols
    step = pl.program_id(0)
    slot = turned(slot_ref[...])
    rows = slot.shape[0]
    copies = []
    for side in range(2):
        owner = (core + side) % 2
        spots = [weight_buf.at[:, pl.ds(pl.multiple_of(owner * q_cols, q_cols), q_cols)]]
        for part in range(2):
            first = pl.multiple_of((2 * owner + part) * kv_cols, kv_cols)
            spots.append(kv_buf.at[pl.ds(first, kv_cols), :])
        for part, spot in enumerate(spots):
            number = 2 * part + side
            copies.append(pltpu.make_async_copy(rest[number], spot, sem.at[number]))

    @pl.when(step == 0)
    def _():
        for copy in copies:
            copy.start()

    chosen = (
        lax.broadcasted_iota(jnp.int32, (rows, table_rows), 1) == slot
    ).astype(jnp.bfloat16)
    found = jnp.dot(chosen, table_ref[...], preferred_element_type=jnp.float32)
    wide_ref[...] = found.astype(jnp.bfloat16)
    gained = (found * gain_ref[...]).astype(jnp.bfloat16)

    @pl.when(step == 0)
    def _():
        for copy in copies:
            copy.wait()

    product = jnp.dot(gained, weight_buf[...], preferred_element_type=jnp.float32)
    out_ref[:, : 2 * q_cols] = product.astype(jnp.bfloat16)
    product = lax.dot_general(
        gained, kv_buf[...], (((1,), (1,)), ((), ())), preferred_element_type=jnp.float32
    )
    out_ref[:, 2 * q_cols : 2 * cols] = product.astype(jnp.bfloat16)
    strip = out_ref.shape[1] - 2 * cols
    out_ref[:, 2 * cols :] = wide_ref[:, pl.ds(pl.multiple_of(chip * strip, strip), strip)]


def project(place, slot, table, gain, weights, held, chips):
    rows = slot.shape[1]
    table_rows, width = table.shape
    q_cols, kv_cols = weights[0].shape[1], weights[2].shape[0]
    cols = q_cols + 2 * kv_cols
    out_cols = 2 * cols + width // chips
    block = 512
    return pl.pallas_call(
        projection_kernel,
        out_shape=jax.ShapeDtypeStruct((rows, out_cols), jnp.bfloat16),
        grid=(rows // block,),
        in_specs=[
            SMEM,
            pl.BlockSpec((1, block), lambda i: (0, i)),
            pl.BlockSpec((table_rows, width), lambda i: (0, 0)),
            pl.BlockSpec((1, width), lambda i: (0, 0)),
        ]
        + [HBM] * (len(weights) + len(held)),
        out_specs=pl.BlockSpec((block, out_cols), lambda i: (i, 0)),
        scratch_shapes=[
            pltpu.VMEM((block, width), jnp.bfloat16),
            pltpu.VMEM((width, 2 * q_cols), jnp.bfloat16),
            pltpu.VMEM((4 * kv_cols, width), jnp.bfloat16),
            pltpu.SemaphoreType.DMA((len(weights),)),
        ],
        compiler_params=pltpu.CompilerParams(vmem_limit_bytes=48 * 1024 * 1024),
        name="project",
    )(place, slot, table, gain, *weights, *held)


def branch_kernel(place_ref, rows_ref, *rest):
    weight_refs, out_ref = rest[:-1], rest[-1]
    core, line = place_ref[1], place_ref[2]
    depth, width = weight_refs[0].shape
    count = len(weight_refs) // 2
    for turn in range(count):
        block = pl.multiple_of(((line + count - turn) % count) * width, width)
        parts = []
        for side in range(2):
            where = pl.multiple_of(((core + side) % 2) * depth, depth)
            parts.append(
                jnp.dot(
                    rows_ref[:, pl.ds(where, depth)],
                    weight_refs[2 * turn + side][...],
                    preferred_element_type=jnp.float32,
                )
            )
        out_ref[:, pl.ds(block, width)] = (parts[0] + parts[1]).astype(jnp.bfloat16)


def branch_out(place, rows, weights):
    count = len(weights)
    width = weights[0].shape[1]
    return pl.pallas_call(
        branch_kernel,
        out_shape=jax.ShapeDtypeStruct((rows.shape[0], count // 2 * width), jnp.bfloat16),
        in_specs=[SMEM, VMEM] + [VMEM] * count,
        out_specs=VMEM,
        compiler_params=pltpu.CompilerParams(vmem_limit_bytes=WHOLE_VMEM),
        name="branch",
    )(place, rows, *weights)


def hidden_kernel(steps, branch_ref, strip_ref, out_ref):
    upper, layers, chips, rows, pair_width = branch_ref.shape
    groups = strip_ref.shape[0]
    strip = out_ref.shape[2] // (groups * chips)
    width = strip * chips
    lower = pair_width // width
    for group in range(groups):
        high, low, layer = group // (lower * layers), group // layers % lower, group % layers
        for part in range(chips):
            start = low * width + part * strip
            total = strip_ref[group, part, :, strip_ref.shape[3] - strip :].astype(jnp.float32)
            for chip in range(chips):
                total = total + branch_ref[high, layer, chip, :, start : start + strip].astype(
                    jnp.float32
                )
            start = group * width + part * strip
            for seq in range(rows // steps):
                out_ref[seq, :, start : start + strip] = total[
                    seq * steps : (seq + 1) * steps
                ].astype(jnp.bfloat16)


def hidden_sum(branches, arrived, steps):
    upper, layers, _, rows, pair_width = branches.shape
    return pl.pallas_call(
        functools.partial(hidden_kernel, steps),
        out_shape=jax.ShapeDtypeStruct(
            (rows // steps, steps, upper * layers * pair_width), jnp.bfloat16
        ),
        in_specs=[VMEM] * 2,
        out_specs=VMEM,
        compiler_params=pltpu.CompilerParams(vmem_limit_bytes=48 * 1024 * 1024),
        name="hidden_sum",
    )(branches, arrived)


def per_device(
    token_ids,
    lengths,
    embedding,
    norm_gain,
    q_weight,
    k_weight,
    v_weight,
    q_bias,
    k_bias,
    v_bias,
    o_weight,
    key_cache,
    value_cache,
):
    seq_here, step_count = token_ids.shape
    rows_here = seq_here * step_count
    vocab_here, width_here = embedding.shape
    line = lax.axis_index("yl")
    replicas = lax.axis_size(DP)
    chips = lax.axis_size(CHIPS)
    chip = lax.axis_index(CHIPS)
    core = lax.axis_index("core")
    parties = replicas * chips
    plane_rows = parties * rows_here
    place = jnp.stack([chip, core, line]).astype(jnp.int32)

    weights = []
    for own in (q_weight, k_weight.T, v_weight.T):
        weights += [own, swap_cores(own)]
    o_line = swap_lines(o_weight)
    o_weights = (o_weight, swap_cores(o_weight), o_line, swap_cores(o_line))
    core_cols = q_bias.shape[0] + k_bias.shape[0] + v_bias.shape[0]
    q_cols = q_bias.shape[0]

    sent_ids = jnp.broadcast_to(token_ids.reshape(1, rows_here), (parties * 2, rows_here))
    every_id = lax.all_to_all(sent_ids, EVERY, split_axis=0, concat_axis=0, tiled=True)
    plane_ids = every_id.reshape(parties, 2, rows_here).transpose(1, 0, 2).reshape(2, plane_rows)
    own_holder = lax.dynamic_index_in_dim(plane_ids, core, 0, keepdims=False) // (2 * vocab_here)
    def exchange(turn):
        first = turn * ROUND_ROWS
        turn_place = jnp.concatenate([place, jnp.asarray(first, jnp.int32).reshape(1)])
        mine, theirs, rank = look_up(turn_place, plane_ids, (q_bias, k_bias, v_bias), embedding)
        merged = mine + swap_cores(theirs)
        table = lax.all_to_all(
            jnp.broadcast_to(merged[None], (chips, SENT_ROWS, width_here)),
            CHIPS,
            split_axis=0,
            concat_axis=0,
            tiled=True,
        ).reshape(chips * SENT_ROWS, width_here)
        own_rank = lax.dynamic_index_in_dim(rank, core, 0, keepdims=False).reshape(-1)
        here = (own_rank >= first) & (own_rank < first + ROUND_ROWS)
        slot = jnp.where(here, own_holder * SENT_ROWS + own_rank - first, -1)
        return slot, table, jnp.max(rank) // ROUND_ROWS + 1

    own_gain = lax.dynamic_slice_in_dim(norm_gain, lax.axis_index(DP) * width_here, width_here)
    own_gain = own_gain.reshape(1, width_here).astype(jnp.float32)
    slot, table, rounds = exchange(0)
    pair_bias = table.reshape(chips, SENT_ROWS, width_here)
    pair_bias = pair_bias[:, ROUND_ROWS : ROUND_ROWS + 2, :core_cols].astype(jnp.float32)
    pair_bias = jnp.concatenate(
        [
            pair_bias[:, :, :q_cols].reshape(chips, 1, -1),
            pair_bias[:, :, q_cols:].reshape(chips, 1, -1),
        ],
        axis=2,
    )
    half_rows = rows_here // HALVES
    kv_heads = key_cache.shape[2] // HD
    positions = (lengths[:, None] + jnp.arange(step_count, dtype=jnp.int32)[None, :]).reshape(-1)
    frequency = rope_base ** (-(2.0 * jnp.arange(HD // 2, dtype=jnp.float32)) / HD)
    angles = positions.astype(jnp.float32)[:, None] * frequency
    cosine, sine = jnp.cos(angles), jnp.sin(angles)
    cosine = jnp.concatenate([cosine, cosine], axis=1)
    sine = jnp.concatenate([-sine, sine], axis=1)
    row_lengths = jnp.repeat(lengths, step_count)

    def part_of(values, half):
        return values.reshape(parties, HALVES, half_rows)[:, half].reshape(1, -1)

    payloads = tuple(
        project(place, part_of(slot, half), table, own_gain, weights, (o_line,), chips)
        for half in range(HALVES)
    )

    def further(turn, sofar):
        turn_slot, turn_table, _ = exchange(turn)
        return tuple(
            sofar[half]
            + project(
                place, part_of(turn_slot, half), turn_table, own_gain, weights, (), chips
            )
            for half in range(HALVES)
        )

    payloads = lax.fori_loop(1, rounds, further, payloads)
    layer_count = lax.axis_size(("yh", "zl"))
    arrived, new_keys, new_values, branches = [], [], [], []
    for half in range(HALVES):
        here = lax.all_to_all(payloads[half], PLANE, split_axis=0, concat_axis=0, tiled=True)
        here = here.reshape(replicas, chips, half_rows, -1)
        rows = slice(half * half_rows, (half + 1) * half_rows)
        spread, keys, values = attend(
            half,
            here,
            pair_bias,
            cosine[rows],
            sine[rows],
            jnp.tile(row_lengths[rows], 8 * kv_heads // chips).reshape(-1, 1),
            key_cache,
            value_cache,
            layer_count,
        )
        gathered = lax.all_to_all(
            spread.reshape(-1, half_rows, 2 * q_cols), LAYER, split_axis=0, concat_axis=0, tiled=True
        ).reshape(-1, 2 * q_cols)
        branch = branch_out(place, gathered, o_weights)
        back = lax.all_to_all(branch, LAYER, split_axis=0, concat_axis=0, tiled=True)
        branches.append(back.reshape(2, layer_count // 2, chips, half_rows, -1))
        arrived.append(here)
        new_keys.append(keys)
        new_values.append(values)
    hidden = hidden_sum(branches[0], arrived[0], step_count)
    new_keys = jnp.concatenate(new_keys, axis=0)
    new_values = jnp.concatenate(new_values, axis=0)
    return (
        hidden,
        new_keys.reshape(seq_here, step_count, -1),
        new_values.reshape(seq_here, step_count, -1),
    )


def solution(mesh):
    fine = Mesh(mesh.devices.reshape(2, 2, 2, 2, 4, 2), EVERY)
    tensor = CHIPS + ("core",)
    placed = (
        P(EVERY, None),
        P(EVERY),
        P(tensor, DP),
        P(),
        P(DP, tensor),
        P(DP, tensor),
        P(DP, tensor),
        P(tensor),
        P(tensor),
        P(tensor),
        P(tensor, DP),
        P(EVERY, None, None),
        P(EVERY, None, None),
    )
    return jax.shard_map(
        per_device,
        mesh=fine,
        in_specs=placed,
        out_specs=(
            P(EVERY, None, None),
            P(EVERY, None, None),
            P(EVERY, None, None),
        ),
        check_vma=False,
    )
```

```python
import functools

import jax
import jax.numpy as jnp
from jax import lax
from jax.experimental import pallas as pl
from jax.experimental.pallas import tpu as pltpu
from jax.sharding import Mesh
from jax.sharding import PartitionSpec as P

HD = 128
ROUND_ROWS = 118
SENT_ROWS = 120
CHIP_COUNT = 8
WHOLE_VMEM = 60 * 1024 * 1024
HALVES = 1

norm_epsilon = 1e-06
rope_base = 1000000.0
masked_low = -1e30

DP = ("yh", "yl", "zl")
CHIPS = ("zh", "x")
LAYER = ("yh", "zl", "zh", "x")
PLANE = ("yh", "yl", "zl", "zh", "x")
EVERY = ("yh", "yl", "zl", "zh", "x", "core")


def swap_cores(value):
    return lax.ppermute(value, "core", [(0, 1), (1, 0)])


def swap_lines(value):
    return lax.ppermute(value, "yl", [(0, 1), (1, 0)])


VMEM = pl.BlockSpec(memory_space=pltpu.VMEM)
SMEM = pl.BlockSpec(memory_space=pltpu.SMEM)
HBM = pl.BlockSpec(memory_space=pltpu.HBM)


def turned(row):
    wide = jnp.broadcast_to(row.astype(jnp.float32), (8, row.shape[1]))
    return jnp.transpose(wide)[:, :1].astype(jnp.int32)


def lookup_kernel(place_ref, id_row_ref, q_ref, k_ref, v_ref, vocab_ref, *rest):
    mine_ref, theirs_ref, rank_ref, list_ref, total_ref, vocab_buf, sem = rest
    chip, core, first = place_ref[0], place_ref[1], place_ref[3]
    planes, _, rows = id_row_ref.shape
    vocab_here = vocab_ref.shape[0]
    steps = sem.shape[0]
    span = vocab_here // steps
    copies = [
        pltpu.make_async_copy(
            vocab_ref.at[pl.ds(step * span, span), :],
            vocab_buf.at[pl.ds(step * span, span), :],
            sem.at[step],
        )
        for step in range(steps)
    ]
    for copy in copies:
        copy.start()
    across = lax.broadcasted_iota(jnp.int32, (rows, rows), 1)
    down = lax.broadcasted_iota(jnp.int32, (rows, rows), 0)
    earlier = across < down
    slot = lax.broadcasted_iota(jnp.int32, (SENT_ROWS, rows), 0)
    for plane in range(planes):
        id_row = id_row_ref[plane]
        id_col = turned(id_row)
        again = jnp.where((id_row == id_col) & earlier, 1, 0)
        key_col = jnp.where(jnp.max(again, axis=1, keepdims=True) == 0, id_col, -1)
        edge_row = jnp.zeros_like(id_row)
        for other in range(1, CHIP_COUNT):
            edge = other * 2 * vocab_here
            edge_row = jnp.where(id_row >= edge, edge, edge_row)
        before = (key_col >= edge_row) & (key_col < id_row)
        rank = jnp.sum(before.astype(jnp.int32), axis=0, keepdims=True)
        rank_ref[plane] = rank
        offset = id_row - (2 * chip + core) * vocab_here
        listed = (offset >= 0) & (offset < vocab_here)
        wanted = jnp.where(listed, rank - first, -1)
        chosen = (wanted == slot) & (slot < ROUND_ROWS)
        list_ref[plane * SENT_ROWS : (plane + 1) * SENT_ROWS, :] = jnp.max(
            jnp.where(chosen, offset, -1), axis=1, keepdims=True
        )

    total = None
    for step in range(steps):
        entry = lax.broadcasted_iota(jnp.int32, (planes * SENT_ROWS, span), 1) + step * span
        chosen = (entry == list_ref[...]).astype(jnp.bfloat16)
        copies[step].wait()
        found = jnp.dot(
            chosen, vocab_buf[step * span : (step + 1) * span, :], preferred_element_type=jnp.float32
        )
        total = found if total is None else total + found
    total_ref[...] = total
    width = total_ref.shape[1]
    pieces = [piece[...].astype(jnp.float32) for piece in (q_ref, k_ref, v_ref)]
    filled = sum(piece.shape[1] for piece in pieces)
    pieces.append(jnp.zeros((1, width - filled), jnp.float32))
    bias = jnp.broadcast_to(jnp.concatenate(pieces, axis=1), (8, width))
    is_bias = (
        lax.broadcasted_iota(jnp.int32, (8, 1), 0) == ROUND_ROWS + core - (SENT_ROWS - 8)
    )
    for side, target in ((0, mine_ref), (1, theirs_ref)):
        plane = (core + side) % 2
        start = pl.multiple_of(plane * SENT_ROWS, SENT_ROWS)
        tail = pl.ds(start + SENT_ROWS - 8, 8)
        total_ref[tail, :] = jnp.where(is_bias, bias, total_ref[tail, :])
        target[...] = total_ref[pl.ds(start, SENT_ROWS), :].astype(jnp.bfloat16)


def look_up(place, plane_ids, biases, embedding):
    planes, rows = plane_ids.shape
    vocab_here, width = embedding.shape
    steps = 3
    return pl.pallas_call(
        lookup_kernel,
        out_shape=(
            jax.ShapeDtypeStruct((SENT_ROWS, width), jnp.bfloat16),
            jax.ShapeDtypeStruct((SENT_ROWS, width), jnp.bfloat16),
            jax.ShapeDtypeStruct((planes, 1, rows), jnp.int32),
        ),
        in_specs=[SMEM] + [VMEM] * (1 + len(biases)) + [HBM],
        out_specs=(VMEM, VMEM, VMEM),
        scratch_shapes=[
            pltpu.VMEM((planes * SENT_ROWS, 1), jnp.int32),
            pltpu.VMEM((planes * SENT_ROWS, width), jnp.float32),
            pltpu.VMEM((vocab_here, width), jnp.bfloat16),
            pltpu.SemaphoreType.DMA((steps,)),
        ],
        compiler_params=pltpu.CompilerParams(vmem_limit_bytes=48 * 1024 * 1024),
        name="look_up",
    )(
        place,
        plane_ids.reshape(planes, 1, rows),
        *[bias.reshape(1, -1) for bias in biases],
        embedding,
    )


def attention_kernel(
    half,
    arrived_ref, bias_ref, cosine_ref, sine_ref, length_ref, keys_ref, values_ref, *rest
):
    out_ref, new_keys_ref, new_values_ref = rest[:3]
    key_buf, value_buf, query_buf, key_sem, value_sem = rest[3:]
    groups, chips, rows, _ = arrived_ref.shape
    seqs, cache_len, _ = key_buf.shape
    steps = rows // seqs
    core_cols = bias_ref.shape[2] // 2
    heads = out_ref.shape[3] // HD
    many = heads * rows
    key_copies, value_copies = [], []
    for seq in range(seqs):
        source = half * seqs + seq
        key_copies.append(
            pltpu.make_async_copy(keys_ref.at[source], key_buf.at[seq], key_sem.at[seq])
        )
        value_copies.append(
            pltpu.make_async_copy(values_ref.at[source], value_buf.at[seq], value_sem.at[seq])
        )
    for copy in key_copies + value_copies:
        copy.start()
    square = None
    for group in range(groups):
        for chip in range(chips):
            part = arrived_ref[group, chip, :, 2 * core_cols :].astype(jnp.float32)
            square = part * part if square is None else square + part * part
    width = groups * chips * square.shape[1]
    scale = lax.rsqrt(jnp.sum(square, axis=1, keepdims=True) / width + norm_epsilon)
    cosine = cosine_ref[...]
    sine = sine_ref[...]
    lane = lax.broadcasted_iota(jnp.int32, (rows, HD), 1)

    def rotated(features):
        return features * cosine + pltpu.roll(features, HD // 2, 1) * sine

    row_at = lax.broadcasted_iota(jnp.int32, (many, 1), 0) % rows
    row_seq = row_at // steps
    row_step = row_at % steps
    fresh_at = lax.broadcasted_iota(jnp.int32, (many, rows), 1)
    fresh_valid = (fresh_at // steps == row_seq) & (fresh_at % steps <= row_step)
    cache_valid = lax.broadcasted_iota(jnp.int32, (many, cache_len), 1) < length_ref[...]
    score_scale = HD ** (-0.5)
    for chip in range(chips):
        span = slice(chip * HD, (chip + 1) * HD)
        joined = arrived_ref[0, chip, :, : 2 * core_cols].astype(jnp.float32)
        for group in range(1, groups):
            joined = joined + arrived_ref[group, chip, :, : 2 * core_cols].astype(jnp.float32)
        joined = (joined * scale + bias_ref[chip]).astype(jnp.bfloat16).astype(jnp.float32)
        parts = []
        for head in range(heads):
            parts.append(rotated(joined[:, head * HD : (head + 1) * HD]))
        query_buf[chip] = jnp.concatenate(parts, axis=0).astype(jnp.bfloat16)
        low = joined[:, heads * HD : (heads + 1) * HD]
        high = joined[:, (heads + 1) * HD :]
        fresh_keys = rotated(jnp.where(lane < HD // 2, low, pltpu.roll(high, HD // 2, 1))).astype(
            jnp.bfloat16
        )
        fresh_values = jnp.where(lane < HD // 2, pltpu.roll(low, HD // 2, 1), high).astype(
            jnp.bfloat16
        )
        new_keys_ref[:, span] = fresh_keys
        new_values_ref[:, span] = fresh_values
    for copy in key_copies:
        copy.wait()
    for chip in range(chips):
        span = slice(chip * HD, (chip + 1) * HD)
        queries = query_buf[chip]
        fresh_keys = new_keys_ref[:, span]
        fresh_values = new_values_ref[:, span]
        scores = None
        for seq in range(seqs):
            found = lax.dot_general(
                queries,
                key_buf[seq, :, span],
                (((1,), (1,)), ((), ())),
                preferred_element_type=jnp.float32,
            )
            scores = found if scores is None else jnp.where(row_seq == seq, found, scores)
        fresh_scores = lax.dot_general(
            queries, fresh_keys, (((1,), (1,)), ((), ())), preferred_element_type=jnp.float32
        )
        scores = jnp.where(cache_valid, scores * score_scale, masked_low)
        fresh_scores = jnp.where(fresh_valid, fresh_scores * score_scale, masked_low)
        top = jnp.maximum(
            jnp.max(scores, axis=1, keepdims=True), jnp.max(fresh_scores, axis=1, keepdims=True)
        )
        scores = jnp.exp(scores - top)
        fresh_scores = jnp.exp(fresh_scores - top)
        share = 1.0 / (
            jnp.sum(scores, axis=1, keepdims=True) + jnp.sum(fresh_scores, axis=1, keepdims=True)
        )
        weights = (scores * share).astype(jnp.bfloat16)
        fresh_weights = (fresh_scores * share).astype(jnp.bfloat16)
        attended = jnp.dot(fresh_weights, fresh_values, preferred_element_type=jnp.float32)
        if chip == 0:
            for copy in value_copies:
                copy.wait()
        for seq in range(seqs):
            found = jnp.dot(
                weights, value_buf[seq, :, span], preferred_element_type=jnp.float32
            )
            attended = attended + jnp.where(row_seq == seq, found, 0.0)
        for head in range(heads):
            piece = attended[head * rows : (head + 1) * rows].astype(jnp.bfloat16)
            for group in range(out_ref.shape[0]):
                out_ref[group, chip, :, head * HD : (head + 1) * HD] = piece


def attend(half, arrived, bias, cosine, sine, row_lengths, key_cache, value_cache, copies):
    _, chips, rows, _ = arrived.shape
    seqs, cache_len, kv_cols = key_cache.shape
    seqs = seqs // HALVES
    heads = 8
    return pl.pallas_call(
        functools.partial(attention_kernel, half),
        out_shape=(
            jax.ShapeDtypeStruct((copies, chips, rows, heads * HD), jnp.bfloat16),
            jax.ShapeDtypeStruct((rows, kv_cols), jnp.bfloat16),
            jax.ShapeDtypeStruct((rows, kv_cols), jnp.bfloat16),
        ),
        in_specs=[VMEM] * 5 + [HBM] * 2,
        out_specs=(VMEM, VMEM, VMEM),
        scratch_shapes=[
            pltpu.VMEM((seqs, cache_len, kv_cols), jnp.bfloat16),
            pltpu.VMEM((seqs, cache_len, kv_cols), jnp.bfloat16),
            pltpu.VMEM((chips, heads * rows, HD), jnp.bfloat16),
            pltpu.SemaphoreType.DMA((seqs,)),
            pltpu.SemaphoreType.DMA((seqs,)),
        ],
        compiler_params=pltpu.CompilerParams(vmem_limit_bytes=48 * 1024 * 1024),
        name="attend",
    )(arrived, bias, cosine, sine, row_lengths, key_cache, value_cache)


def projection_kernel(place_ref, slot_ref, table_ref, gain_ref, *rest):
    out_ref, wide_ref, weight_buf, kv_buf, sem = rest[-5:]
    chip, core = place_ref[0], place_ref[1]
    table_rows = table_ref.shape[0]
    q_cols, kv_cols = rest[0].shape[1], rest[2].shape[0]
    cols = q_cols + 2 * kv_cols
    step = pl.program_id(0)
    slot = turned(slot_ref[...])
    rows = slot.shape[0]
    copies = []
    for side in range(2):
        owner = (core + side) % 2
        spots = [weight_buf.at[:, pl.ds(pl.multiple_of(owner * q_cols, q_cols), q_cols)]]
        for part in range(2):
            first = pl.multiple_of((2 * owner + part) * kv_cols, kv_cols)
            spots.append(kv_buf.at[pl.ds(first, kv_cols), :])
        for part, spot in enumerate(spots):
            number = 2 * part + side
            copies.append(pltpu.make_async_copy(rest[number], spot, sem.at[number]))

    @pl.when(step == 0)
    def _():
        for copy in copies:
            copy.start()

    chosen = (
        lax.broadcasted_iota(jnp.int32, (rows, table_rows), 1) == slot
    ).astype(jnp.bfloat16)
    found = jnp.dot(chosen, table_ref[...], preferred_element_type=jnp.float32)
    wide_ref[...] = found.astype(jnp.bfloat16)
    gained = (found * gain_ref[...]).astype(jnp.bfloat16)

    @pl.when(step == 0)
    def _():
        for copy in copies:
            copy.wait()

    product = jnp.dot(gained, weight_buf[...], preferred_element_type=jnp.float32)
    out_ref[:, : 2 * q_cols] = product.astype(jnp.bfloat16)
    product = lax.dot_general(
        gained, kv_buf[...], (((1,), (1,)), ((), ())), preferred_element_type=jnp.float32
    )
    out_ref[:, 2 * q_cols : 2 * cols] = product.astype(jnp.bfloat16)
    strip = out_ref.shape[1] - 2 * cols
    out_ref[:, 2 * cols :] = wide_ref[:, pl.ds(pl.multiple_of(chip * strip, strip), strip)]


def project(place, slot, table, gain, weights, held, chips):
    rows = slot.shape[1]
    table_rows, width = table.shape
    q_cols, kv_cols = weights[0].shape[1], weights[2].shape[0]
    cols = q_cols + 2 * kv_cols
    out_cols = 2 * cols + width // chips
    block = 512
    return pl.pallas_call(
        projection_kernel,
        out_shape=jax.ShapeDtypeStruct((rows, out_cols), jnp.bfloat16),
        grid=(rows // block,),
        in_specs=[
            SMEM,
            pl.BlockSpec((1, block), lambda i: (0, i)),
            pl.BlockSpec((table_rows, width), lambda i: (0, 0)),
            pl.BlockSpec((1, width), lambda i: (0, 0)),
        ]
        + [HBM] * (len(weights) + len(held)),
        out_specs=pl.BlockSpec((block, out_cols), lambda i: (i, 0)),
        scratch_shapes=[
            pltpu.VMEM((block, width), jnp.bfloat16),
            pltpu.VMEM((width, 2 * q_cols), jnp.bfloat16),
            pltpu.VMEM((4 * kv_cols, width), jnp.bfloat16),
            pltpu.SemaphoreType.DMA((len(weights),)),
        ],
        compiler_params=pltpu.CompilerParams(vmem_limit_bytes=48 * 1024 * 1024),
        name="project",
    )(place, slot, table, gain, *weights, *held)


def branch_kernel(place_ref, rows_ref, *rest):
    weight_refs, out_ref = rest[:-1], rest[-1]
    core, line = place_ref[1], place_ref[2]
    depth, width = weight_refs[0].shape
    count = len(weight_refs) // 2
    for turn in range(count):
        block = pl.multiple_of(((line + count - turn) % count) * width, width)
        parts = []
        for side in range(2):
            where = pl.multiple_of(((core + side) % 2) * depth, depth)
            parts.append(
                jnp.dot(
                    rows_ref[:, pl.ds(where, depth)],
                    weight_refs[2 * turn + side][...],
                    preferred_element_type=jnp.float32,
                )
            )
        out_ref[:, pl.ds(block, width)] = (parts[0] + parts[1]).astype(jnp.bfloat16)


def branch_out(place, rows, weights):
    count = len(weights)
    width = weights[0].shape[1]
    return pl.pallas_call(
        branch_kernel,
        out_shape=jax.ShapeDtypeStruct((rows.shape[0], count // 2 * width), jnp.bfloat16),
        in_specs=[SMEM, VMEM] + [VMEM] * count,
        out_specs=VMEM,
        compiler_params=pltpu.CompilerParams(vmem_limit_bytes=WHOLE_VMEM),
        name="branch",
    )(place, rows, *weights)


def hidden_kernel(steps, branch_ref, strip_ref, out_ref):
    upper, layers, chips, rows, pair_width = branch_ref.shape
    groups = strip_ref.shape[0]
    strip = out_ref.shape[2] // (groups * chips)
    width = strip * chips
    lower = pair_width // width
    for group in range(groups):
        high, low, layer = group // (lower * layers), group // layers % lower, group % layers
        for part in range(chips):
            start = low * width + part * strip
            total = strip_ref[group, part, :, strip_ref.shape[3] - strip :].astype(jnp.float32)
            for chip in range(chips):
                total = total + branch_ref[high, layer, chip, :, start : start + strip].astype(
                    jnp.float32
                )
            start = group * width + part * strip
            for seq in range(rows // steps):
                out_ref[seq, :, start : start + strip] = total[
                    seq * steps : (seq + 1) * steps
                ].astype(jnp.bfloat16)


def hidden_sum(branches, arrived, steps):
    upper, layers, _, rows, pair_width = branches.shape
    return pl.pallas_call(
        functools.partial(hidden_kernel, steps),
        out_shape=jax.ShapeDtypeStruct(
            (rows // steps, steps, upper * layers * pair_width), jnp.bfloat16
        ),
        in_specs=[VMEM] * 2,
        out_specs=VMEM,
        compiler_params=pltpu.CompilerParams(vmem_limit_bytes=48 * 1024 * 1024),
        name="hidden_sum",
    )(branches, arrived)


def per_device(
    token_ids,
    lengths,
    embedding,
    norm_gain,
    q_weight,
    k_weight,
    v_weight,
    q_bias,
    k_bias,
    v_bias,
    o_weight,
    key_cache,
    value_cache,
):
    seq_here, step_count = token_ids.shape
    rows_here = seq_here * step_count
    vocab_here, width_here = embedding.shape
    line = lax.axis_index("yl")
    replicas = lax.axis_size(DP)
    chips = lax.axis_size(CHIPS)
    chip = lax.axis_index(CHIPS)
    core = lax.axis_index("core")
    parties = replicas * chips
    plane_rows = parties * rows_here
    place = jnp.stack([chip, core, line]).astype(jnp.int32)

    weights = []
    for own in (q_weight, k_weight.T, v_weight.T):
        weights += [own, swap_cores(own)]
    o_line = swap_lines(o_weight)
    o_weights = (o_weight, swap_cores(o_weight), o_line, swap_cores(o_line))
    core_cols = q_bias.shape[0] + k_bias.shape[0] + v_bias.shape[0]
    q_cols = q_bias.shape[0]

    layer_parties = parties // 2
    sent_ids = jnp.broadcast_to(token_ids.reshape(1, rows_here), (layer_parties, rows_here))
    near_ids = lax.all_to_all(sent_ids, LAYER, split_axis=0, concat_axis=0, tiled=True)
    other_ids = swap_cores(near_ids)
    core_ids = jnp.stack(
        [jnp.where(core == 0, near_ids, other_ids), jnp.where(core == 0, other_ids, near_ids)]
    )
    line_ids = swap_lines(core_ids)
    every_id = jnp.stack(
        [jnp.where(line == 0, core_ids, line_ids), jnp.where(line == 0, line_ids, core_ids)]
    )
    plane_ids = (
        every_id.reshape(2, 2, 2, layer_parties // 2, rows_here)
        .transpose(1, 2, 0, 3, 4)
        .reshape(2, plane_rows)
    )
    own_holder = lax.dynamic_index_in_dim(plane_ids, core, 0, keepdims=False) // (2 * vocab_here)
    def exchange(turn):
        first = turn * ROUND_ROWS
        turn_place = jnp.concatenate([place, jnp.asarray(first, jnp.int32).reshape(1)])
        mine, theirs, rank = look_up(turn_place, plane_ids, (q_bias, k_bias, v_bias), embedding)
        merged = mine + swap_cores(theirs)
        table = lax.all_to_all(
            jnp.broadcast_to(merged[None], (chips, SENT_ROWS, width_here)),
            CHIPS,
            split_axis=0,
            concat_axis=0,
            tiled=True,
        ).reshape(chips * SENT_ROWS, width_here)
        own_rank = lax.dynamic_index_in_dim(rank, core, 0, keepdims=False).reshape(-1)
        here = (own_rank >= first) & (own_rank < first + ROUND_ROWS)
        slot = jnp.where(here, own_holder * SENT_ROWS + own_rank - first, -1)
        return slot, table, jnp.max(rank) // ROUND_ROWS + 1

    own_gain = lax.dynamic_slice_in_dim(norm_gain, lax.axis_index(DP) * width_here, width_here)
    own_gain = own_gain.reshape(1, width_here).astype(jnp.float32)
    slot, table, rounds = exchange(0)
    pair_bias = table.reshape(chips, SENT_ROWS, width_here)
    pair_bias = pair_bias[:, ROUND_ROWS : ROUND_ROWS + 2, :core_cols].astype(jnp.float32)
    pair_bias = jnp.concatenate(
        [
            pair_bias[:, :, :q_cols].reshape(chips, 1, -1),
            pair_bias[:, :, q_cols:].reshape(chips, 1, -1),
        ],
        axis=2,
    )
    half_rows = rows_here // HALVES
    kv_heads = key_cache.shape[2] // HD
    positions = (lengths[:, None] + jnp.arange(step_count, dtype=jnp.int32)[None, :]).reshape(-1)
    frequency = rope_base ** (-(2.0 * jnp.arange(HD // 2, dtype=jnp.float32)) / HD)
    angles = positions.astype(jnp.float32)[:, None] * frequency
    cosine, sine = jnp.cos(angles), jnp.sin(angles)
    cosine = jnp.concatenate([cosine, cosine], axis=1)
    sine = jnp.concatenate([-sine, sine], axis=1)
    row_lengths = jnp.repeat(lengths, step_count)

    def part_of(values, half):
        return values.reshape(parties, HALVES, half_rows)[:, half].reshape(1, -1)

    payloads = tuple(
        project(place, part_of(slot, half), table, own_gain, weights, (o_line,), chips)
        for half in range(HALVES)
    )

    def further(turn, sofar):
        turn_slot, turn_table, _ = exchange(turn)
        return tuple(
            sofar[half]
            + project(
                place, part_of(turn_slot, half), turn_table, own_gain, weights, (), chips
            )
            for half in range(HALVES)
        )

    payloads = lax.fori_loop(1, rounds, further, payloads)
    layer_count = lax.axis_size(("yh", "zl"))
    arrived, new_keys, new_values, branches = [], [], [], []
    for half in range(HALVES):
        here = lax.all_to_all(payloads[half], PLANE, split_axis=0, concat_axis=0, tiled=True)
        here = here.reshape(replicas, chips, half_rows, -1)
        rows = slice(half * half_rows, (half + 1) * half_rows)
        spread, keys, values = attend(
            half,
            here,
            pair_bias,
            cosine[rows],
            sine[rows],
            jnp.tile(row_lengths[rows], 8 * kv_heads // chips).reshape(-1, 1),
            key_cache,
            value_cache,
            layer_count,
        )
        gathered = lax.all_to_all(
            spread.reshape(-1, half_rows, 2 * q_cols), LAYER, split_axis=0, concat_axis=0, tiled=True
        ).reshape(-1, 2 * q_cols)
        branch = branch_out(place, gathered, o_weights)
        back = lax.all_to_all(branch, LAYER, split_axis=0, concat_axis=0, tiled=True)
        branches.append(back.reshape(2, layer_count // 2, chips, half_rows, -1))
        arrived.append(here)
        new_keys.append(keys)
        new_values.append(values)
    hidden = hidden_sum(branches[0], arrived[0], step_count)
    new_keys = jnp.concatenate(new_keys, axis=0)
    new_values = jnp.concatenate(new_values, axis=0)
    return (
        hidden,
        new_keys.reshape(seq_here, step_count, -1),
        new_values.reshape(seq_here, step_count, -1),
    )


def solution(mesh):
    fine = Mesh(mesh.devices.reshape(2, 2, 2, 2, 4, 2), EVERY)
    tensor = CHIPS + ("core",)
    placed = (
        P(EVERY, None),
        P(EVERY),
        P(tensor, DP),
        P(),
        P(DP, tensor),
        P(DP, tensor),
        P(DP, tensor),
        P(tensor),
        P(tensor),
        P(tensor),
        P(tensor, DP),
        P(EVERY, None, None),
        P(EVERY, None, None),
    )
    return jax.shard_map(
        per_device,
        mesh=fine,
        in_specs=placed,
        out_specs=(
            P(EVERY, None, None),
            P(EVERY, None, None),
            P(EVERY, None, None),
        ),
        check_vma=False,
    )
```

```python
import functools

import jax
import jax.numpy as jnp
from jax import lax
from jax.experimental import pallas as pl
from jax.experimental.pallas import tpu as pltpu
from jax.sharding import Mesh
from jax.sharding import PartitionSpec as P

HD = 128
ROUND_ROWS = 118
SENT_ROWS = 120
CHIP_COUNT = 8
WHOLE_VMEM = 60 * 1024 * 1024
HALVES = 1

norm_epsilon = 1e-06
rope_base = 1000000.0
masked_low = -1e30

DP = ("yh", "yl", "zl")
CHIPS = ("zh", "x")
LAYER = ("yh", "zl", "zh", "x")
PLANE = ("yh", "yl", "zl", "zh", "x")
EVERY = ("yh", "yl", "zl", "zh", "x", "core")


def swap_cores(value):
    return lax.ppermute(value, "core", [(0, 1), (1, 0)])


def swap_lines(value):
    return lax.ppermute(value, "yl", [(0, 1), (1, 0)])


VMEM = pl.BlockSpec(memory_space=pltpu.VMEM)
SMEM = pl.BlockSpec(memory_space=pltpu.SMEM)
HBM = pl.BlockSpec(memory_space=pltpu.HBM)


def turned(row):
    wide = jnp.broadcast_to(row.astype(jnp.float32), (8, row.shape[1]))
    return jnp.transpose(wide)[:, :1].astype(jnp.int32)


def lookup_kernel(place_ref, id_row_ref, q_ref, k_ref, v_ref, vocab_ref, *rest):
    mine_ref, theirs_ref, rank_ref, list_ref, total_ref, vocab_buf, sem = rest
    chip, core, first = place_ref[0], place_ref[1], place_ref[3]
    planes, _, rows = id_row_ref.shape
    vocab_here = vocab_ref.shape[0]
    steps = sem.shape[0]
    span = vocab_here // steps
    copies = [
        pltpu.make_async_copy(
            vocab_ref.at[pl.ds(step * span, span), :],
            vocab_buf.at[pl.ds(step * span, span), :],
            sem.at[step],
        )
        for step in range(steps)
    ]
    for copy in copies:
        copy.start()
    across = lax.broadcasted_iota(jnp.int32, (rows, rows), 1)
    down = lax.broadcasted_iota(jnp.int32, (rows, rows), 0)
    earlier = across < down
    slot = lax.broadcasted_iota(jnp.int32, (SENT_ROWS, rows), 0)
    for plane in range(planes):
        id_row = id_row_ref[plane]
        id_col = turned(id_row)
        again = jnp.where((id_row == id_col) & earlier, 1, 0)
        key_col = jnp.where(jnp.max(again, axis=1, keepdims=True) == 0, id_col, -1)
        edge_row = jnp.zeros_like(id_row)
        for other in range(1, CHIP_COUNT):
            edge = other * 2 * vocab_here
            edge_row = jnp.where(id_row >= edge, edge, edge_row)
        before = (key_col >= edge_row) & (key_col < id_row)
        rank = jnp.sum(before.astype(jnp.int32), axis=0, keepdims=True)
        rank_ref[plane] = rank
        offset = id_row - (2 * chip + core) * vocab_here
        listed = (offset >= 0) & (offset < vocab_here)
        wanted = jnp.where(listed, rank - first, -1)
        chosen = (wanted == slot) & (slot < ROUND_ROWS)
        list_ref[plane * SENT_ROWS : (plane + 1) * SENT_ROWS, :] = jnp.max(
            jnp.where(chosen, offset, -1), axis=1, keepdims=True
        )

    total = None
    for step in range(steps):
        entry = lax.broadcasted_iota(jnp.int32, (planes * SENT_ROWS, span), 1) + step * span
        chosen = (entry == list_ref[...]).astype(jnp.bfloat16)
        copies[step].wait()
        found = jnp.dot(
            chosen, vocab_buf[step * span : (step + 1) * span, :], preferred_element_type=jnp.float32
        )
        total = found if total is None else total + found
    total_ref[...] = total
    width = total_ref.shape[1]
    pieces = [piece[...].astype(jnp.float32) for piece in (q_ref, k_ref, v_ref)]
    filled = sum(piece.shape[1] for piece in pieces)
    pieces.append(jnp.zeros((1, width - filled), jnp.float32))
    bias = jnp.broadcast_to(jnp.concatenate(pieces, axis=1), (8, width))
    is_bias = (
        lax.broadcasted_iota(jnp.int32, (8, 1), 0) == ROUND_ROWS + core - (SENT_ROWS - 8)
    )
    for side, target in ((0, mine_ref), (1, theirs_ref)):
        plane = (core + side) % 2
        start = pl.multiple_of(plane * SENT_ROWS, SENT_ROWS)
        tail = pl.ds(start + SENT_ROWS - 8, 8)
        total_ref[tail, :] = jnp.where(is_bias, bias, total_ref[tail, :])
        target[...] = total_ref[pl.ds(start, SENT_ROWS), :].astype(jnp.bfloat16)


def look_up(place, plane_ids, biases, embedding):
    planes, rows = plane_ids.shape
    vocab_here, width = embedding.shape
    steps = 3
    return pl.pallas_call(
        lookup_kernel,
        out_shape=(
            jax.ShapeDtypeStruct((SENT_ROWS, width), jnp.bfloat16),
            jax.ShapeDtypeStruct((SENT_ROWS, width), jnp.bfloat16),
            jax.ShapeDtypeStruct((planes, 1, rows), jnp.int32),
        ),
        in_specs=[SMEM] + [VMEM] * (1 + len(biases)) + [HBM],
        out_specs=(VMEM, VMEM, VMEM),
        scratch_shapes=[
            pltpu.VMEM((planes * SENT_ROWS, 1), jnp.int32),
            pltpu.VMEM((planes * SENT_ROWS, width), jnp.float32),
            pltpu.VMEM((vocab_here, width), jnp.bfloat16),
            pltpu.SemaphoreType.DMA((steps,)),
        ],
        compiler_params=pltpu.CompilerParams(vmem_limit_bytes=48 * 1024 * 1024),
        name="look_up",
    )(
        place,
        plane_ids.reshape(planes, 1, rows),
        *[bias.reshape(1, -1) for bias in biases],
        embedding,
    )


def attention_kernel(
    half,
    arrived_ref, bias_ref, cosine_ref, sine_ref, length_ref, keys_ref, values_ref, *rest
):
    out_ref, new_keys_ref, new_values_ref = rest[:3]
    key_buf, value_buf, query_buf, key_sem, value_sem = rest[3:]
    groups, chips, rows, _ = arrived_ref.shape
    seqs, cache_len, _ = key_buf.shape
    steps = rows // seqs
    core_cols = bias_ref.shape[2] // 2
    heads = out_ref.shape[3] // HD
    many = heads * rows
    key_copies, value_copies = [], []
    for seq in range(seqs):
        source = half * seqs + seq
        key_copies.append(
            pltpu.make_async_copy(keys_ref.at[source], key_buf.at[seq], key_sem.at[seq])
        )
        value_copies.append(
            pltpu.make_async_copy(values_ref.at[source], value_buf.at[seq], value_sem.at[seq])
        )
    for copy in key_copies + value_copies:
        copy.start()
    square = None
    for group in range(groups):
        for chip in range(chips):
            part = arrived_ref[group, chip, :, 2 * core_cols :].astype(jnp.float32)
            square = part * part if square is None else square + part * part
    width = groups * chips * square.shape[1]
    scale = lax.rsqrt(jnp.sum(square, axis=1, keepdims=True) / width + norm_epsilon)
    cosine = cosine_ref[...]
    sine = sine_ref[...]
    lane = lax.broadcasted_iota(jnp.int32, (rows, HD), 1)

    def rotated(features):
        return features * cosine + pltpu.roll(features, HD // 2, 1) * sine

    row_at = lax.broadcasted_iota(jnp.int32, (many, 1), 0) % rows
    row_seq = row_at // steps
    row_step = row_at % steps
    fresh_at = lax.broadcasted_iota(jnp.int32, (many, rows), 1)
    fresh_valid = (fresh_at // steps == row_seq) & (fresh_at % steps <= row_step)
    cache_valid = lax.broadcasted_iota(jnp.int32, (many, cache_len), 1) < length_ref[...]
    score_scale = HD ** (-0.5)
    for chip in range(chips):
        span = slice(chip * HD, (chip + 1) * HD)
        joined = arrived_ref[0, chip, :, : 2 * core_cols].astype(jnp.float32)
        for group in range(1, groups):
            joined = joined + arrived_ref[group, chip, :, : 2 * core_cols].astype(jnp.float32)
        joined = (joined * scale + bias_ref[chip]).astype(jnp.bfloat16).astype(jnp.float32)
        parts = []
        for head in range(heads):
            parts.append(rotated(joined[:, head * HD : (head + 1) * HD]))
        query_buf[chip] = jnp.concatenate(parts, axis=0).astype(jnp.bfloat16)
        low = joined[:, heads * HD : (heads + 1) * HD]
        high = joined[:, (heads + 1) * HD :]
        fresh_keys = rotated(jnp.where(lane < HD // 2, low, pltpu.roll(high, HD // 2, 1))).astype(
            jnp.bfloat16
        )
        fresh_values = jnp.where(lane < HD // 2, pltpu.roll(low, HD // 2, 1), high).astype(
            jnp.bfloat16
        )
        new_keys_ref[:, span] = fresh_keys
        new_values_ref[:, span] = fresh_values
    for copy in key_copies:
        copy.wait()
    for chip in range(chips):
        span = slice(chip * HD, (chip + 1) * HD)
        queries = query_buf[chip]
        fresh_keys = new_keys_ref[:, span]
        fresh_values = new_values_ref[:, span]
        scores = None
        for seq in range(seqs):
            found = lax.dot_general(
                queries,
                key_buf[seq, :, span],
                (((1,), (1,)), ((), ())),
                preferred_element_type=jnp.float32,
            )
            scores = found if scores is None else jnp.where(row_seq == seq, found, scores)
        fresh_scores = lax.dot_general(
            queries, fresh_keys, (((1,), (1,)), ((), ())), preferred_element_type=jnp.float32
        )
        scores = jnp.where(cache_valid, scores * score_scale, masked_low)
        fresh_scores = jnp.where(fresh_valid, fresh_scores * score_scale, masked_low)
        top = jnp.maximum(
            jnp.max(scores, axis=1, keepdims=True), jnp.max(fresh_scores, axis=1, keepdims=True)
        )
        scores = jnp.exp(scores - top)
        fresh_scores = jnp.exp(fresh_scores - top)
        share = 1.0 / (
            jnp.sum(scores, axis=1, keepdims=True) + jnp.sum(fresh_scores, axis=1, keepdims=True)
        )
        weights = (scores * share).astype(jnp.bfloat16)
        fresh_weights = (fresh_scores * share).astype(jnp.bfloat16)
        attended = jnp.dot(fresh_weights, fresh_values, preferred_element_type=jnp.float32)
        if chip == 0:
            for copy in value_copies:
                copy.wait()
        for seq in range(seqs):
            found = jnp.dot(
                weights, value_buf[seq, :, span], preferred_element_type=jnp.float32
            )
            attended = attended + jnp.where(row_seq == seq, found, 0.0)
        for head in range(heads):
            piece = attended[head * rows : (head + 1) * rows].astype(jnp.bfloat16)
            for group in range(out_ref.shape[0]):
                out_ref[group, chip, :, head * HD : (head + 1) * HD] = piece


def attend(half, arrived, bias, cosine, sine, row_lengths, key_cache, value_cache, copies):
    _, chips, rows, _ = arrived.shape
    seqs, cache_len, kv_cols = key_cache.shape
    seqs = seqs // HALVES
    heads = 8
    return pl.pallas_call(
        functools.partial(attention_kernel, half),
        out_shape=(
            jax.ShapeDtypeStruct((copies, chips, rows, heads * HD), jnp.bfloat16),
            jax.ShapeDtypeStruct((rows, kv_cols), jnp.bfloat16),
            jax.ShapeDtypeStruct((rows, kv_cols), jnp.bfloat16),
        ),
        in_specs=[VMEM] * 5 + [HBM] * 2,
        out_specs=(VMEM, VMEM, VMEM),
        scratch_shapes=[
            pltpu.VMEM((seqs, cache_len, kv_cols), jnp.bfloat16),
            pltpu.VMEM((seqs, cache_len, kv_cols), jnp.bfloat16),
            pltpu.VMEM((chips, heads * rows, HD), jnp.bfloat16),
            pltpu.SemaphoreType.DMA((seqs,)),
            pltpu.SemaphoreType.DMA((seqs,)),
        ],
        compiler_params=pltpu.CompilerParams(vmem_limit_bytes=56 * 1024 * 1024),
        name="attend",
    )(arrived, bias, cosine, sine, row_lengths, key_cache, value_cache)


def projection_kernel(place_ref, slot_ref, table_ref, gain_ref, *rest):
    out_ref, wide_ref, weight_buf, kv_buf, sem = rest[-5:]
    chip, core = place_ref[0], place_ref[1]
    table_rows = table_ref.shape[0]
    q_cols, kv_cols = rest[0].shape[1], rest[2].shape[0]
    cols = q_cols + 2 * kv_cols
    step = pl.program_id(0)
    slot = turned(slot_ref[...])
    rows = slot.shape[0]
    copies = []
    for side in range(2):
        owner = (core + side) % 2
        spots = [weight_buf.at[:, pl.ds(pl.multiple_of(owner * q_cols, q_cols), q_cols)]]
        for part in range(2):
            first = pl.multiple_of((2 * owner + part) * kv_cols, kv_cols)
            spots.append(kv_buf.at[pl.ds(first, kv_cols), :])
        for part, spot in enumerate(spots):
            number = 2 * part + side
            copies.append(pltpu.make_async_copy(rest[number], spot, sem.at[number]))

    @pl.when(step == 0)
    def _():
        for copy in copies:
            copy.start()

    chosen = (
        lax.broadcasted_iota(jnp.int32, (rows, table_rows), 1) == slot
    ).astype(jnp.bfloat16)
    found = jnp.dot(chosen, table_ref[...], preferred_element_type=jnp.float32)
    wide_ref[...] = found.astype(jnp.bfloat16)
    gained = (found * gain_ref[...]).astype(jnp.bfloat16)

    @pl.when(step == 0)
    def _():
        for copy in copies:
            copy.wait()

    product = jnp.dot(gained, weight_buf[...], preferred_element_type=jnp.float32)
    out_ref[:, : 2 * q_cols] = product.astype(jnp.bfloat16)
    product = lax.dot_general(
        gained, kv_buf[...], (((1,), (1,)), ((), ())), preferred_element_type=jnp.float32
    )
    out_ref[:, 2 * q_cols : 2 * cols] = product.astype(jnp.bfloat16)
    strip = out_ref.shape[1] - 2 * cols
    out_ref[:, 2 * cols :] = wide_ref[:, pl.ds(pl.multiple_of(chip * strip, strip), strip)]


def project(place, slot, table, gain, weights, held, chips):
    rows = slot.shape[1]
    table_rows, width = table.shape
    q_cols, kv_cols = weights[0].shape[1], weights[2].shape[0]
    cols = q_cols + 2 * kv_cols
    out_cols = 2 * cols + width // chips
    block = 512
    return pl.pallas_call(
        projection_kernel,
        out_shape=jax.ShapeDtypeStruct((rows, out_cols), jnp.bfloat16),
        grid=(rows // block,),
        in_specs=[
            SMEM,
            pl.BlockSpec((1, block), lambda i: (0, i)),
            pl.BlockSpec((table_rows, width), lambda i: (0, 0)),
            pl.BlockSpec((1, width), lambda i: (0, 0)),
        ]
        + [HBM] * (len(weights) + len(held)),
        out_specs=pl.BlockSpec((block, out_cols), lambda i: (i, 0)),
        scratch_shapes=[
            pltpu.VMEM((block, width), jnp.bfloat16),
            pltpu.VMEM((width, 2 * q_cols), jnp.bfloat16),
            pltpu.VMEM((4 * kv_cols, width), jnp.bfloat16),
            pltpu.SemaphoreType.DMA((len(weights),)),
        ],
        compiler_params=pltpu.CompilerParams(vmem_limit_bytes=48 * 1024 * 1024),
        name="project",
    )(place, slot, table, gain, *weights, *held)


def branch_kernel(place_ref, rows_ref, *rest):
    weight_refs, out_ref = rest[:-1], rest[-1]
    core, line = place_ref[1], place_ref[2]
    depth, width = weight_refs[0].shape
    count = len(weight_refs) // 2
    for turn in range(count):
        block = pl.multiple_of(((line + count - turn) % count) * width, width)
        parts = []
        for side in range(2):
            where = pl.multiple_of(((core + side) % 2) * depth, depth)
            parts.append(
                jnp.dot(
                    rows_ref[:, pl.ds(where, depth)],
                    weight_refs[2 * turn + side][...],
                    preferred_element_type=jnp.float32,
                )
            )
        out_ref[:, pl.ds(block, width)] = (parts[0] + parts[1]).astype(jnp.bfloat16)


def branch_out(place, rows, weights):
    count = len(weights)
    width = weights[0].shape[1]
    return pl.pallas_call(
        branch_kernel,
        out_shape=jax.ShapeDtypeStruct((rows.shape[0], count // 2 * width), jnp.bfloat16),
        in_specs=[SMEM, VMEM] + [VMEM] * count,
        out_specs=VMEM,
        compiler_params=pltpu.CompilerParams(vmem_limit_bytes=WHOLE_VMEM),
        name="branch",
    )(place, rows, *weights)


def hidden_kernel(steps, branch_ref, strip_ref, out_ref):
    upper, layers, chips, rows, pair_width = branch_ref.shape
    groups = strip_ref.shape[0]
    strip = out_ref.shape[2] // (groups * chips)
    width = strip * chips
    lower = pair_width // width
    for group in range(groups):
        high, low, layer = group // (lower * layers), group // layers % lower, group % layers
        for part in range(chips):
            start = low * width + part * strip
            total = strip_ref[group, part, :, strip_ref.shape[3] - strip :].astype(jnp.float32)
            for chip in range(chips):
                total = total + branch_ref[high, layer, chip, :, start : start + strip].astype(
                    jnp.float32
                )
            start = group * width + part * strip
            for seq in range(rows // steps):
                out_ref[seq, :, start : start + strip] = total[
                    seq * steps : (seq + 1) * steps
                ].astype(jnp.bfloat16)


def hidden_sum(branches, arrived, steps):
    upper, layers, _, rows, pair_width = branches.shape
    return pl.pallas_call(
        functools.partial(hidden_kernel, steps),
        out_shape=jax.ShapeDtypeStruct(
            (rows // steps, steps, upper * layers * pair_width), jnp.bfloat16
        ),
        in_specs=[VMEM] * 2,
        out_specs=VMEM,
        compiler_params=pltpu.CompilerParams(vmem_limit_bytes=48 * 1024 * 1024),
        name="hidden_sum",
    )(branches, arrived)


def per_device(
    token_ids,
    lengths,
    embedding,
    norm_gain,
    q_weight,
    k_weight,
    v_weight,
    q_bias,
    k_bias,
    v_bias,
    o_weight,
    key_cache,
    value_cache,
):
    seq_here, step_count = token_ids.shape
    rows_here = seq_here * step_count
    vocab_here, width_here = embedding.shape
    line = lax.axis_index("yl")
    replicas = lax.axis_size(DP)
    chips = lax.axis_size(CHIPS)
    chip = lax.axis_index(CHIPS)
    core = lax.axis_index("core")
    parties = replicas * chips
    plane_rows = parties * rows_here
    place = jnp.stack([chip, core, line]).astype(jnp.int32)

    weights = []
    for own in (q_weight, k_weight.T, v_weight.T):
        weights += [own, swap_cores(own)]
    o_line = swap_lines(o_weight)
    o_weights = (o_weight, swap_cores(o_weight), o_line, swap_cores(o_line))
    core_cols = q_bias.shape[0] + k_bias.shape[0] + v_bias.shape[0]
    q_cols = q_bias.shape[0]

    sent_ids = jnp.broadcast_to(token_ids.reshape(1, rows_here), (parties * 2, rows_here))
    every_id = lax.all_to_all(sent_ids, EVERY, split_axis=0, concat_axis=0, tiled=True)
    plane_ids = every_id.reshape(parties, 2, rows_here).transpose(1, 0, 2).reshape(2, plane_rows)
    own_holder = lax.dynamic_index_in_dim(plane_ids, core, 0, keepdims=False) // (2 * vocab_here)
    def exchange(turn):
        first = turn * ROUND_ROWS
        turn_place = jnp.concatenate([place, jnp.asarray(first, jnp.int32).reshape(1)])
        mine, theirs, rank = look_up(turn_place, plane_ids, (q_bias, k_bias, v_bias), embedding)
        merged = mine + swap_cores(theirs)
        table = lax.all_to_all(
            jnp.broadcast_to(merged[None], (chips, SENT_ROWS, width_here)),
            CHIPS,
            split_axis=0,
            concat_axis=0,
            tiled=True,
        ).reshape(chips * SENT_ROWS, width_here)
        own_rank = lax.dynamic_index_in_dim(rank, core, 0, keepdims=False).reshape(-1)
        here = (own_rank >= first) & (own_rank < first + ROUND_ROWS)
        slot = jnp.where(here, own_holder * SENT_ROWS + own_rank - first, -1)
        return slot, table, jnp.max(rank) // ROUND_ROWS + 1

    own_gain = lax.dynamic_slice_in_dim(norm_gain, lax.axis_index(DP) * width_here, width_here)
    own_gain = own_gain.reshape(1, width_here).astype(jnp.float32)
    slot, table, rounds = exchange(0)
    pair_bias = table.reshape(chips, SENT_ROWS, width_here)
    pair_bias = pair_bias[:, ROUND_ROWS : ROUND_ROWS + 2, :core_cols].astype(jnp.float32)
    pair_bias = jnp.concatenate(
        [
            pair_bias[:, :, :q_cols].reshape(chips, 1, -1),
            pair_bias[:, :, q_cols:].reshape(chips, 1, -1),
        ],
        axis=2,
    )
    half_rows = rows_here // HALVES
    kv_heads = key_cache.shape[2] // HD
    positions = (lengths[:, None] + jnp.arange(step_count, dtype=jnp.int32)[None, :]).reshape(-1)
    frequency = rope_base ** (-(2.0 * jnp.arange(HD // 2, dtype=jnp.float32)) / HD)
    angles = positions.astype(jnp.float32)[:, None] * frequency
    cosine, sine = jnp.cos(angles), jnp.sin(angles)
    cosine = jnp.concatenate([cosine, cosine], axis=1)
    sine = jnp.concatenate([-sine, sine], axis=1)
    row_lengths = jnp.repeat(lengths, step_count)

    def part_of(values, half):
        return values.reshape(parties, HALVES, half_rows)[:, half].reshape(1, -1)

    payloads = tuple(
        project(place, part_of(slot, half), table, own_gain, weights, (o_line,), chips)
        for half in range(HALVES)
    )

    def further(turn, sofar):
        turn_slot, turn_table, _ = exchange(turn)
        return tuple(
            sofar[half]
            + project(
                place, part_of(turn_slot, half), turn_table, own_gain, weights, (), chips
            )
            for half in range(HALVES)
        )

    payloads = lax.fori_loop(1, rounds, further, payloads)
    layer_count = lax.axis_size(("yh", "zl"))
    arrived, new_keys, new_values, branches = [], [], [], []
    for half in range(HALVES):
        here = lax.all_to_all(payloads[half], PLANE, split_axis=0, concat_axis=0, tiled=True)
        here = here.reshape(replicas, chips, half_rows, -1)
        rows = slice(half * half_rows, (half + 1) * half_rows)
        spread, keys, values = attend(
            half,
            here,
            pair_bias,
            cosine[rows],
            sine[rows],
            jnp.tile(row_lengths[rows], 8 * kv_heads // chips).reshape(-1, 1),
            key_cache,
            value_cache,
            layer_count,
        )
        gathered = lax.all_to_all(
            spread.reshape(-1, half_rows, 2 * q_cols), LAYER, split_axis=0, concat_axis=0, tiled=True
        ).reshape(-1, 2 * q_cols)
        branch = branch_out(place, gathered, o_weights)
        back = lax.all_to_all(branch, LAYER, split_axis=0, concat_axis=0, tiled=True)
        branches.append(back.reshape(2, layer_count // 2, chips, half_rows, -1))
        arrived.append(here)
        new_keys.append(keys)
        new_values.append(values)
    hidden = hidden_sum(branches[0], arrived[0], step_count)
    new_keys = jnp.concatenate(new_keys, axis=0)
    new_values = jnp.concatenate(new_values, axis=0)
    return (
        hidden,
        new_keys.reshape(seq_here, step_count, -1),
        new_values.reshape(seq_here, step_count, -1),
    )


def solution(mesh):
    fine = Mesh(mesh.devices.reshape(2, 2, 2, 2, 4, 2), EVERY)
    tensor = CHIPS + ("core",)
    placed = (
        P(EVERY, None),
        P(EVERY),
        P(tensor, DP),
        P(),
        P(DP, tensor),
        P(DP, tensor),
        P(DP, tensor),
        P(tensor),
        P(tensor),
        P(tensor),
        P(tensor, DP),
        P(EVERY, None, None),
        P(EVERY, None, None),
    )
    return jax.shard_map(
        per_device,
        mesh=fine,
        in_specs=placed,
        out_specs=(
            P(EVERY, None, None),
            P(EVERY, None, None),
            P(EVERY, None, None),
        ),
        check_vma=False,
    )
```
